32 devices in a mesh: fsdp: 8 (over z, x), seq: 4 (over y, core).
Axes of the slice: x: 2, y: 2, z: 4, core: 2. Of those that a mesh axis runs over, the one named last changes fastest.
Arguments:
- tokens: bfloat16 [8, 512, 3584], P('fsdp', 'seq'), may hold values from -6 to 6
- queries: bfloat16 [8, 512, 3584], P('fsdp', 'seq'), may hold values from -21 to 21
- cotangent: bfloat16 [8, 512, 3584], P('fsdp', 'seq'), may hold values from -6 to 6
- modality: int32 [8, 512], P('fsdp', 'seq'), may hold values from 0 to 1, as said below
- block_ids: int32 [8, 512], P('fsdp', 'seq'), may hold values from 0 to 511, as said below
- kv_weight: bfloat16 [2, 3584, 1024], P(None, 'fsdp', 'seq'), may hold values from -0.09375 to 0.09375
Outputs:
- attended: bfloat16 [8, 512, 3584], P('fsdp', 'seq')
- grad_queries: bfloat16 [8, 512, 3584], P('fsdp', 'seq')
- grad_tokens: bfloat16 [8, 512, 3584], P('fsdp', 'seq')
- grad_kv_weight: float32 [2, 3584, 1024], P(None, 'fsdp', 'seq')
The draws below stay inside these ranges and needn't reach their ends.
Inputs may be any that keep to these rules, and one draw needn't show every extreme that they name: `modality`: the first 32 tokens of a sequence are text; video tokens come in whole frames of 32 tokens starting at multiples of 32. `block_ids`: a text token's id is its position in its sequence; a video token's id is the position of the last token of its frame.
All inputs are finite; a program needn't handle non-finite values.
Results may differ from the reference program's by a relative error of at most 0.015.
The reference program's roundings to bfloat16 on the way count: a program that leaves them out, or rounds other values in their place, can miss the bound.
Values may be sent and summed in bfloat16 or wider, within the bound.
No kernel may reach another device: no remote copies, remote signals or barrier semaphores. Data moves between devices by JAX's collectives and lax.ppermute only.
A program may use at most 128 MiB of HBM per device.

```python
import jax
import jax.numpy as jnp
from jax import lax

D = 3584
KV_HEADS = 4
HEAD_DIM = 128
GROUP = 7
EXPERTS = 2
FRAME = 32
HEADS = 28
LENGTH = 512
SEQS = 8


def unit_kinds(key):
    count = LENGTH // FRAME
    kinds = jax.random.randint(key, (SEQS, count), 0, 2)
    kinds = kinds.at[:, 0].set(0).at[:, 1].set(1)
    return jnp.repeat(kinds, FRAME, axis=1).astype(jnp.int32)


def draw_modality(key, part):
    return unit_kinds(key)


def draw_block_ids(key, part):
    kinds = unit_kinds(key)
    position = jnp.arange(LENGTH, dtype=jnp.int32)[None, :]
    frame_end = position // FRAME * FRAME + FRAME - 1
    return jnp.where(kinds == 1, frame_end, position).astype(jnp.int32)


def draw_queries(key, part):
    key = jax.random.fold_in(key, 7)
    first = jax.random.fold_in(key, 0)
    shape = (SEQS, LENGTH, HEADS * HEAD_DIM)
    return jnp.clip(jax.random.normal(first, shape, jnp.float32), -6.0, 6.0).astype(jnp.bfloat16)


def shard_levels(rng, shape, shards, least, high):
    def one(dim, blocks):
        steps = jax.random.uniform(jax.random.fold_in(jax.random.fold_in(rng, 6), dim), (blocks,), jnp.float32, least / len(shards), high / len(shards))
        return jnp.repeat(jnp.exp(steps), shape[dim] // blocks).reshape((-1,) + (1,) * (len(shape) - dim - 1))

    factor_of = one(*shards[0])
    for cut in shards[1:]:
        factor_of = factor_of * one(*cut)
    return factor_of


def noise(own_key, extent, scale, limit, cuts=(), kind=jnp.bfloat16):
    values = jax.random.normal(own_key, extent, jnp.float32) * scale
    if len(cuts) > 0:
        values = shard_levels(own_key, extent, cuts, -0.22, 0.18) * values
    return jnp.clip(values, min=-limit, max=limit).astype(kind)


def setup_inputs(seed: int = 0) -> dict:
    arg_keys = jax.random.split(jax.random.key(seed), 7)
    return {
        "tokens": noise(arg_keys[0], (SEQS, LENGTH, D), 1.0, 6.0, ((0, 8), (1, 4))),
        "queries": draw_queries(jax.random.fold_in(arg_keys[6], 71), 0),
        "cotangent": noise(arg_keys[2], (SEQS, LENGTH, HEADS * HEAD_DIM), 1.0, 6.0, ((0, 8), (1, 4))),
        "modality": draw_modality(jax.random.fold_in(arg_keys[6], 71), 0),
        "block_ids": draw_block_ids(jax.random.fold_in(arg_keys[6], 71), 0),
        "kv_weight": noise(arg_keys[5], (EXPERTS, D, 2 * KV_HEADS * HEAD_DIM), D ** -0.5, 0.09375, ((1, 8), (2, 4))),
    }


def attend(query_rows, key_value, query_blocks, key_blocks):
    count = query_rows.shape[0]
    length = key_value.shape[0]
    groups = key_value.shape[1] // (2 * HEAD_DIM)
    split_kv = key_value.reshape(length, groups, 2, HEAD_DIM)
    keys = split_kv[:, :, 0]
    values = split_kv[:, :, 1]
    heads = query_rows.reshape(count, groups, GROUP, HEAD_DIM)
    scores = jnp.einsum('rgjd,lgd->gjrl', heads, keys) * HEAD_DIM ** (-0.5)
    visible = key_blocks[None, :] <= query_blocks[:, None]
    scores = jnp.where(visible, scores, -1e+30)
    top = lax.optimization_barrier(jnp.max(scores, axis=-1, keepdims=True))
    expo = jnp.exp(scores - top)
    probs = expo / lax.optimization_barrier(jnp.sum(expo, axis=-1, keepdims=True))
    rounded = lax.optimization_barrier(probs.astype(jnp.bfloat16)).astype(jnp.float32)
    result = jnp.einsum('gjrl,lgd->rgjd', rounded, values)
    return result.reshape(count, groups * GROUP * HEAD_DIM)

def one_sequence(hidden, query_rows, upstream, modal, blocks, kv_weight):
    text_part = jnp.dot(hidden, kv_weight[0], preferred_element_type=jnp.float32)
    video_part = jnp.dot(hidden, kv_weight[1], preferred_element_type=jnp.float32)
    key_value = jnp.where(modal[:, None] == 1, video_part, text_part).astype(jnp.bfloat16)
    kv_float = lax.optimization_barrier(key_value).astype(jnp.float32)

    def local_attend(query_float, kv_in):
        return attend(query_float, kv_in, blocks, blocks)
    result, pullback = jax.vjp(local_attend, query_rows.astype(jnp.float32), kv_float)
    grad_query, grad_kv = pullback(upstream.astype(jnp.float32))
    grad_kv_b = grad_kv.astype(jnp.bfloat16)
    zeros = jnp.zeros_like(grad_kv_b)
    text_grad = jnp.where(modal[:, None] == 0, grad_kv_b, zeros)
    video_grad = jnp.where(modal[:, None] == 1, grad_kv_b, zeros)
    grad_hidden = jnp.dot(text_grad, kv_weight[0].T, preferred_element_type=jnp.float32) + jnp.dot(video_grad, kv_weight[1].T, preferred_element_type=jnp.float32)
    grad_weight = jnp.stack([jnp.dot(hidden.T, text_grad, preferred_element_type=jnp.float32), jnp.dot(hidden.T, video_grad, preferred_element_type=jnp.float32)])
    return (result.astype(jnp.bfloat16), grad_query.astype(jnp.bfloat16), grad_hidden.astype(jnp.bfloat16), grad_weight)

def reference(tokens, queries, cotangent, modality, block_ids, kv_weight):

    def step(total, item):
        hidden, query_rows, upstream, modal, blocks = item
        result, grad_query, grad_hidden, grad_weight = one_sequence(hidden, query_rows, upstream, modal, blocks, kv_weight)
        return (total + grad_weight, (result, grad_query, grad_hidden))
    start = jnp.zeros(kv_weight.shape, jnp.float32)
    grad_kv_weight, outputs = lax.scan(step, start, (tokens, queries, cotangent, modality, block_ids))
    return (outputs[0], outputs[1], outputs[2], grad_kv_weight)
```

```python
import functools

import jax
import jax.numpy as jnp
from jax import lax
from jax.experimental import pallas as pl
from jax.experimental.pallas import tpu as pltpu
from jax.sharding import PartitionSpec as P

HEAD_DIM = 128
GROUP = 7
SCALE = HEAD_DIM ** (-0.5)
F32 = jnp.float32
BF16 = jnp.bfloat16


def contract(a, b, da, db):
    return lax.dot_general(a, b, (((da,), (db,)), ((), ())), preferred_element_type=F32)


def attend_kernel(heads_ref, q_ref, up_ref, kv_ref, qb_ref, kb_ref, att_ref, gq_ref, gkv_ref, qs, ups, pbs, his, los):
    keys = kv_ref[0, :, :HEAD_DIM]
    values = kv_ref[0, :, HEAD_DIM:]
    rows = q_ref.shape[0]
    visible = kb_ref[...] <= qb_ref[...]
    for h in range(GROUP):
        cols = slice(h * HEAD_DIM, (h + 1) * HEAD_DIM)
        here = slice(h * rows, (h + 1) * rows)
        q = q_ref[:, cols]
        up = up_ref[:, cols]
        scores = contract(q, keys, 1, 1) * SCALE
        scores = jnp.where(visible, scores, -1e30)
        top = jnp.max(scores, axis=-1, keepdims=True)
        expo = jnp.exp(scores - top)
        probs = expo / jnp.sum(expo, axis=-1, keepdims=True)
        pb = probs.astype(BF16)
        att_ref[:, cols] = contract(pb, values, 1, 0).astype(BF16)
        dp = contract(up, values, 1, 1).astype(BF16).astype(F32)
        ds = probs * (dp - jnp.sum(probs * dp, axis=-1, keepdims=True))
        hi = ds.astype(BF16)
        lo = (ds - hi.astype(F32)).astype(BF16)
        gq_ref[:, cols] = ((contract(hi, keys, 1, 0) + contract(lo, keys, 1, 0)) * SCALE).astype(BF16)
        qs[here, :] = q
        ups[here, :] = up
        pbs[here, :] = pb
        his[here, :] = hi
        los[here, :] = lo
    dk = (contract(qs[...], his[...], 0, 0) + contract(qs[...], los[...], 0, 0)) * SCALE
    dv = contract(ups[...], pbs[...], 0, 0)
    gkv_ref[0, :, :HEAD_DIM] = dk.T
    gkv_ref[0, :, HEAD_DIM:] = dv.T


def attend(heads, queries, upstream, kv, query_blocks, key_blocks):
    rows, width = queries.shape
    count, length, pair = kv.shape
    span = GROUP * HEAD_DIM
    by_head = pl.BlockSpec((rows, span), lambda r, heads: (0, heads[r]))
    return pl.pallas_call(
        attend_kernel,
        grid_spec=pltpu.PrefetchScalarGridSpec(
            num_scalar_prefetch=1,
            grid=(count,),
            in_specs=[
                by_head,
                by_head,
                pl.BlockSpec((1, length, pair), lambda r, heads: (r, 0, 0)),
                pl.BlockSpec((rows, 1), lambda r, heads: (0, 0)),
                pl.BlockSpec((1, length), lambda r, heads: (0, 0)),
            ],
            out_specs=[
                by_head,
                by_head,
                pl.BlockSpec((1, length, pair), lambda r, heads: (r, 0, 0)),
            ],
            scratch_shapes=[
                pltpu.VMEM((GROUP * rows, HEAD_DIM), BF16),
                pltpu.VMEM((GROUP * rows, HEAD_DIM), BF16),
                pltpu.VMEM((GROUP * rows, length), BF16),
                pltpu.VMEM((GROUP * rows, length), BF16),
                pltpu.VMEM((GROUP * rows, length), BF16),
            ],
        ),
        out_shape=[
            jax.ShapeDtypeStruct((rows, width), BF16),
            jax.ShapeDtypeStruct((rows, width), BF16),
            jax.ShapeDtypeStruct((count, length, pair), F32),
        ],
        compiler_params=pltpu.CompilerParams(vmem_limit_bytes=40 * 1024 * 1024),
        cost_estimate=pl.CostEstimate(
            flops=2 * 7 * count * GROUP * rows * length * HEAD_DIM,
            bytes_accessed=8 * rows * count * span + 6 * count * length * pair,
            transcendentals=count * GROUP * rows * length,
        ),
    )(heads, queries, upstream, kv, query_blocks, key_blocks)


def per_device(fsdp, seq, tokens, queries, cotangent, modality, block_ids, kv_weight):
    tokens, queries, cotangent = tokens[0], queries[0], cotangent[0]
    me_f = lax.axis_index("fsdp")
    me_s = lax.axis_index("seq")
    rows, width = tokens.shape
    depth = kv_weight.shape[1]

    def swap(x, axis, bit):
        size = fsdp if axis == "fsdp" else seq
        return lax.ppermute(x, axis, [(i, i ^ bit) for i in range(size)])

    def over_seq(x):
        across = swap(x, "seq", 2)
        return [x, swap(x, "seq", 1), across, swap(across, "seq", 1)]

    def place(parts, axis):
        shape = list(parts[0].shape)
        shape.insert(axis, seq)
        whole = jnp.zeros(shape, parts[0].dtype)
        for r, part in enumerate(parts):
            whole = lax.dynamic_update_index_in_dim(whole, part, me_s ^ r, axis)
        return whole

    def over_fsdp(x, axis):
        if fsdp != 8:
            return lax.all_gather(x, "fsdp", axis=axis)
        shape = list(x.shape)
        shape.insert(axis, fsdp)
        whole = jnp.zeros(shape, x.dtype)
        for step in range(4):
            owner = lax.rem(me_f + fsdp - 2 * step, fsdp)
            whole = lax.dynamic_update_index_in_dim(whole, x, owner, axis)
            whole = lax.dynamic_update_index_in_dim(whole, swap(x, "fsdp", 1), owner ^ 1, axis)
            if step < 3:
                x = lax.ppermute(x, "fsdp", [(i, (i + 2) % fsdp) for i in range(fsdp)])
        return whole

    weight = over_fsdp(kv_weight, 1).reshape(2, width, -1)
    hidden = place(over_seq(tokens), 0).reshape(seq * rows, width)
    ids = lax.all_gather(jnp.stack([modality[0], block_ids[0]]), ("fsdp", "seq"), axis=0)
    ids = ids.reshape(fsdp, seq, 2, rows)
    modal = ids[:, :, 0].reshape(fsdp, seq * rows)
    mine = lax.dynamic_index_in_dim(ids, me_f, 0, keepdims=False)
    modal_here = mine[:, 0].reshape(seq * rows)
    blocks_here = mine[:, 1].reshape(1, seq * rows)

    text_part = jnp.dot(hidden, weight[0], preferred_element_type=F32)
    video_part = jnp.dot(hidden, weight[1], preferred_element_type=F32)
    key_value = jnp.where(modal_here[:, None] == 1, video_part, text_part).astype(BF16)

    kv = jnp.stack(over_seq(key_value))
    heads = me_s ^ jnp.arange(seq, dtype=jnp.int32)
    attended, grad_queries, partial = attend(heads, queries, cotangent, kv, block_ids[0][:, None], blocks_here)

    own = partial[0] + swap(partial[1], "seq", 1)
    other = partial[2] + swap(partial[3], "seq", 1)
    grad_kv = (own + swap(other, "seq", 2)).astype(BF16)

    all_grad = over_fsdp(grad_kv, 0).reshape(fsdp * seq * rows, -1)
    by_rows = tokens.reshape(rows, fsdp, depth).transpose(1, 0, 2)
    by_rows = lax.all_to_all(by_rows, "fsdp", split_axis=0, concat_axis=0, tiled=True)
    columns = place(over_seq(by_rows), 1).reshape(fsdp * seq * rows, depth)
    flat = modal.reshape(-1)[:, None]
    grad_weight = jnp.stack(
        [contract(columns, jnp.where(flat == e, all_grad, jnp.zeros_like(all_grad)), 0, 0) for e in range(2)]
    )

    weight_c = swap(weight, "seq", 1)
    grad_c = swap(grad_kv, "seq", 1)

    def hidden_grad(quarter):
        kind = lax.dynamic_slice_in_dim(modal_here, quarter * rows, rows)[:, None]
        total = 0.0
        for g, w in ((grad_kv, weight), (grad_c, weight_c)):
            g = lax.dynamic_slice_in_dim(g, quarter * rows, rows)
            for e in range(2):
                total = total + contract(jnp.where(kind == e, g, jnp.zeros_like(g)), w[e], 1, 1)
        return total

    away = swap(hidden_grad(me_s ^ 2).astype(BF16), "seq", 2)
    grad_tokens = (hidden_grad(me_s) + away.astype(F32)).astype(BF16)
    return attended[None], grad_queries[None], grad_tokens[None], grad_weight


def solution(mesh):
    split = P("fsdp", "seq", None)
    weights = P(None, "fsdp", "seq")
    return jax.shard_map(
        functools.partial(per_device, mesh.shape["fsdp"], mesh.shape["seq"]),
        mesh=mesh,
        in_specs=(split, split, split, P("fsdp", "seq"), P("fsdp", "seq"), weights),
        out_specs=(split, split, split, weights),
        check_vma=False,
    )
```

```python
import functools

import jax
import jax.numpy as jnp
from jax import lax
from jax.experimental import pallas as pl
from jax.experimental.pallas import tpu as pltpu
from jax.sharding import PartitionSpec as P

HEAD_DIM = 128
GROUP = 7
SCALE = HEAD_DIM ** (-0.5)
LOG2E = 1.4426950408889634
HIDDEN = -1e30
F32 = jnp.float32
BF16 = jnp.bfloat16


def contract(a, b, da, db):
    return lax.dot_general(a, b, (((da,), (db,)), ((), ())), preferred_element_type=F32)


def attend_kernel(count, heads_ref, q_ref, up_ref, *refs):
    kv_refs, (qb_ref, kb_ref) = refs[:count], refs[count : count + 2]
    att_ref, gq_ref, gkv_ref, bias, qs, ups, pbs, his, los = refs[-9:]
    rows = q_ref.shape[0]
    step = pl.program_id(0)

    @pl.when(step == 0)
    def _():
        bias[...] = jnp.where(kb_ref[...] <= qb_ref[...], 0.0, HIDDEN).astype(F32)

    kv = kv_refs[0][...]
    for r in range(1, count):
        kv = jnp.where(step == r, kv_refs[r][...], kv)
    keys = kv[:, :HEAD_DIM]
    values = kv[:, HEAD_DIM:]
    for h in range(GROUP):
        cols = slice(h * HEAD_DIM, (h + 1) * HEAD_DIM)
        here = slice(h * rows, (h + 1) * rows)
        q = q_ref[:, cols]
        up = up_ref[:, cols]
        scores = contract(q, keys, 1, 1) * (SCALE * LOG2E) + bias[...]
        expo = jnp.exp2(scores - jnp.max(scores, axis=-1, keepdims=True))
        probs = expo * (1.0 / jnp.sum(expo, axis=-1, keepdims=True))
        pb = probs.astype(BF16)
        att_ref[:, cols] = contract(pb, values, 1, 0).astype(BF16)
        dp = contract(up, values, 1, 1).astype(BF16).astype(F32)
        ds = probs * (dp - jnp.sum(probs * dp, axis=-1, keepdims=True))
        hi = ds.astype(BF16)
        lo = (ds - hi.astype(F32)).astype(BF16)
        gq_ref[:, cols] = ((contract(hi, keys, 1, 0) + contract(lo, keys, 1, 0)) * SCALE).astype(BF16)
        qs[here, :] = q
        ups[here, :] = up
        pbs[here, :] = pb
        his[here, :] = hi
        los[here, :] = lo
    dk = (contract(qs[...], his[...], 0, 0) + contract(qs[...], los[...], 0, 0)) * SCALE
    dv = contract(ups[...], pbs[...], 0, 0)
    gkv_ref[0, :, :HEAD_DIM] = dk.T
    gkv_ref[0, :, HEAD_DIM:] = dv.T


def attend(heads, queries, upstream, kvs, query_blocks, key_blocks, before=()):
    rows, width = queries.shape
    length, pair = kvs[0].shape
    count = len(kvs)
    span = GROUP * HEAD_DIM
    by_head = pl.BlockSpec((rows, span), lambda r, heads: (0, heads[r]))
    whole = pl.BlockSpec((length, pair), lambda r, heads: (0, 0))
    stacked = (GROUP * rows, length)
    return pl.pallas_call(
        functools.partial(attend_kernel, count),
        grid_spec=pltpu.PrefetchScalarGridSpec(
            num_scalar_prefetch=1,
            grid=(count,),
            in_specs=[by_head, by_head]
            + [whole] * count
            + [
                pl.BlockSpec((rows, 1), lambda r, heads: (0, 0)),
                pl.BlockSpec((1, length), lambda r, heads: (0, 0)),
            ]
            + [pl.BlockSpec(memory_space=pl.ANY)] * len(before),
            out_specs=[
                by_head,
                by_head,
                pl.BlockSpec((1, length, pair), lambda r, heads: (r, 0, 0)),
            ],
            scratch_shapes=[
                pltpu.VMEM((rows, length), F32),
                pltpu.VMEM((GROUP * rows, HEAD_DIM), BF16),
                pltpu.VMEM((GROUP * rows, HEAD_DIM), BF16),
                pltpu.VMEM(stacked, BF16),
                pltpu.VMEM(stacked, BF16),
                pltpu.VMEM(stacked, BF16),
            ],
        ),
        out_shape=[
            jax.ShapeDtypeStruct((rows, width), BF16),
            jax.ShapeDtypeStruct((rows, width), BF16),
            jax.ShapeDtypeStruct((count, length, pair), F32),
        ],
        input_output_aliases={5 + count + i: i for i in range(len(before))},
        compiler_params=pltpu.CompilerParams(vmem_limit_bytes=32 * 1024 * 1024),
        cost_estimate=pl.CostEstimate(
            flops=2 * 7 * count * GROUP * rows * length * HEAD_DIM,
            bytes_accessed=8 * rows * count * span + 6 * count * length * pair,
            transcendentals=count * GROUP * rows * length,
        ),
    )(heads, queries, upstream, *kvs, query_blocks, key_blocks, *before)


def per_device(fsdp, seq, tokens, queries, cotangent, modality, block_ids, kv_weight):
    tokens, queries, cotangent = tokens[0], queries[0], cotangent[0]
    me_f = lax.axis_index("fsdp")
    me_s = lax.axis_index("seq")
    rows, width = tokens.shape
    depth, pair = kv_weight.shape[1:]
    length = seq * rows

    def swap(x, axis, bit):
        size = fsdp if axis == "fsdp" else seq
        return lax.ppermute(x, axis, [(i, i ^ bit) for i in range(size)])

    def over_seq(x):
        across = swap(x, "seq", 2)
        return [x, swap(x, "seq", 1), across, swap(across, "seq", 1)]

    def place(parts):
        whole = jnp.zeros((seq, *parts[0].shape), parts[0].dtype)
        for r, part in enumerate(parts):
            whole = lax.dynamic_update_index_in_dim(whole, part, me_s ^ r, 0)
        return whole

    def over_fsdp(x):
        if fsdp != 8:
            return lax.all_gather(x, "fsdp", axis=0)
        whole = jnp.zeros((fsdp, *x.shape), x.dtype)
        for step in range(4):
            owner = lax.rem(me_f + fsdp - 2 * step, fsdp)
            whole = lax.dynamic_update_index_in_dim(whole, x, owner, 0)
            whole = lax.dynamic_update_index_in_dim(whole, swap(x, "fsdp", 1), owner ^ 1, 0)
            if step < 3:
                x = lax.ppermute(x, "fsdp", [(i, (i + 2) % fsdp) for i in range(fsdp)])
        return whole

    def by_expert(kind, x):
        zero = jnp.zeros_like(x)
        return jnp.concatenate([jnp.where(kind == e, x, zero) for e in range(2)], axis=-1)

    both = jnp.concatenate([kv_weight[0], kv_weight[1]], axis=-1)
    weight = over_fsdp(both).reshape(width, 2 * pair)
    hidden = place(over_seq(tokens)).reshape(length, width)
    ids = place(over_seq(jnp.stack([modality[0], block_ids[0]])))
    modal_here = ids[:, 0].reshape(length, 1)
    blocks_here = ids[:, 1].reshape(1, length)

    parts = jnp.dot(hidden, weight, preferred_element_type=F32)
    key_value = jnp.where(modal_here == 1, parts[:, pair:], parts[:, :pair]).astype(BF16)

    kvs = over_seq(key_value)
    heads = me_s ^ jnp.arange(seq, dtype=jnp.int32)
    query_blocks = block_ids[0][:, None]
    out_a, out_q, far = attend(heads[2:], queries, cotangent, kvs[2:], query_blocks, blocks_here)
    attended, grad_queries, near = attend(
        heads[:2], queries, cotangent, kvs[:2], query_blocks, blocks_here, (out_a, out_q)
    )
    arriving = swap(far[0] + swap(far[1], "seq", 1), "seq", 2)
    grad_kv = (near[0] + swap(near[1], "seq", 1) + arriving).astype(BF16)

    lanes = -(-(depth + 1) // 128) * 128
    columns = tokens.reshape(rows, fsdp, depth).transpose(1, 0, 2)
    kinds = jnp.broadcast_to(modality[0].astype(BF16)[None, :, None], (fsdp, rows, 1))
    blank = jnp.zeros((fsdp, rows, lanes - depth - 1), BF16)
    columns = jnp.concatenate([columns, kinds, blank], axis=-1)
    columns = lax.all_to_all(columns, "fsdp", split_axis=0, concat_axis=0, tiled=True)
    columns = over_seq(columns)

    all_grad = over_fsdp(grad_kv)
    total = 0.0
    for r, part in enumerate(columns):
        quarter = lax.dynamic_slice_in_dim(all_grad, (me_s ^ r) * rows, rows, 1).reshape(fsdp * rows, pair)
        part = part.reshape(fsdp * rows, lanes)
        total = total + contract(part, by_expert(part[:, depth : depth + 1], quarter), 0, 0)
    grad_weight = jnp.stack([total[:depth, :pair], total[:depth, pair:]])

    weight_c = swap(weight, "seq", 1)
    grad_c = swap(grad_kv, "seq", 1)

    def hidden_grad(quarter):
        kind = lax.dynamic_slice_in_dim(modal_here, quarter * rows, rows)
        total = 0.0
        for g, w in ((grad_kv, weight), (grad_c, weight_c)):
            g = lax.dynamic_slice_in_dim(g, quarter * rows, rows)
            total = total + contract(by_expert(kind, g), w, 1, 1)
        return total

    away = swap(hidden_grad(me_s ^ 2).astype(BF16), "seq", 2)
    grad_tokens = (hidden_grad(me_s) + away.astype(F32)).astype(BF16)
    return attended[None], grad_queries[None], grad_tokens[None], grad_weight


def solution(mesh):
    split = P("fsdp", "seq", None)
    weights = P(None, "fsdp", "seq")
    return jax.shard_map(
        functools.partial(per_device, mesh.shape["fsdp"], mesh.shape["seq"]),
        mesh=mesh,
        in_specs=(split, split, split, P("fsdp", "seq"), P("fsdp", "seq"), weights),
        out_specs=(split, split, split, weights),
        check_vma=False,
    )
```

```python
import functools

import jax
import jax.numpy as jnp
from jax import lax
from jax.experimental import pallas as pl
from jax.experimental.pallas import tpu as pltpu
from jax.sharding import PartitionSpec as P

HEAD_DIM = 128
GROUP = 7
SCALE = HEAD_DIM ** (-0.5)
LOG2E = 1.4426950408889634
HIDDEN = -1e30
F32 = jnp.float32
BF16 = jnp.bfloat16


def contract(a, b, da, db):
    return lax.dot_general(a, b, (((da,), (db,)), ((), ())), preferred_element_type=F32)


def after(x, *others):
    return pl.pallas_call(
        lambda *refs: None,
        in_specs=[pl.BlockSpec(memory_space=pl.ANY)] * (1 + len(others)),
        out_specs=pl.BlockSpec(memory_space=pl.ANY),
        out_shape=jax.ShapeDtypeStruct(x.shape, x.dtype),
        input_output_aliases={0: 0},
        cost_estimate=pl.CostEstimate(flops=0, bytes_accessed=0, transcendentals=0),
    )(x, *others)


def attend_kernel(count, heads_ref, q_ref, up_ref, *refs):
    kv_refs, (qb_ref, kb_ref) = refs[:count], refs[count : count + 2]
    att_ref, gq_ref, gkv_ref, bias, scores_all, dp_all, pbs, his, los = refs[-9:]
    rows = q_ref.shape[0]
    step = pl.program_id(0)

    @pl.when(step == 0)
    def _():
        bias[...] = jnp.where(kb_ref[...] <= qb_ref[...], 0.0, HIDDEN).astype(F32)

    kv = kv_refs[0][...]
    for r in range(1, count):
        kv = jnp.where(step == r, kv_refs[r][...], kv)
    keys = kv[:, :HEAD_DIM]
    values = kv[:, HEAD_DIM:]
    heads = [slice(h * HEAD_DIM, (h + 1) * HEAD_DIM) for h in range(GROUP)]
    q = jnp.concatenate([q_ref[:, cols] for cols in heads], axis=0)
    up = jnp.concatenate([up_ref[:, cols] for cols in heads], axis=0)
    scores_all[...] = contract(q, keys, 1, 1)
    dp_all[...] = contract(up, values, 1, 1).astype(BF16)
    for h in range(GROUP):
        here = slice(h * rows, (h + 1) * rows)
        scores = scores_all[here, :] * (SCALE * LOG2E) + bias[...]
        expo = jnp.exp2(scores - jnp.max(scores, axis=-1, keepdims=True))
        probs = expo * (1.0 / jnp.sum(expo, axis=-1, keepdims=True))
        pbs[here, :] = probs.astype(BF16)
        dp = dp_all[here, :].astype(F32)
        ds = probs * (dp - jnp.sum(probs * dp, axis=-1, keepdims=True))
        hi = ds.astype(BF16)
        his[here, :] = hi
        los[here, :] = (ds - hi.astype(F32)).astype(BF16)
    att = contract(pbs[...], values, 1, 0).astype(BF16)
    gq = ((contract(his[...], keys, 1, 0) + contract(los[...], keys, 1, 0)) * SCALE).astype(BF16)
    for h, cols in enumerate(heads):
        att_ref[:, cols] = att[h * rows : (h + 1) * rows, :]
        gq_ref[:, cols] = gq[h * rows : (h + 1) * rows, :]
    dk = (contract(q, his[...], 0, 0) + contract(q, los[...], 0, 0)) * SCALE
    dv = contract(up, pbs[...], 0, 0)
    gkv_ref[0, :, :HEAD_DIM] = dk.T
    gkv_ref[0, :, HEAD_DIM:] = dv.T


def attend(heads, queries, upstream, kvs, query_blocks, key_blocks, before=(), wait=()):
    rows, width = queries.shape
    length, pair = kvs[0].shape
    count = len(kvs)
    span = GROUP * HEAD_DIM
    by_head = pl.BlockSpec((rows, span), lambda r, heads: (0, heads[r]))
    whole = pl.BlockSpec((length, pair), lambda r, heads: (0, 0))
    stacked = (GROUP * rows, length)
    return pl.pallas_call(
        functools.partial(attend_kernel, count),
        grid_spec=pltpu.PrefetchScalarGridSpec(
            num_scalar_prefetch=1,
            grid=(count,),
            in_specs=[by_head, by_head]
            + [whole] * count
            + [
                pl.BlockSpec((rows, 1), lambda r, heads: (0, 0)),
                pl.BlockSpec((1, length), lambda r, heads: (0, 0)),
            ]
            + [pl.BlockSpec(memory_space=pl.ANY)] * (len(before) + len(wait)),
            out_specs=[
                by_head,
                by_head,
                pl.BlockSpec((1, length, pair), lambda r, heads: (r, 0, 0)),
            ],
            scratch_shapes=[
                pltpu.VMEM((rows, length), F32),
                pltpu.VMEM(stacked, F32),
                pltpu.VMEM(stacked, BF16),
                pltpu.VMEM(stacked, BF16),
                pltpu.VMEM(stacked, BF16),
                pltpu.VMEM(stacked, BF16),
            ],
        ),
        out_shape=[
            jax.ShapeDtypeStruct((rows, width), BF16),
            jax.ShapeDtypeStruct((rows, width), BF16),
            jax.ShapeDtypeStruct((count, length, pair), F32),
        ],
        input_output_aliases={5 + count + i: i for i in range(len(before))},
        compiler_params=pltpu.CompilerParams(vmem_limit_bytes=32 * 1024 * 1024),
        cost_estimate=pl.CostEstimate(
            flops=2 * 7 * count * GROUP * rows * length * HEAD_DIM,
            bytes_accessed=8 * rows * count * span + 6 * count * length * pair,
            transcendentals=count * GROUP * rows * length,
        ),
    )(heads, queries, upstream, *kvs, query_blocks, key_blocks, *before, *wait)


def by_expert(kind, x):
    zero = jnp.zeros_like(x)
    return jnp.concatenate([jnp.where(kind == e, x, zero) for e in range(2)], axis=-1)


def hidden_kernel(quarters_ref, kind_ref, g_ref, gc_ref, w_ref, wc_ref, mine_ref, away_ref):
    rows = mine_ref.shape[0]
    sides = []
    for i in range(2):
        here = pl.ds(pl.multiple_of(quarters_ref[i] * rows, rows), rows)
        kind = kind_ref[here, :]
        sides.append([by_expert(kind, ref[here, :].astype(F32)).astype(BF16) for ref in (g_ref, gc_ref)])
    g = jnp.concatenate([sides[0][0], sides[1][0]], axis=0)
    gc = jnp.concatenate([sides[0][1], sides[1][1]], axis=0)
    total = contract(g, w_ref[...], 1, 1) + contract(gc, wc_ref[...], 1, 1)
    mine_ref[...] = total[:rows]
    away_ref[...] = total[rows:].astype(BF16)


def hidden_grad(quarters, kind, grad, grad_c, weight, weight_c, rows):
    width, span = weight.shape
    length, pair = grad.shape
    tile = 512
    whole = pl.BlockSpec((length, pair), lambda i, q: (0, 0))
    by_tile = pl.BlockSpec((tile, span), lambda i, q: (i, 0))
    out = pl.BlockSpec((rows, tile), lambda i, q: (0, i))
    return pl.pallas_call(
        hidden_kernel,
        grid_spec=pltpu.PrefetchScalarGridSpec(
            num_scalar_prefetch=1,
            grid=(width // tile,),
            in_specs=[pl.BlockSpec((length, 1), lambda i, q: (0, 0)), whole, whole, by_tile, by_tile],
            out_specs=[out, out],
        ),
        out_shape=[jax.ShapeDtypeStruct((rows, width), F32), jax.ShapeDtypeStruct((rows, width), BF16)],
        compiler_params=pltpu.CompilerParams(vmem_limit_bytes=24 * 1024 * 1024),
        cost_estimate=pl.CostEstimate(
            flops=8 * rows * width * span, bytes_accessed=4 * width * span + 6 * rows * width, transcendentals=0
        ),
    )(quarters, kind, grad, grad_c, weight, weight_c)


def weight_kernel(depth, quarters_ref, *refs):
    part_refs, (g_ref, out_ref, total) = refs[:-3], refs[-3:]
    step = pl.program_id(0)
    seqs, rows, lanes = part_refs[0].shape
    pair = g_ref.shape[-1]
    part = part_refs[0][...]
    for r in range(1, len(part_refs)):
        part = jnp.where(step == r, part_refs[r][...], part)
    part = part.reshape(seqs * rows, lanes)
    kind = part[:, depth : depth + 1].astype(F32)
    grads = g_ref[...].reshape(seqs * rows, pair).astype(F32)
    product = contract(part, by_expert(kind, grads).astype(BF16), 0, 0)

    @pl.when(step == 0)
    def _():
        total[...] = product

    @pl.when(step != 0)
    def _():
        total[...] += product

    @pl.when(step == len(part_refs) - 1)
    def _():
        for e in range(2):
            out_ref[e] = total[:depth, e * pair : (e + 1) * pair]


def weight_grad(quarters, parts, grads, depth):
    seqs, rows, lanes = parts[0].shape
    pair = grads.shape[-1]
    count = len(parts)
    return pl.pallas_call(
        functools.partial(weight_kernel, depth),
        grid_spec=pltpu.PrefetchScalarGridSpec(
            num_scalar_prefetch=1,
            grid=(count,),
            in_specs=[pl.BlockSpec((seqs, rows, lanes), lambda r, q: (0, 0, 0))] * count
            + [pl.BlockSpec((seqs, rows, pair), lambda r, q: (0, q[r], 0))],
            out_specs=pl.BlockSpec((2, depth, pair), lambda r, q: (0, 0, 0)),
            scratch_shapes=[pltpu.VMEM((lanes, 2 * pair), F32)],
        ),
        out_shape=jax.ShapeDtypeStruct((2, depth, pair), F32),
        compiler_params=pltpu.CompilerParams(vmem_limit_bytes=40 * 1024 * 1024),
        cost_estimate=pl.CostEstimate(
            flops=4 * count * seqs * rows * lanes * pair,
            bytes_accessed=2 * count * seqs * rows * (lanes + pair) + 8 * depth * pair,
            transcendentals=0,
        ),
    )(quarters, *parts, grads)


def per_device(fsdp, seq, tokens, queries, cotangent, modality, block_ids, kv_weight):
    tokens, queries, cotangent = tokens[0], queries[0], cotangent[0]
    me_f = lax.axis_index("fsdp")
    me_s = lax.axis_index("seq")
    rows, width = tokens.shape
    depth, pair = kv_weight.shape[1:]
    length = seq * rows

    def swap(x, bit):
        return lax.ppermute(x, "seq", [(i, i ^ bit) for i in range(seq)])

    def over_seq(x):
        across = swap(x, 2)
        return [x, swap(x, 1), across, swap(across, 1)]

    def place(parts):
        whole = jnp.zeros((seq, *parts[0].shape), parts[0].dtype)
        for r, part in enumerate(parts):
            whole = lax.dynamic_update_index_in_dim(whole, part, me_s ^ r, 0)
        return whole

    def over_fsdp(x, hold=None):
        if fsdp != 8:
            return lax.all_gather(x, "fsdp", axis=0)
        cycle = [0, 2, 4, 6, 7, 5, 3, 1]
        order = jnp.array(cycle, jnp.int32)
        spot = jnp.array([cycle.index(i) for i in range(fsdp)], jnp.int32)[me_f]

        def turn(y, by):
            return lax.ppermute(y, "fsdp", [(cycle[i], cycle[(i + by) % fsdp]) for i in range(fsdp)])

        whole = jnp.zeros((fsdp, *x.shape), x.dtype)
        whole = lax.dynamic_update_index_in_dim(whole, x, me_f, 0)
        half = x.shape[0] // 2
        ups, downs = x, x
        for step in range(1, 5):
            if step == 2 and hold is not None:
                ups, downs = after(ups, *hold), after(downs, *hold)
            if step == 4:
                ups, downs = ups[:half], downs[half:]
            ups, downs = turn(ups, 1), turn(downs, -1)
            before = order[lax.rem(spot + fsdp - step, fsdp)]
            behind = order[lax.rem(spot + step, fsdp)]
            whole = lax.dynamic_update_slice(whole, ups[None], (before, 0, 0))
            whole = lax.dynamic_update_slice(whole, downs[None], (behind, half if step == 4 else 0, 0))
        return whole

    both = jnp.concatenate([kv_weight[0], kv_weight[1]], axis=-1)
    weight = over_fsdp(both).reshape(width, 2 * pair)
    hidden = place(over_seq(tokens)).reshape(length, width)
    ids = place(over_seq(jnp.stack([modality[0], block_ids[0]])))
    modal_here = ids[:, 0].reshape(length, 1)
    blocks_here = ids[:, 1].reshape(1, length)

    parts = jnp.dot(hidden, weight, preferred_element_type=F32)
    key_value = jnp.where(modal_here == 1, parts[:, pair:], parts[:, :pair]).astype(BF16)

    kvs = over_seq(key_value)
    heads = me_s ^ jnp.arange(seq, dtype=jnp.int32)
    given = (block_ids[0][:, None], blocks_here)
    out_a, out_q, far_c = attend(heads[3:], queries, cotangent, kvs[3:], *given)
    out_a, out_q, far = attend(heads[2:3], queries, cotangent, kvs[2:3], *given, (out_a, out_q))
    far = far[0] + swap(far_c[0], 1)
    attended, grad_queries, near = attend(heads[:2], queries, cotangent, kvs[:2], *given, (out_a, out_q), (far,))
    grad_kv = (near[0] + swap(near[1], 1) + swap(far, 2)).astype(BF16)

    lanes = -(-(depth + 1) // 128) * 128
    columns = tokens.reshape(rows, fsdp, depth).transpose(1, 0, 2)
    kinds = jnp.broadcast_to(modality[0].astype(BF16)[None, :, None], (fsdp, rows, 1))
    blank = jnp.zeros((fsdp, rows, lanes - depth - 1), BF16)
    columns = jnp.concatenate([columns, kinds, blank], axis=-1)
    columns = lax.all_to_all(columns, "fsdp", split_axis=0, concat_axis=0, tiled=True)
    columns = over_seq(columns)

    weight_c = swap(weight, 1)
    mine, away = hidden_grad(
        jnp.stack([me_s, me_s ^ 2]), modal_here, grad_kv, swap(grad_kv, 1), weight, weight_c, rows
    )
    grad_weight = weight_grad(heads, columns, over_fsdp(grad_kv, (away,)), depth)
    grad_tokens = (mine + swap(away, 2).astype(F32)).astype(BF16)
    return attended[None], grad_queries[None], grad_tokens[None], grad_weight


def solution(mesh):
    split = P("fsdp", "seq", None)
    weights = P(None, "fsdp", "seq")
    return jax.shard_map(
        functools.partial(per_device, mesh.shape["fsdp"], mesh.shape["seq"]),
        mesh=mesh,
        in_specs=(split, split, split, P("fsdp", "seq"), P("fsdp", "seq"), weights),
        out_specs=(split, split, split, weights),
        check_vma=False,
    )
```

```python
import functools

import jax
import jax.numpy as jnp
from jax import lax
from jax.experimental import pallas as pl
from jax.experimental.pallas import tpu as pltpu
from jax.sharding import PartitionSpec as P

HEAD_DIM = 128
GROUP = 7
SPAN = GROUP * HEAD_DIM
PAIR = 2 * HEAD_DIM
SCALE = HEAD_DIM ** (-0.5)
LOG2E = 1.4426950408889634
HIDDEN = -1e30
DIGIT = 16
F32 = jnp.float32
BF16 = jnp.bfloat16
ANYWHERE = pl.BlockSpec(memory_space=pl.ANY)
CYCLE = (0, 2, 4, 6, 7, 5, 3, 1)


def contract(a, b, da, db):
    return lax.dot_general(a, b, (((da,), (db,)), ((), ())), preferred_element_type=F32)


def shaped(shape, dtype):
    return jax.ShapeDtypeStruct(shape, dtype)


def constant_block(shape):
    return pl.BlockSpec(shape, lambda i, *prefetched: (0,) * len(shape))


def call(body, grid, prefetched, operands, in_specs, out_specs, out_shape, flops, scratch=(), aliases=None, mib=32):
    moved = sum(x.size * x.dtype.itemsize for x in operands)
    return pl.pallas_call(
        body,
        grid_spec=pltpu.PrefetchScalarGridSpec(
            num_scalar_prefetch=len(prefetched),
            grid=(grid,),
            in_specs=in_specs,
            out_specs=out_specs,
            scratch_shapes=scratch,
        ),
        out_shape=out_shape,
        input_output_aliases=aliases or {},
        compiler_params=pltpu.CompilerParams(vmem_limit_bytes=mib * 1024 * 1024),
        cost_estimate=pl.CostEstimate(flops=flops, bytes_accessed=moved, transcendentals=0),
    )(*prefetched, *operands)


def after(x, *others):
    return pl.pallas_call(
        lambda *refs: None,
        in_specs=[ANYWHERE] * (1 + len(others)),
        out_specs=ANYWHERE,
        out_shape=shaped(x.shape, x.dtype),
        input_output_aliases={0: 0},
        cost_estimate=pl.CostEstimate(flops=0, bytes_accessed=0, transcendentals=0),
    )(x, *others)


def blocks_kernel(depth, tok_ref, kind_ref, ids_ref, out_ref):
    count, rows, lanes = out_ref.shape
    base = lanes - 128
    lane = lax.broadcasted_iota(jnp.int32, (rows, 128), 1) - (depth - base)
    ids = ids_ref[...]
    marks = (kind_ref[...], lax.div(ids, DIGIT), lax.rem(ids, DIGIT))
    for j in range(count):
        out_ref[j, :, :depth] = tok_ref[:, j * depth : (j + 1) * depth]
        last = out_ref[j, :, base:].astype(F32)
        last = jnp.where(lane >= 0, 0.0, last)
        for i, mark in enumerate(marks):
            last = jnp.where(lane == i, mark.astype(F32), last)
        out_ref[j, :, base:] = last.astype(BF16)


def token_blocks(tokens, kinds, ids, count):
    rows, width = tokens.shape
    depth = width // count
    lanes = -(-(depth + 3) // 128) * 128
    return call(
        functools.partial(blocks_kernel, depth),
        1,
        (),
        (tokens, kinds, ids),
        [constant_block((rows, width)), constant_block((rows, 1)), constant_block((rows, 1))],
        constant_block((count, rows, lanes)),
        shaped((count, rows, lanes), BF16),
        0,
    )


def read_marks(block, depth):
    mark = [block[:, depth + i : depth + i + 1].astype(F32) for i in range(3)]
    return mark[0], mark[1] * DIGIT + mark[2]


def pack_kernel(heads_ref, q_ref, up_ref, out_ref):
    out_ref[0, 0] = q_ref[...]
    out_ref[0, 1] = up_ref[...]


def pack_heads(heads, queries, upstream):
    rows = queries.shape[0]
    by_head = pl.BlockSpec((rows, SPAN), lambda i, heads: (0, heads[i]))
    return call(
        pack_kernel,
        2,
        (heads,),
        (queries, upstream),
        [by_head, by_head],
        pl.BlockSpec((1, 2, rows, SPAN), lambda i, heads: (i, 0, 0, 0)),
        shaped((2, 2, rows, SPAN), BF16),
        0,
    )


def place_kernel(heads_ref, near_ref, far_ref, att_in, gq_in, att_ref, gq_ref):
    step = pl.program_id(0)
    for i, ref in enumerate((near_ref, far_ref)):

        @pl.when(step == i)
        def _():
            att_ref[...] = ref[0]
            gq_ref[...] = ref[1]


def place_heads(heads, near, far, attended, grad_queries):
    rows = attended.shape[0]
    by_head = pl.BlockSpec((rows, SPAN), lambda i, heads: (0, heads[i]))
    return call(
        place_kernel,
        2,
        (heads,),
        (near, far, attended, grad_queries),
        [constant_block(near.shape)] * 2 + [ANYWHERE] * 2,
        [by_head, by_head],
        [shaped(attended.shape, BF16)] * 2,
        0,
        aliases={3: 0, 4: 1},
    )


def project_kernel(depth, count, halves, first, last, quarters_ref, owners_ref, *refs):
    parts, refs = refs[: 4 * count], refs[4 * count :]
    weights, refs = refs[: count + halves], refs[count + halves :]
    rows, lanes = parts[0].shape[1:]
    sums = [0.0, 0.0]
    for b in range(count):
        left = jnp.concatenate([ref[0][:, :depth] for ref in parts[4 * b : 4 * b + 4]], axis=0)
        for e in range(2):
            right = jnp.concatenate([ref[e] for ref in weights], axis=0) if halves else weights[b][e]
            sums[e] = sums[e] + contract(left, right, 1, 0)
    if not first:
        sums = [s + refs[0][:, e * PAIR : (e + 1) * PAIR] for e, s in enumerate(sums)]
        refs = refs[1:]
    if not last:
        for e in range(2):
            refs[0][:, e * PAIR : (e + 1) * PAIR] = sums[e]
        return
    kv_ref, kind_ref, ids_ref, ids_row_ref = refs
    for r in range(4):
        here = pl.ds(pl.multiple_of(quarters_ref[r] * rows, rows), rows)
        kind, ids = read_marks(parts[r][0], depth)
        mine = slice(r * rows, (r + 1) * rows)
        kv_ref[here, :] = jnp.where(kind == 1.0, sums[1][mine], sums[0][mine]).astype(BF16)
        kind_ref[here, :] = kind
        ids_ref[here, :] = ids
    ids_row_ref[...] = jnp.broadcast_to(ids_ref[...], (4 * rows, 128)).T[:1]


def project(quarters, owners, parts, weights, total, depth, last, halves):
    rows, lanes = parts[0].shape[1:]
    count = 1 if halves else len(weights)
    length = 4 * rows
    part_specs = [
        pl.BlockSpec((1, rows, lanes), functools.partial(lambda b, i, q, o: (o[b], 0, 0), b))
        for b in range(count)
        for _ in range(4)
    ]
    full = (length, 2 * PAIR)
    before = [] if total is None else [total]
    if last:
        outs = [(length, PAIR), (length, 1), (length, 1), (1, length)]
        out_specs = [constant_block(shape) for shape in outs]
        out_shape = [shaped(shape, BF16 if i == 0 else F32) for i, shape in enumerate(outs)]
    else:
        out_specs, out_shape = constant_block(full), shaped(full, F32)
    operands = (*(list(parts) * count), *weights, *before)
    return call(
        functools.partial(project_kernel, depth, count, int(halves), total is None, last),
        1,
        (quarters, owners),
        operands,
        part_specs + [constant_block(w.shape) for w in weights] + [constant_block(full)] * len(before),
        out_specs,
        out_shape,
        4 * length * depth * PAIR * count,
        aliases={1 + len(operands): 0} if before and not last else None,
    )


def attend_kernel(spot, where_ref, q_ref, up_ref, pack_ref, kv_ref, ids_ref, ids_row_ref, *refs):
    att_ref, gq_ref, other_ref, gkv_ref, bias, scores_all, dp_all, pbs, his, los = refs[-10:]
    rows = q_ref.shape[0]
    heads = [slice(h * HEAD_DIM, (h + 1) * HEAD_DIM) for h in range(GROUP)]
    for i in range(2):
        here = pl.ds(pl.multiple_of(where_ref[1 + i] * rows, rows), rows)
        bias[i * rows : (i + 1) * rows, :] = jnp.where(ids_row_ref[...] <= ids_ref[here, :], 0.0, HIDDEN)
    keys = kv_ref[:, :HEAD_DIM]
    values = kv_ref[:, HEAD_DIM:]
    q = jnp.concatenate([q_ref[:, cols] for cols in heads] + [pack_ref[0, 0, :, cols] for cols in heads], axis=0)
    up = jnp.concatenate([up_ref[:, cols] for cols in heads] + [pack_ref[0, 1, :, cols] for cols in heads], axis=0)
    scores_all[...] = contract(q, keys, 1, 1)
    dp_all[...] = contract(up, values, 1, 1).astype(BF16)
    for h in range(2 * GROUP):
        here = slice(h * rows, (h + 1) * rows)
        side = h // GROUP
        scores = scores_all[here, :] * (SCALE * LOG2E) + bias[side * rows : (side + 1) * rows, :]
        expo = jnp.exp2(scores - jnp.max(scores, axis=-1, keepdims=True))
        probs = expo * (1.0 / jnp.sum(expo, axis=-1, keepdims=True))
        pbs[here, :] = probs.astype(BF16)
        dp = dp_all[here, :].astype(F32)
        ds = probs * (dp - jnp.sum(probs * dp, axis=-1, keepdims=True))
        hi = ds.astype(BF16)
        his[here, :] = hi
        los[here, :] = (ds - hi.astype(F32)).astype(BF16)
    att = contract(pbs[...], values, 1, 0).astype(BF16)
    gq = ((contract(his[...], keys, 1, 0) + contract(los[...], keys, 1, 0)) * SCALE).astype(BF16)
    for h, cols in enumerate(heads):
        here = slice(h * rows, (h + 1) * rows)
        there = slice((GROUP + h) * rows, (GROUP + h + 1) * rows)
        att_ref[:, cols] = att[here]
        gq_ref[:, cols] = gq[here]
        other_ref[0, :, cols] = att[there]
        other_ref[1, :, cols] = gq[there]
    dk = (contract(q, his[...], 0, 0) + contract(q, los[...], 0, 0)) * SCALE
    dv = contract(up, pbs[...], 0, 0)
    gkv_ref[:, :HEAD_DIM] = dk.T
    gkv_ref[:, HEAD_DIM:] = dv.T


def attend(where, spot, queries, upstream, pack, kv, ids, ids_row, before=()):
    rows, width = queries.shape
    length = kv.shape[0]
    by_head = pl.BlockSpec((rows, SPAN), lambda i, where: (0, where[0]))
    stacked = (2 * GROUP * rows, length)
    operands = (queries, upstream, pack, kv, ids, ids_row, *before)
    return call(
        functools.partial(attend_kernel, spot),
        1,
        (where,),
        operands,
        [
            by_head,
            by_head,
            pl.BlockSpec((1, 2, rows, SPAN), lambda i, where: (spot, 0, 0, 0)),
            constant_block((length, PAIR)),
            constant_block((length, 1)),
            constant_block((1, length)),
        ]
        + [ANYWHERE] * len(before),
        [by_head, by_head, constant_block((2, rows, SPAN)), constant_block((length, PAIR))],
        [
            shaped((rows, width), BF16),
            shaped((rows, width), BF16),
            shaped((2, rows, SPAN), BF16),
            shaped((length, PAIR), F32),
        ],
        16 * 2 * GROUP * rows * length * HEAD_DIM,
        scratch=[pltpu.VMEM((2 * rows, length), F32), pltpu.VMEM(stacked, F32)] + [pltpu.VMEM(stacked, BF16)] * 4,
        aliases={7 + i: i for i in range(len(before))},
        mib=40,
    )


def by_expert(kind, x):
    return [jnp.where(kind == float(e), x, 0.0).astype(BF16) for e in range(2)]


def hidden_kernel(quarters_ref, kind_ref, g_ref, gc_ref, w_ref, wc_ref, mine_ref, away_ref, masked):
    rows = mine_ref.shape[0]

    @pl.when(pl.program_id(0) == 0)
    def _():
        for i in range(2):
            here = pl.ds(pl.multiple_of(quarters_ref[i] * rows, rows), rows)
            for k, ref in enumerate((g_ref, gc_ref)):
                for e, part in enumerate(by_expert(kind_ref[here, :], ref[here, :].astype(F32))):
                    masked[2 * k + e, i * rows : (i + 1) * rows, :] = part

    total = 0.0
    for k, ref in enumerate((w_ref, wc_ref)):
        for e in range(2):
            total = total + contract(masked[2 * k + e], ref[:, e].reshape(-1, PAIR), 1, 1)
    mine_ref[...] = total[:rows]
    away_ref[...] = total[rows:].astype(BF16)


def hidden_grad(quarters, kind, grad, grad_c, weight, weight_c, rows):
    count, _, depth, _ = weight.shape
    length = grad.shape[0]
    group = count // 4
    by_tile = pl.BlockSpec((group, 2, depth, PAIR), lambda i, q: (i, 0, 0, 0))
    out = pl.BlockSpec((rows, group * depth), lambda i, q: (0, i))
    width = count * depth
    return call(
        hidden_kernel,
        4,
        (quarters,),
        (kind, grad, grad_c, weight, weight_c),
        [constant_block((length, 1)), constant_block((length, PAIR)), constant_block((length, PAIR)), by_tile, by_tile],
        [out, out],
        [shaped((rows, width), F32), shaped((rows, width), BF16)],
        16 * rows * width * PAIR,
        scratch=[pltpu.VMEM((4, 2 * rows, PAIR), BF16)],
    )


def weight_kernel(depth, count, halves, first, last, quarters_ref, owners_ref, *refs):
    parts, refs = refs[: 4 * count], refs[4 * count :]
    grads, refs = refs[: count + halves], refs[count + halves :]
    rows, lanes = parts[0].shape[1:]
    size = grads[0].shape[0]
    total = 0.0
    for b in range(count):
        left = jnp.concatenate([ref[0] for ref in parts[4 * b : 4 * b + 4]], axis=0)
        quarter = []
        for r in range(4):
            start = quarters_ref[r] * rows
            if halves:
                inner = pl.ds(pl.multiple_of(lax.rem(start, size), rows), rows)
                quarter.append(jnp.where(start < size, grads[0][inner, :].astype(F32), grads[1][inner, :].astype(F32)))
            else:
                quarter.append(grads[b][pl.ds(pl.multiple_of(start, rows), rows), :].astype(F32))
        kind = left[:, depth : depth + 1].astype(F32)
        right = jnp.concatenate(by_expert(kind, jnp.concatenate(quarter, axis=0)), axis=-1)
        total = total + contract(left, right, 0, 0)
    if not first:
        total = total + refs[0][...]
        refs = refs[1:]
    if not last:
        refs[0][...] = total
        return
    for e in range(2):
        refs[0][e] = total[:depth, e * PAIR : (e + 1) * PAIR]


def weight_grad(quarters, owners, parts, grads, total, depth, last, halves):
    rows, lanes = parts[0].shape[1:]
    count = 1 if halves else len(grads)
    part_specs = [
        pl.BlockSpec((1, rows, lanes), functools.partial(lambda b, i, q, o: (o[b], 0, 0), b))
        for b in range(count)
        for _ in range(4)
    ]
    full = (lanes, 2 * PAIR)
    out = (2, depth, PAIR) if last else full
    before = [] if total is None else [total]
    operands = (*(list(parts) * count), *grads, *before)
    return call(
        functools.partial(weight_kernel, depth, count, int(halves), total is None, last),
        1,
        (quarters, owners),
        operands,
        part_specs + [constant_block(g.shape) for g in grads] + [constant_block(full)] * len(before),
        constant_block(out),
        shaped(out, F32),
        16 * rows * lanes * PAIR * count,
        aliases={1 + len(operands): 0} if before and not last else None,
    )


def in_order(parts, quarters):
    count, rows, lanes = parts[0].shape
    whole = jnp.stack(parts, axis=1)
    return jnp.take(whole, quarters, axis=1).reshape(count, 4 * rows, lanes)


def project_plain(quarters, parts, weights, depth):
    tokens = in_order(parts, quarters)
    kind, ids = read_marks(tokens[0], depth)
    sums = jnp.einsum("jmk,jekn->emn", tokens[:, :, :depth], weights, preferred_element_type=F32)
    return jnp.where(kind == 1.0, sums[1], sums[0]).astype(BF16), kind, ids, ids.reshape(1, -1)


def weight_plain(quarters, parts, grads, depth):
    tokens = in_order(parts, quarters)
    kind = tokens[:, :, depth : depth + 1].astype(F32)
    sums = [
        jnp.einsum("jmk,jmn->kn", tokens[:, :, :depth], g, preferred_element_type=F32)
        for g in by_expert(kind, grads.astype(F32))
    ]
    return jnp.stack(sums)


def per_device(fsdp, seq, tokens, queries, cotangent, modality, block_ids, kv_weight):
    tokens, queries, cotangent = tokens[0], queries[0], cotangent[0]
    me_f = lax.axis_index("fsdp")
    me_s = lax.axis_index("seq")
    rows, width = tokens.shape
    depth = kv_weight.shape[1]
    near_link = fsdp == len(CYCLE)

    def swap(x, bit):
        return lax.ppermute(x, "seq", [(i, i ^ bit) for i in range(seq)])

    def over_seq(x):
        across = swap(x, 2)
        return [x, swap(x, 1), across, swap(across, 1)]

    def turn(x, by):
        return lax.ppermute(x, "fsdp", [(CYCLE[i], CYCLE[(i + by) % fsdp]) for i in range(fsdp)])

    if near_link:
        spot = jnp.array([CYCLE.index(i) for i in range(fsdp)], jnp.int32)[me_f]
        order = jnp.array(CYCLE, jnp.int32)
        around = [order[lax.rem(spot + fsdp + by, fsdp)] for by in (0, -1, 1, -2, 2, -3, 3, 4)]

    def round_cycle(x, cut, hold=None):
        ups, downs = x, x
        found = [x]
        for step in range(1, 5):
            if step == 4:
                size = x.shape[cut] // 2
                ups = lax.slice_in_dim(ups, 0, size, axis=cut)
                downs = lax.slice_in_dim(downs, size, 2 * size, axis=cut)
            if step == 2 and hold is not None:
                ups, downs = after(ups, hold), after(downs, hold)
            ups, downs = turn(ups, 1), turn(downs, -1)
            found += [ups, downs]
        return found

    quarters = me_s ^ jnp.arange(seq, dtype=jnp.int32)
    if near_link:
        weights = round_cycle(kv_weight, 1)
    else:
        weight = lax.all_gather(kv_weight, "fsdp", axis=0)

    own_blocks = token_blocks(tokens, modality.reshape(rows, 1), block_ids.reshape(rows, 1), fsdp)
    parts = over_seq(own_blocks)
    pack = swap(pack_heads(me_s ^ jnp.array([1, 3], jnp.int32), queries, cotangent), 1)
    columns = over_seq(lax.all_to_all(own_blocks, "fsdp", split_axis=0, concat_axis=0, tiled=True))

    if near_link:
        groups = ((0, 5), (5, 7), (7, 8))
        owners = [jnp.stack(around[a:b]) for a, b in groups]
        total = project(quarters, owners[0], parts, weights[:5], None, depth, False, False)
        total = project(quarters, owners[1], parts, weights[5:7], total, depth, False, False)
        kv, kind, ids, ids_row = project(quarters, owners[2], parts, weights[7:], total, depth, True, True)
        weight = jnp.zeros((fsdp, *kv_weight.shape), BF16)
        for owner, block in zip(around, weights[:7]):
            weight = lax.dynamic_update_index_in_dim(weight, block, owner, 0)
        for i, block in enumerate(weights[7:]):
            weight = lax.dynamic_update_slice(weight, block[None], (around[7], 0, i * (depth // 2), 0))
    else:
        kv, kind, ids, ids_row = project_plain(quarters, parts, weight, depth)
    weight_c = swap(weight, 1)

    where_near = jnp.stack([me_s, me_s, me_s ^ 1])
    where_far = jnp.stack([me_s ^ 2, me_s, me_s ^ 1])
    kv_far = swap(kv, 2)
    attended, grad_queries, other_near, near = attend(where_near, 0, queries, cotangent, pack, kv, ids, ids_row)
    attended, grad_queries, other_far, far = attend(
        where_far, 1, queries, cotangent, pack, kv_far, ids, ids_row, (attended, grad_queries)
    )
    grad_kv = (near + swap(far, 2)).astype(BF16)
    attended, grad_queries = place_heads(
        me_s ^ jnp.array([1, 3], jnp.int32), swap(other_near, 1), swap(other_far, 1), attended, grad_queries
    )

    mine, away = hidden_grad(
        jnp.stack([me_s, me_s ^ 2]), kind, grad_kv, swap(grad_kv, 1), weight, weight_c, rows
    )
    if near_link:
        grads = round_cycle(grad_kv, 0, away)
        total = weight_grad(quarters, owners[0], columns, grads[:5], None, depth, False, False)
        total = weight_grad(quarters, owners[1], columns, grads[5:7], total, depth, False, False)
        grad_weight = weight_grad(quarters, owners[2], columns, grads[7:], total, depth, True, True)
    else:
        grad_weight = weight_plain(quarters, columns, lax.all_gather(grad_kv, "fsdp", axis=0), depth)
    grad_tokens = (mine + swap(away, 2).astype(F32)).astype(BF16)
    return attended[None], grad_queries[None], grad_tokens[None], grad_weight


def solution(mesh):
    split = P("fsdp", "seq", None)
    weights = P(None, "fsdp", "seq")
    return jax.shard_map(
        functools.partial(per_device, mesh.shape["fsdp"], mesh.shape["seq"]),
        mesh=mesh,
        in_specs=(split, split, split, P("fsdp", "seq"), P("fsdp", "seq"), weights),
        out_specs=(split, split, split, weights),
        check_vma=False,
    )
```

```python
import functools

import jax
import jax.numpy as jnp
from jax import lax
from jax.experimental import pallas as pl
from jax.experimental.pallas import tpu as pltpu
from jax.sharding import PartitionSpec as P

HEAD_DIM = 128
GROUP = 7
SPAN = GROUP * HEAD_DIM
PAIR = 2 * HEAD_DIM
SCALE = HEAD_DIM ** (-0.5)
LOG2E = 1.4426950408889634
HIDDEN = -1e30
DIGIT = 16
F32 = jnp.float32
BF16 = jnp.bfloat16
ANYWHERE = pl.BlockSpec(memory_space=pl.ANY)
CYCLE = (0, 2, 4, 6, 7, 5, 3, 1)
STEPS = (0, -1, 1, -2, 2, -3, 3, 4)


def contract(a, b, da, db):
    return lax.dot_general(a, b, (((da,), (db,)), ((), ())), preferred_element_type=F32)


def shaped(shape, dtype):
    return jax.ShapeDtypeStruct(shape, dtype)


def constant_block(shape):
    return pl.BlockSpec(shape, lambda i, *prefetched: (0,) * len(shape))


def call(body, grid, prefetched, operands, in_specs, out_specs, out_shape, flops, scratch=(), aliases=None):
    moved = sum(x.size * x.dtype.itemsize for x in operands)
    return pl.pallas_call(
        body,
        grid_spec=pltpu.PrefetchScalarGridSpec(
            num_scalar_prefetch=len(prefetched),
            grid=(grid,),
            in_specs=in_specs,
            out_specs=out_specs,
            scratch_shapes=scratch,
        ),
        out_shape=out_shape,
        input_output_aliases=aliases or {},
        compiler_params=pltpu.CompilerParams(vmem_limit_bytes=56 * 1024 * 1024),
        cost_estimate=pl.CostEstimate(flops=flops, bytes_accessed=moved, transcendentals=0),
    )(*prefetched, *operands)


def owner_at(me_f, by):
    size = len(CYCLE)
    half = size // 2
    line, side = lax.div(me_f, 2), lax.rem(me_f, 2)
    spot = jnp.where(side == 1, size - 1 - line, line)
    spot = lax.rem(spot + (size + by), size)
    return jnp.where(spot < half, 2 * spot, 2 * (size - 1 - spot) + 1)


def after(x, *others):
    return pl.pallas_call(
        lambda *refs: None,
        in_specs=[ANYWHERE] * (1 + len(others)),
        out_specs=ANYWHERE,
        out_shape=shaped(x.shape, x.dtype),
        input_output_aliases={0: 0},
        cost_estimate=pl.CostEstimate(flops=0, bytes_accessed=0, transcendentals=0),
    )(x, *others)


def blocks_kernel(depth, tok_ref, kind_ref, ids_ref, out_ref):
    count, rows, lanes = out_ref.shape
    base = lanes - 128
    lane = lax.broadcasted_iota(jnp.int32, (rows, 128), 1) - (depth - base)
    ids = ids_ref[...]
    marks = (kind_ref[...], lax.div(ids, DIGIT), lax.rem(ids, DIGIT))
    for j in range(count):
        out_ref[j, :, :depth] = tok_ref[:, j * depth : (j + 1) * depth]
        last = out_ref[j, :, base:].astype(F32)
        last = jnp.where(lane >= 0, 0.0, last)
        for i, mark in enumerate(marks):
            last = jnp.where(lane == i, mark.astype(F32), last)
        out_ref[j, :, base:] = last.astype(BF16)


def token_blocks(tokens, kinds, ids, count):
    rows, width = tokens.shape
    depth = width // count
    lanes = -(-(depth + 3) // 128) * 128
    return call(
        functools.partial(blocks_kernel, depth),
        1,
        (),
        (tokens, kinds, ids),
        [constant_block((rows, width)), constant_block((rows, 1)), constant_block((rows, 1))],
        constant_block((count, rows, lanes)),
        shaped((count, rows, lanes), BF16),
        0,
    )


def read_marks(block, depth):
    mark = [block[:, depth + i : depth + i + 1].astype(F32) for i in range(3)]
    return mark[0], mark[1] * DIGIT + mark[2]


def pack_kernel(me_ref, q_ref, up_ref, out_ref):
    out_ref[0, 0] = q_ref[...]
    out_ref[0, 1] = up_ref[...]


def pack_heads(me, queries, upstream):
    rows = queries.shape[0]
    by_head = pl.BlockSpec((rows, SPAN), lambda i, me: (0, me[0] ^ (1 + 2 * i)))
    return call(
        pack_kernel,
        2,
        (me,),
        (queries, upstream),
        [by_head, by_head],
        pl.BlockSpec((1, 2, rows, SPAN), lambda i, me: (i, 0, 0, 0)),
        shaped((2, 2, rows, SPAN), BF16),
        0,
    )


def place_kernel(me_ref, near_ref, far_ref, att_in, gq_in, att_ref, gq_ref):
    step = pl.program_id(0)
    for i, ref in enumerate((near_ref, far_ref)):

        @pl.when(step == i)
        def _():
            att_ref[...] = ref[0]
            gq_ref[...] = ref[1]


def place_heads(me, near, far, attended, grad_queries):
    rows = attended.shape[0]
    by_head = pl.BlockSpec((rows, SPAN), lambda i, me: (0, me[0] ^ (1 + 2 * i)))
    return call(
        place_kernel,
        2,
        (me,),
        (near, far, attended, grad_queries),
        [constant_block(near.shape)] * 2 + [ANYWHERE] * 2,
        [by_head, by_head],
        [shaped(attended.shape, BF16)] * 2,
        0,
        aliases={3: 0, 4: 1},
    )


def project_kernel(depth, count, halves, first, last, me_ref, *refs):
    parts, refs = refs[: 4 * count], refs[4 * count :]
    weights, refs = refs[: count + halves], refs[count + halves :]
    rows, lanes = parts[0].shape[1:]
    sums = [0.0, 0.0]
    for b in range(count):
        left = jnp.concatenate([ref[0][:, :depth] for ref in parts[4 * b : 4 * b + 4]], axis=0)
        for e in range(2):
            right = jnp.concatenate([ref[e] for ref in weights], axis=0) if halves else weights[b][e]
            sums[e] = sums[e] + contract(left, right, 1, 0)
    if not first:
        sums = [s + refs[0][:, e * PAIR : (e + 1) * PAIR] for e, s in enumerate(sums)]
        refs = refs[1:]
    if not last:
        for e in range(2):
            refs[0][:, e * PAIR : (e + 1) * PAIR] = sums[e]
        return
    kv_ref, kind_ref, ids_ref, ids_row_ref = refs
    for r in range(4):
        here = pl.ds(pl.multiple_of((me_ref[0] ^ r) * rows, rows), rows)
        kind, ids = read_marks(parts[r][0], depth)
        mine = slice(r * rows, (r + 1) * rows)
        kv_ref[here, :] = jnp.where(kind == 1.0, sums[1][mine], sums[0][mine]).astype(BF16)
        kind_ref[here, :] = kind
        ids_ref[here, :] = ids
    ids_row_ref[...] = jnp.broadcast_to(ids_ref[...], (4 * rows, 128)).T[:1]


def project(me, steps, parts, weights, total, depth, last, halves):
    rows, lanes = parts[0].shape[1:]
    count = 1 if halves else len(weights)
    length = 4 * rows
    part_specs = [
        pl.BlockSpec((1, rows, lanes), functools.partial(lambda by, i, me: (owner_at(me[1], by), 0, 0), by))
        for by in steps
        for _ in range(4)
    ]
    full = (length, 2 * PAIR)
    before = [] if total is None else [total]
    if last:
        outs = [(length, PAIR), (length, 1), (length, 1), (1, length)]
        out_specs = [constant_block(shape) for shape in outs]
        out_shape = [shaped(shape, BF16 if i == 0 else F32) for i, shape in enumerate(outs)]
    else:
        out_specs, out_shape = constant_block(full), shaped(full, F32)
    operands = (*(list(parts) * count), *weights, *before)
    return call(
        functools.partial(project_kernel, depth, count, int(halves), total is None, last),
        1,
        (me,),
        operands,
        part_specs + [constant_block(w.shape) for w in weights] + [constant_block(full)] * len(before),
        out_specs,
        out_shape,
        4 * length * depth * PAIR * count,
        aliases={len(operands): 0} if before and not last else None,
    )


def attend_kernel(spot, me_ref, q_ref, up_ref, pack_ref, kv_ref, ids_ref, ids_row_ref, *refs):
    att_ref, gq_ref, other_ref, gkv_ref, bias, scores_all, dp_all, pbs, his, los = refs[-10:]
    rows = q_ref.shape[0]
    heads = [slice(h * HEAD_DIM, (h + 1) * HEAD_DIM) for h in range(GROUP)]
    for i in range(2):
        here = pl.ds(pl.multiple_of((me_ref[0] ^ i) * rows, rows), rows)
        bias[i * rows : (i + 1) * rows, :] = jnp.where(ids_row_ref[...] <= ids_ref[here, :], 0.0, HIDDEN)
    keys = kv_ref[:, :HEAD_DIM]
    values = kv_ref[:, HEAD_DIM:]
    q = jnp.concatenate([q_ref[:, cols] for cols in heads] + [pack_ref[0, 0, :, cols] for cols in heads], axis=0)
    up = jnp.concatenate([up_ref[:, cols] for cols in heads] + [pack_ref[0, 1, :, cols] for cols in heads], axis=0)
    scores_all[...] = contract(q, keys, 1, 1)
    dp_all[...] = contract(up, values, 1, 1).astype(BF16)
    for h in range(2 * GROUP):
        here = slice(h * rows, (h + 1) * rows)
        side = h // GROUP
        scores = scores_all[here, :] * (SCALE * LOG2E) + bias[side * rows : (side + 1) * rows, :]
        expo = jnp.exp2(scores - jnp.max(scores, axis=-1, keepdims=True))
        probs = expo * (1.0 / jnp.sum(expo, axis=-1, keepdims=True))
        pbs[here, :] = probs.astype(BF16)
        dp = dp_all[here, :].astype(F32)
        ds = probs * (dp - jnp.sum(probs * dp, axis=-1, keepdims=True))
        hi = ds.astype(BF16)
        his[here, :] = hi
        los[here, :] = (ds - hi.astype(F32)).astype(BF16)
    att = contract(pbs[...], values, 1, 0).astype(BF16)
    gq = ((contract(his[...], keys, 1, 0) + contract(los[...], keys, 1, 0)) * SCALE).astype(BF16)
    for h, cols in enumerate(heads):
        here = slice(h * rows, (h + 1) * rows)
        there = slice((GROUP + h) * rows, (GROUP + h + 1) * rows)
        att_ref[:, cols] = att[here]
        gq_ref[:, cols] = gq[here]
        other_ref[0, :, cols] = att[there]
        other_ref[1, :, cols] = gq[there]
    dk = (contract(q, his[...], 0, 0) + contract(q, los[...], 0, 0)) * SCALE
    dv = contract(up, pbs[...], 0, 0)
    gkv_ref[:, :HEAD_DIM] = dk.T
    gkv_ref[:, HEAD_DIM:] = dv.T


def attend(me, spot, queries, upstream, pack, kv, ids, ids_row, before=()):
    rows, width = queries.shape
    length = kv.shape[0]
    by_head = pl.BlockSpec((rows, SPAN), lambda i, me: (0, me[0] ^ (2 * spot)))
    stacked = (2 * GROUP * rows, length)
    operands = (queries, upstream, pack, kv, ids, ids_row, *before)
    return call(
        functools.partial(attend_kernel, spot),
        1,
        (me,),
        operands,
        [
            by_head,
            by_head,
            pl.BlockSpec((1, 2, rows, SPAN), lambda i, me: (spot, 0, 0, 0)),
            constant_block((length, PAIR)),
            constant_block((length, 1)),
            constant_block((1, length)),
        ]
        + [ANYWHERE] * len(before),
        [by_head, by_head, constant_block((2, rows, SPAN)), constant_block((length, PAIR))],
        [
            shaped((rows, width), BF16),
            shaped((rows, width), BF16),
            shaped((2, rows, SPAN), BF16),
            shaped((length, PAIR), F32),
        ],
        16 * 2 * GROUP * rows * length * HEAD_DIM,
        scratch=[pltpu.VMEM((2 * rows, length), F32), pltpu.VMEM(stacked, F32)] + [pltpu.VMEM(stacked, BF16)] * 4,
        aliases={7 + i: i for i in range(len(before))},
    )


def by_expert(kind, x):
    return [jnp.where(kind == float(e), x, 0.0).astype(BF16) for e in range(2)]


def hidden_kernel(me_ref, kind_ref, g_ref, gc_ref, w_ref, wc_ref, mine_ref, away_ref, masked):
    rows = mine_ref.shape[0]

    @pl.when(pl.program_id(0) == 0)
    def _():
        for i in range(2):
            here = pl.ds(pl.multiple_of((me_ref[0] ^ (2 * i)) * rows, rows), rows)
            for k, ref in enumerate((g_ref, gc_ref)):
                for e, part in enumerate(by_expert(kind_ref[here, :], ref[here, :].astype(F32))):
                    masked[2 * k + e, i * rows : (i + 1) * rows, :] = part

    total = 0.0
    for k, ref in enumerate((w_ref, wc_ref)):
        for e in range(2):
            total = total + contract(ref[:, e].reshape(-1, PAIR), masked[2 * k + e], 1, 1)
    total = total.T
    mine_ref[...] = total[:rows]
    away_ref[...] = total[rows:].astype(BF16)


def hidden_grad(me, kind, grad, grad_c, weight, weight_c, rows):
    count, _, depth, _ = weight.shape
    length = grad.shape[0]
    group = count // 4
    by_tile = pl.BlockSpec((group, 2, depth, PAIR), lambda i, q: (i, 0, 0, 0))
    out = pl.BlockSpec((rows, group * depth), lambda i, q: (0, i))
    width = count * depth
    return call(
        hidden_kernel,
        4,
        (me,),
        (kind, grad, grad_c, weight, weight_c),
        [constant_block((length, 1)), constant_block((length, PAIR)), constant_block((length, PAIR)), by_tile, by_tile],
        [out, out],
        [shaped((rows, width), F32), shaped((rows, width), BF16)],
        16 * rows * width * PAIR,
        scratch=[pltpu.VMEM((4, 2 * rows, PAIR), BF16)],
    )


def weight_kernel(depth, count, halves, first, last, me_ref, *refs):
    parts, refs = refs[: 4 * count], refs[4 * count :]
    grads, refs = refs[: count + halves], refs[count + halves :]
    rows, lanes = parts[0].shape[1:]
    size = grads[0].shape[0]
    total = 0.0
    for b in range(count):
        left = jnp.concatenate([ref[0] for ref in parts[4 * b : 4 * b + 4]], axis=0)
        quarter = []
        for r in range(4):
            start = (me_ref[0] ^ r) * rows
            if halves:
                inner = pl.ds(pl.multiple_of(lax.rem(start, size), rows), rows)
                quarter.append(jnp.where(start < size, grads[0][inner, :].astype(F32), grads[1][inner, :].astype(F32)))
            else:
                quarter.append(grads[b][pl.ds(pl.multiple_of(start, rows), rows), :].astype(F32))
        kind = left[:, depth : depth + 1].astype(F32)
        right = jnp.concatenate(by_expert(kind, jnp.concatenate(quarter, axis=0)), axis=-1)
        total = total + contract(left, right, 0, 0)
    if not first:
        total = total + refs[0][...]
        refs = refs[1:]
    if not last:
        refs[0][...] = total
        return
    for e in range(2):
        refs[0][e] = total[:depth, e * PAIR : (e + 1) * PAIR]


def weight_grad(me, steps, parts, grads, total, depth, last, halves):
    rows, lanes = parts[0].shape[1:]
    count = 1 if halves else len(grads)
    part_specs = [
        pl.BlockSpec((1, rows, lanes), functools.partial(lambda by, i, me: (owner_at(me[1], by), 0, 0), by))
        for by in steps
        for _ in range(4)
    ]
    full = (lanes, 2 * PAIR)
    out = (2, depth, PAIR) if last else full
    before = [] if total is None else [total]
    operands = (*(list(parts) * count), *grads, *before)
    return call(
        functools.partial(weight_kernel, depth, count, int(halves), total is None, last),
        1,
        (me,),
        operands,
        part_specs + [constant_block(g.shape) for g in grads] + [constant_block(full)] * len(before),
        constant_block(out),
        shaped(out, F32),
        16 * rows * lanes * PAIR * count,
        aliases={len(operands): 0} if before and not last else None,
    )


def gather_kernel(me_ref, *refs):
    blocks, whole_ref, sems = refs[:-2], refs[-2], refs[-1]
    size = blocks[-1].shape[1]
    copies = []
    for i, block in enumerate(blocks):
        owner = owner_at(me_ref[1], STEPS[min(i, len(STEPS) - 1)])
        there = whole_ref.at[owner]
        if i >= len(STEPS) - 1:
            there = whole_ref.at[owner, :, pl.ds((i - len(STEPS) + 1) * size, size), :]
        copies.append(pltpu.make_async_copy(block, there, sems.at[i]))
    for copy in copies:
        copy.start()
    for copy in copies:
        copy.wait()


def gather_blocks(me, blocks):
    return call(
        gather_kernel,
        1,
        (me,),
        tuple(blocks),
        [ANYWHERE] * len(blocks),
        ANYWHERE,
        shaped((len(CYCLE), *blocks[0].shape), blocks[0].dtype),
        0,
        scratch=[pltpu.SemaphoreType.DMA((len(blocks),))],
    )


def in_order(parts, quarters):
    count, rows, lanes = parts[0].shape
    whole = jnp.stack(parts, axis=1)
    return jnp.take(whole, quarters, axis=1).reshape(count, 4 * rows, lanes)


def project_plain(quarters, parts, weights, depth):
    tokens = in_order(parts, quarters)
    kind, ids = read_marks(tokens[0], depth)
    sums = jnp.einsum("jmk,jekn->emn", tokens[:, :, :depth], weights, preferred_element_type=F32)
    return jnp.where(kind == 1.0, sums[1], sums[0]).astype(BF16), kind, ids, ids.reshape(1, -1)


def weight_plain(quarters, parts, grads, depth):
    tokens = in_order(parts, quarters)
    kind = tokens[:, :, depth : depth + 1].astype(F32)
    sums = [
        jnp.einsum("jmk,jmn->kn", tokens[:, :, :depth], g, preferred_element_type=F32)
        for g in by_expert(kind, grads.astype(F32))
    ]
    return jnp.stack(sums)


def per_device(fsdp, seq, tokens, queries, cotangent, modality, block_ids, kv_weight):
    tokens, queries, cotangent = tokens[0], queries[0], cotangent[0]
    me_f = lax.axis_index("fsdp")
    me_s = lax.axis_index("seq")
    rows, width = tokens.shape
    depth = kv_weight.shape[1]
    near_link = fsdp == len(CYCLE)

    def swap(x, bit):
        return lax.ppermute(x, "seq", [(i, i ^ bit) for i in range(seq)])

    def turn(x, by):
        return lax.ppermute(x, "fsdp", [(CYCLE[i], CYCLE[(i + by) % fsdp]) for i in range(fsdp)])

    def both_ways(ups, downs):
        return turn(ups, 1), turn(downs, -1)

    def halves(ups, downs, axis):
        size = ups.shape[axis] // 2
        return lax.slice_in_dim(ups, 0, size, axis=axis), lax.slice_in_dim(downs, size, 2 * size, axis=axis)

    def exchange_columns(x):
        return lax.all_to_all(x, "fsdp", split_axis=0, concat_axis=0, tiled=True)

    me = jnp.stack([me_s, me_f])
    quarters = me_s ^ jnp.arange(seq, dtype=jnp.int32)
    if near_link:
        weights = [kv_weight, *both_ways(kv_weight, kv_weight)]
    else:
        weight = lax.all_gather(kv_weight, "fsdp", axis=0)

    blocks = token_blocks(tokens, modality.reshape(rows, 1), block_ids.reshape(rows, 1), fsdp)
    across = swap(blocks, 2)
    parts = [blocks, swap(blocks, 1), across, swap(across, 1)]
    pack = swap(pack_heads(me, queries, cotangent), 1)
    columns = exchange_columns(blocks)
    columns_across = exchange_columns(across)

    if near_link:
        ups, downs = after(weights[1], parts[1], pack), after(weights[2], parts[1], pack)
        weights += both_ways(ups, downs)
        weights += both_ways(*weights[3:])
        ups, downs = halves(*weights[5:], 1)
        weights += both_ways(after(ups, parts[3], columns), after(downs, parts[3], columns))
        total = project(me, STEPS[:5], parts, weights[:5], None, depth, False, False)
        total = project(me, STEPS[5:7], parts, weights[5:7], total, depth, False, False)
        kv, kind, ids, ids_row = project(me, STEPS[7:], parts, weights[7:], total, depth, True, True)
        weight = gather_blocks(me, weights[:6] + [after(weights[6], kv)] + weights[7:])
    else:
        kv, kind, ids, ids_row = project_plain(quarters, parts, weight, depth)
    weight_c = swap(weight, 1)

    kv_far = swap(kv, 2)
    attended, grad_queries, other_near, near = attend(me, 0, queries, cotangent, pack, kv, ids, ids_row)
    attended, grad_queries, other_far, far = attend(
        me, 1, queries, cotangent, pack, kv_far, ids, ids_row, (attended, grad_queries)
    )
    grad_kv = (after(near, columns_across) + swap(far, 2)).astype(BF16)
    attended, grad_queries = place_heads(me, swap(other_near, 1), swap(other_far, 1), attended, grad_queries)

    mine, away = hidden_grad(me, kind, grad_kv, swap(grad_kv, 1), weight, weight_c, rows)
    columns = [columns, swap(columns, 1), columns_across, swap(columns_across, 1)]
    if near_link:
        first = after(grad_kv, away)
        grads = [first, *both_ways(first, first)]
        grads += both_ways(*grads[1:])
        grads += both_ways(*grads[3:])
        grads += both_ways(*halves(*grads[5:], 0))
        total = weight_grad(me, STEPS[:5], columns, grads[:5], None, depth, False, False)
        total = weight_grad(me, STEPS[5:7], columns, grads[5:7], total, depth, False, False)
        grad_weight = weight_grad(me, STEPS[7:], columns, grads[7:], total, depth, True, True)
    else:
        grad_weight = weight_plain(quarters, columns, lax.all_gather(grad_kv, "fsdp", axis=0), depth)
    grad_tokens = (mine + swap(away, 2).astype(F32)).astype(BF16)
    return attended[None], grad_queries[None], grad_tokens[None], grad_weight


def solution(mesh):
    split = P("fsdp", "seq", None)
    weights = P(None, "fsdp", "seq")
    return jax.shard_map(
        functools.partial(per_device, mesh.shape["fsdp"], mesh.shape["seq"]),
        mesh=mesh,
        in_specs=(split, split, split, P("fsdp", "seq"), P("fsdp", "seq"), weights),
        out_specs=(split, split, split, weights),
        check_vma=False,
    )
```

```python
import functools

import jax
import jax.numpy as jnp
from jax import lax
from jax.experimental import pallas as pl
from jax.experimental.pallas import tpu as pltpu
from jax.sharding import PartitionSpec as P

HEAD_DIM = 128
GROUP = 7
SPAN = GROUP * HEAD_DIM
PAIR = 2 * HEAD_DIM
SCALE = HEAD_DIM ** (-0.5)
LOG2E = 1.4426950408889634
HIDDEN = -1e30
DIGIT = 16
F32 = jnp.float32
BF16 = jnp.bfloat16
ANYWHERE = pl.BlockSpec(memory_space=pl.ANY)
CYCLE = (0, 2, 4, 6, 7, 5, 3, 1)
STEPS = (0, -1, 1, -2, 2, -3, 3, 4)


def contract(a, b, da, db):
    return lax.dot_general(a, b, (((da,), (db,)), ((), ())), preferred_element_type=F32)


def shaped(shape, dtype):
    return jax.ShapeDtypeStruct(shape, dtype)


def call(body, me, operands, out_shape, flops, scratch=(), aliases=None, anywhere=0):
    moved = sum(x.size * x.dtype.itemsize for x in operands)
    near = pl.BlockSpec(memory_space=pltpu.VMEM)
    return pl.pallas_call(
        body,
        in_specs=[pl.BlockSpec(memory_space=pltpu.SMEM)]
        + [near] * (len(operands) - anywhere)
        + [ANYWHERE] * anywhere,
        out_specs=[near] * len(out_shape) if isinstance(out_shape, list) else near,
        out_shape=out_shape,
        scratch_shapes=scratch,
        input_output_aliases=aliases or {},
        compiler_params=pltpu.CompilerParams(vmem_limit_bytes=24 * 1024 * 1024),
        cost_estimate=pl.CostEstimate(flops=flops, bytes_accessed=moved, transcendentals=0),
    )(me, *operands)


def owner_at(me_f, by):
    size = len(CYCLE)
    half = size // 2
    line, side = lax.div(me_f, 2), lax.rem(me_f, 2)
    spot = jnp.where(side == 1, size - 1 - line, line)
    spot = lax.rem(spot + (size + by), size)
    return jnp.where(spot < half, 2 * spot, 2 * (size - 1 - spot) + 1)


def after(x, *others):
    return pl.pallas_call(
        lambda *refs: None,
        in_specs=[ANYWHERE] * (1 + len(others)),
        out_specs=ANYWHERE,
        out_shape=shaped(x.shape, x.dtype),
        input_output_aliases={0: 0},
        cost_estimate=pl.CostEstimate(flops=0, bytes_accessed=0, transcendentals=0),
    )(x, *others)


def as_column(row):
    return jnp.broadcast_to(row, (128, row.shape[1])).T[:, :1]


def blocks_kernel(depth, me_ref, tok_ref, kind_ref, ids_ref, out_ref):
    count, rows, lanes = out_ref.shape
    base = lanes - 128
    lane = lax.broadcasted_iota(jnp.int32, (rows, 128), 1) - (depth - base)
    ids = ids_ref[...]
    marks = [as_column(x.astype(F32)) for x in (kind_ref[...], lax.div(ids, DIGIT), lax.rem(ids, DIGIT))]
    for j in range(count):
        out_ref[j, :, :depth] = tok_ref[:, j * depth : (j + 1) * depth]
        last = out_ref[j, :, base:].astype(F32)
        last = jnp.where(lane >= 0, 0.0, last)
        for i, mark in enumerate(marks):
            last = jnp.where(lane == i, mark, last)
        out_ref[j, :, base:] = last.astype(BF16)


def token_blocks(me, tokens, kinds, ids, count):
    rows, width = tokens.shape
    depth = width // count
    lanes = -(-(depth + 3) // 128) * 128
    out = shaped((count, rows, lanes), BF16)
    return call(functools.partial(blocks_kernel, depth), me, (tokens, kinds, ids), out, 0)


def read_marks(block, depth):
    mark = [block[:, depth + i : depth + i + 1].astype(F32) for i in range(3)]
    return mark[0], mark[1] * DIGIT + mark[2]


def pack_kernel(me_ref, q_ref, up_ref, own_ref, other_ref):
    for i in range(4):
        here = pl.ds(pl.multiple_of((me_ref[0] ^ i) * SPAN, SPAN), SPAN)
        out_ref = other_ref if i % 2 else own_ref
        out_ref[i // 2, 0] = q_ref[:, here]
        out_ref[i // 2, 1] = up_ref[:, here]


def pack_heads(me, queries, upstream):
    out = shaped((2, 2, queries.shape[0], SPAN), BF16)
    return call(pack_kernel, me, (queries, upstream), [out, out], 0)


def place_kernel(me_ref, *refs):
    att_ref, gq_ref = refs[4:]
    for i, ref in enumerate(refs[:4]):
        here = pl.ds(pl.multiple_of((me_ref[0] ^ i) * SPAN, SPAN), SPAN)
        att_ref[:, here] = ref[0]
        gq_ref[:, here] = ref[1]


def place_heads(me, found):
    out = shaped((found[0].shape[1], 4 * SPAN), BF16)
    return call(place_kernel, me, found, [out, out], 0)


def project_kernel(steps, depth, halves, first, last, me_ref, *refs):
    parts, refs = refs[:4], refs[4:]
    weights, refs = refs[: len(steps) + halves], refs[len(steps) + halves :]
    rows, lanes = parts[0].shape[1:]
    sums = [0.0, 0.0]
    for b, by in enumerate(steps):
        owner = owner_at(me_ref[1], by)
        left = jnp.concatenate([ref[owner][:, :depth] for ref in parts], axis=0)
        for e in range(2):
            right = jnp.concatenate([ref[e] for ref in weights], axis=0) if halves else weights[b][e]
            sums[e] = sums[e] + contract(left, right, 1, 0)
    if not first:
        sums = [s + refs[0][:, e * PAIR : (e + 1) * PAIR] for e, s in enumerate(sums)]
        refs = refs[1:]
    if not last:
        for e in range(2):
            refs[-1][:, e * PAIR : (e + 1) * PAIR] = sums[e]
        return
    kv_ref, kind_ref, ids_ref, ids_row_ref = refs[-4:]
    for r in range(4):
        here = pl.ds(pl.multiple_of((me_ref[0] ^ r) * rows, rows), rows)
        kind, ids = read_marks(parts[r][0], depth)
        mine = slice(r * rows, (r + 1) * rows)
        kv_ref[here, :] = jnp.where(kind == 1.0, sums[1][mine], sums[0][mine]).astype(BF16)
        kind_ref[here, :] = kind
        ids_ref[here, :] = ids
    ids_row_ref[...] = jnp.broadcast_to(ids_ref[...], (4 * rows, 128)).T[:1]


def project(me, steps, parts, weights, total, depth, last=False, halves=False, wait=()):
    rows, lanes = parts[0].shape[1:]
    length = 4 * rows
    before = () if total is None else (total,)
    out = shaped((length, 2 * PAIR), F32)
    if last:
        out = [shaped((length, PAIR), BF16)] + [shaped(x, F32) for x in ((length, 1), (length, 1), (1, length))]
    operands = (*parts, *weights, *before, *wait)
    return call(
        functools.partial(project_kernel, steps, depth, int(halves), total is None, last),
        me,
        operands,
        out,
        4 * length * depth * PAIR * len(steps),
        anywhere=len(wait),
    )


def attend_kernel(me_ref, own_ref, pack_ref, kv_ref, ids_ref, ids_row_ref, *refs):
    mine_ref, other_ref, gkv_ref, bias, scores_all, dp_all, pbs, his, los = refs[-9:]
    rows = own_ref.shape[2]
    heads = [slice(h * HEAD_DIM, (h + 1) * HEAD_DIM) for h in range(GROUP)]
    for i in range(2):
        here = pl.ds(pl.multiple_of((me_ref[0] ^ i) * rows, rows), rows)
        bias[i * rows : (i + 1) * rows, :] = jnp.where(ids_row_ref[...] <= ids_ref[here, :], 0.0, HIDDEN)
    keys = kv_ref[:, :HEAD_DIM]
    values = kv_ref[:, HEAD_DIM:]
    spot = me_ref[2]
    q, up = [
        jnp.concatenate([ref[spot, i, :, cols] for ref in (own_ref, pack_ref) for cols in heads], axis=0)
        for i in range(2)
    ]
    scores_all[...] = contract(q, keys, 1, 1)
    dp_all[...] = contract(up, values, 1, 1).astype(BF16)
    for h in range(2 * GROUP):
        here = slice(h * rows, (h + 1) * rows)
        side = h // GROUP
        scores = scores_all[here, :] * (SCALE * LOG2E) + bias[side * rows : (side + 1) * rows, :]
        expo = jnp.exp2(scores - jnp.max(scores, axis=-1, keepdims=True))
        probs = expo * (1.0 / jnp.sum(expo, axis=-1, keepdims=True))
        pbs[here, :] = probs.astype(BF16)
        dp = dp_all[here, :].astype(F32)
        ds = probs * (dp - jnp.sum(probs * dp, axis=-1, keepdims=True))
        hi = ds.astype(BF16)
        his[here, :] = hi
        los[here, :] = (ds - hi.astype(F32)).astype(BF16)
    att = contract(pbs[...], values, 1, 0).astype(BF16)
    gq = ((contract(his[...], keys, 1, 0) + contract(los[...], keys, 1, 0)) * SCALE).astype(BF16)
    for i, ref in enumerate((mine_ref, other_ref)):
        for h, cols in enumerate(heads):
            here = slice((i * GROUP + h) * rows, (i * GROUP + h + 1) * rows)
            ref[0, :, cols] = att[here]
            ref[1, :, cols] = gq[here]
    dk = (contract(q, his[...], 0, 0) + contract(q, los[...], 0, 0)) * SCALE
    dv = contract(up, pbs[...], 0, 0)
    gkv_ref[:, :HEAD_DIM] = dk.T
    gkv_ref[:, HEAD_DIM:] = dv.T


def attend(me, own, pack, kv, ids, ids_row, wait=()):
    rows = own.shape[2]
    length = kv.shape[0]
    stacked = (2 * GROUP * rows, length)
    side = shaped((2, rows, SPAN), BF16)
    return call(
        attend_kernel,
        me,
        (own, pack, kv, ids, ids_row, *wait),
        [side, side, shaped((length, PAIR), F32)],
        16 * 2 * GROUP * rows * length * HEAD_DIM,
        scratch=[pltpu.VMEM((2 * rows, length), F32), pltpu.VMEM(stacked, F32)] + [pltpu.VMEM(stacked, BF16)] * 4,
        anywhere=len(wait),
    )


def by_expert(kind, x):
    return [jnp.where(kind == float(e), x, 0.0).astype(BF16) for e in range(2)]


def hidden_kernel(me_ref, kind_ref, g_ref, gc_ref, w_ref, wc_ref, mine_ref, away_ref):
    rows = mine_ref.shape[0]
    count, _, depth, _ = w_ref.shape
    masked = []
    for ref in (g_ref, gc_ref):
        sides = []
        for i in range(2):
            here = pl.ds(pl.multiple_of((me_ref[0] ^ (2 * i)) * rows, rows), rows)
            sides.append(by_expert(kind_ref[here, :], ref[here, :].astype(F32)))
        masked += [jnp.concatenate([sides[0][e], sides[1][e]], axis=0) for e in range(2)]
    group = count // 4
    for j in range(4):
        total = 0.0
        for k, ref in enumerate((w_ref, wc_ref)):
            for e in range(2):
                w = ref[j * group : (j + 1) * group, e].reshape(group * depth, PAIR)
                total = total + contract(w, masked[2 * k + e], 1, 1)
        total = total.T
        cols = slice(j * group * depth, (j + 1) * group * depth)
        mine_ref[:, cols] = total[:rows]
        away_ref[:, cols] = total[rows:].astype(BF16)


def hidden_grad(me, kind, grad, grad_c, weight, weight_c, rows):
    count, _, depth, _ = weight.shape
    width = count * depth
    return call(
        hidden_kernel,
        me,
        (kind, grad, grad_c, weight, weight_c),
        [shaped((rows, width), F32), shaped((rows, width), BF16)],
        16 * rows * width * PAIR,
    )


def weight_kernel(steps, depth, halves, first, last, me_ref, *refs):
    parts, refs = refs[:4], refs[4:]
    grads, refs = refs[: len(steps) + halves], refs[len(steps) + halves :]
    rows, lanes = parts[0].shape[1:]
    size = grads[0].shape[0]
    total = 0.0
    for b, by in enumerate(steps):
        owner = owner_at(me_ref[1], by)
        left = jnp.concatenate([ref[owner] for ref in parts], axis=0)
        quarter = []
        for r in range(4):
            start = (me_ref[0] ^ r) * rows
            if halves:
                inner = pl.ds(pl.multiple_of(lax.rem(start, size), rows), rows)
                quarter.append(jnp.where(start < size, grads[0][inner, :].astype(F32), grads[1][inner, :].astype(F32)))
            else:
                quarter.append(grads[b][pl.ds(pl.multiple_of(start, rows), rows), :].astype(F32))
        kind = left[:, depth : depth + 1].astype(F32)
        right = jnp.concatenate(by_expert(kind, jnp.concatenate(quarter, axis=0)), axis=-1)
        total = total + contract(left, right, 0, 0)
    if not first:
        total = total + refs[0][...]
    if not last:
        refs[-1][...] = total
        return
    for e in range(2):
        refs[-1][e] = total[:depth, e * PAIR : (e + 1) * PAIR]


def weight_grad(me, steps, parts, grads, total, depth, last=False, halves=False):
    rows, lanes = parts[0].shape[1:]
    before = () if total is None else (total,)
    return call(
        functools.partial(weight_kernel, steps, depth, int(halves), total is None, last),
        me,
        (*parts, *grads, *before),
        shaped((2, depth, PAIR) if last else (lanes, 2 * PAIR), F32),
        16 * rows * lanes * PAIR * len(steps),
    )


def gather_kernel(me_ref, *refs):
    blocks, whole_ref = refs[: len(STEPS) + 1], refs[-1]
    size = blocks[-1].shape[1]
    for i, block in enumerate(blocks):
        owner = owner_at(me_ref[1], STEPS[min(i, len(STEPS) - 1)])
        if i < len(STEPS) - 1:
            whole_ref[owner] = block[...]
        else:
            whole_ref[owner, :, (i - len(STEPS) + 1) * size : (i - len(STEPS) + 2) * size, :] = block[...]


def gather_blocks(me, blocks, wait=()):
    out = shaped((len(CYCLE), *blocks[0].shape), blocks[0].dtype)
    return call(gather_kernel, me, (*blocks, *wait), out, 0, anywhere=len(wait))


def in_order(parts, quarters):
    count, rows, lanes = parts[0].shape
    whole = jnp.stack(parts, axis=1)
    return jnp.take(whole, quarters, axis=1).reshape(count, 4 * rows, lanes)


def project_plain(quarters, parts, weights, depth):
    tokens = in_order(parts, quarters)
    kind, ids = read_marks(tokens[0], depth)
    sums = jnp.einsum("jmk,jekn->emn", tokens[:, :, :depth], weights, preferred_element_type=F32)
    return jnp.where(kind == 1.0, sums[1], sums[0]).astype(BF16), kind, ids, ids.reshape(1, -1)


def weight_plain(quarters, parts, grads, depth):
    tokens = in_order(parts, quarters)
    kind = tokens[:, :, depth : depth + 1].astype(F32)
    sums = [
        jnp.einsum("jmk,jmn->kn", tokens[:, :, :depth], g, preferred_element_type=F32)
        for g in by_expert(kind, grads.astype(F32))
    ]
    return jnp.stack(sums)


def per_device(fsdp, seq, tokens, queries, cotangent, modality, block_ids, kv_weight):
    tokens, queries, cotangent = tokens[0], queries[0], cotangent[0]
    me_f = lax.axis_index("fsdp")
    me_s = lax.axis_index("seq")
    rows, width = tokens.shape
    depth = kv_weight.shape[1]
    near_link = fsdp == len(CYCLE)

    def swap(x, bit):
        return lax.ppermute(x, "seq", [(i, i ^ bit) for i in range(seq)])

    def turn(x, by):
        return lax.ppermute(x, "fsdp", [(CYCLE[i], CYCLE[(i + by) % fsdp]) for i in range(fsdp)])

    def both_ways(ups, downs):
        return turn(ups, 1), turn(downs, -1)

    def halves(ups, downs, axis):
        size = ups.shape[axis] // 2
        return lax.slice_in_dim(ups, 0, size, axis=axis), lax.slice_in_dim(downs, size, 2 * size, axis=axis)

    def exchange_columns(x):
        return lax.all_to_all(x, "fsdp", split_axis=0, concat_axis=0, tiled=True)

    me = jnp.stack([me_s, me_f, jnp.int32(0)])
    me_far = jnp.stack([me_s, me_f, jnp.int32(1)])
    quarters = me_s ^ jnp.arange(seq, dtype=jnp.int32)
    if near_link:
        weights = [kv_weight, *both_ways(kv_weight, kv_weight)]
        weights += both_ways(*weights[1:])
        weights += both_ways(*weights[3:])
    else:
        weight = lax.all_gather(kv_weight, "fsdp", axis=0)

    blocks = token_blocks(me, tokens, modality, block_ids, fsdp)
    across = swap(blocks, 2)
    parts = [blocks, swap(blocks, 1), across, swap(across, 1)]
    own, pack = pack_heads(me, queries, cotangent)
    pack = swap(pack, 1)
    columns = exchange_columns(blocks)
    columns_across = exchange_columns(across)

    if near_link:
        ups, downs = halves(*weights[5:], 1)
        weights += both_ways(after(ups, parts[1], pack), after(downs, parts[1], pack))
        total = project(me, STEPS[:5], parts, weights[:5], None, depth)
        total = project(me, STEPS[5:7], parts, weights[5:7], total, depth)
        kv, kind, ids, ids_row = project(me, STEPS[7:], parts, weights[7:], total, depth, True, True, (columns,))
        weight = gather_blocks(me, weights, (kv,))
    else:
        kv, kind, ids, ids_row = project_plain(quarters, parts, weight, depth)
    weight_c = swap(weight, 1)

    kv_far = swap(kv, 2)
    near_own, near_other, near = attend(me, own, pack, kv, ids, ids_row)
    far_own, far_other, far = attend(me_far, own, pack, kv_far, ids, ids_row, (near,))
    grad_kv = (after(near, columns_across) + swap(far, 2)).astype(BF16)
    attended, grad_queries = place_heads(me, (near_own, swap(near_other, 1), far_own, swap(far_other, 1)))

    mine, away = hidden_grad(me, kind, grad_kv, swap(grad_kv, 1), weight, weight_c, rows)
    columns = [columns, swap(columns, 1), columns_across, swap(columns_across, 1)]
    if near_link:
        first = after(grad_kv, away)
        grads = [first, *both_ways(first, first)]
        grads += both_ways(*grads[1:])
        grads += both_ways(*grads[3:])
        grads += both_ways(*halves(*grads[5:], 0))
        total = weight_grad(me, STEPS[:5], columns, grads[:5], None, depth)
        total = weight_grad(me, STEPS[5:7], columns, grads[5:7], total, depth)
        grad_weight = weight_grad(me, STEPS[7:], columns, grads[7:], total, depth, True, True)
    else:
        grad_weight = weight_plain(quarters, columns, lax.all_gather(grad_kv, "fsdp", axis=0), depth)
    grad_tokens = (mine + swap(away, 2).astype(F32)).astype(BF16)
    return attended[None], grad_queries[None], grad_tokens[None], grad_weight


def solution(mesh):
    split = P("fsdp", "seq", None)
    weights = P(None, "fsdp", "seq")
    return jax.shard_map(
        functools.partial(per_device, mesh.shape["fsdp"], mesh.shape["seq"]),
        mesh=mesh,
        in_specs=(split, split, split, P("fsdp", "seq"), P("fsdp", "seq"), weights),
        out_specs=(split, split, split, weights),
        check_vma=False,
    )
```

```python
import functools

import jax
import jax.numpy as jnp
from jax import lax
from jax.experimental import pallas as pl
from jax.experimental.pallas import tpu as pltpu
from jax.sharding import PartitionSpec as P

HEAD_DIM = 128
GROUP = 7
SPAN = GROUP * HEAD_DIM
PAIR = 2 * HEAD_DIM
SCALE = HEAD_DIM ** (-0.5)
LOG2E = 1.4426950408889634
HIDDEN = -1e30
DIGIT = 16
F32 = jnp.float32
BF16 = jnp.bfloat16
ANYWHERE = pl.BlockSpec(memory_space=pl.ANY)
CYCLE = (0, 2, 4, 6, 7, 5, 3, 1)
STEPS = (0, -1, 1, -2, 2, -3, 3, 4)


def contract(a, b, da, db):
    return lax.dot_general(a, b, (((da,), (db,)), ((), ())), preferred_element_type=F32)


def shaped(shape, dtype):
    return jax.ShapeDtypeStruct(shape, dtype)


def call(body, me, operands, out_shape, scratch=(), anywhere=0):
    near = pl.BlockSpec(memory_space=pltpu.VMEM)
    return pl.pallas_call(
        body,
        in_specs=[pl.BlockSpec(memory_space=pltpu.SMEM)]
        + [near] * (len(operands) - anywhere)
        + [ANYWHERE] * anywhere,
        out_specs=[near] * len(out_shape) if isinstance(out_shape, list) else near,
        out_shape=out_shape,
        scratch_shapes=scratch,
        compiler_params=pltpu.CompilerParams(vmem_limit_bytes=24 * 1024 * 1024),
        cost_estimate=pl.CostEstimate(flops=0, bytes_accessed=0, transcendentals=0),
    )(me, *operands)


def owner_at(me_f, by):
    size = len(CYCLE)
    half = size // 2
    line, side = lax.div(me_f, 2), lax.rem(me_f, 2)
    spot = jnp.where(side == 1, size - 1 - line, line)
    spot = lax.rem(spot + (size + by), size)
    return jnp.where(spot < half, 2 * spot, 2 * (size - 1 - spot) + 1)


def after(x, *others):
    return pl.pallas_call(
        lambda *refs: None,
        in_specs=[ANYWHERE] * (1 + len(others)),
        out_specs=ANYWHERE,
        out_shape=shaped(x.shape, x.dtype),
        input_output_aliases={0: 0},
        cost_estimate=pl.CostEstimate(flops=0, bytes_accessed=0, transcendentals=0),
    )(x, *others)


def as_column(row):
    return jnp.broadcast_to(row, (128, row.shape[1])).T[:, :1]


def blocks_kernel(depth, me_ref, tok_ref, kind_ref, ids_ref, out_ref):
    count, rows, lanes = out_ref.shape
    base = lanes - 128
    lane = lax.broadcasted_iota(jnp.int32, (rows, 128), 1) - (depth - base)
    ids = ids_ref[...]
    marks = [as_column(x.astype(F32)) for x in (kind_ref[...], lax.div(ids, DIGIT), lax.rem(ids, DIGIT))]
    for j in range(count):
        out_ref[j, :, :depth] = tok_ref[:, j * depth : (j + 1) * depth]
        last = out_ref[j, :, base:].astype(F32)
        last = jnp.where(lane >= 0, 0.0, last)
        for i, mark in enumerate(marks):
            last = jnp.where(lane == i, mark, last)
        out_ref[j, :, base:] = last.astype(BF16)


def token_blocks(me, tokens, kinds, ids, count):
    rows, width = tokens.shape
    depth = width // count
    lanes = -(-(depth + 3) // 128) * 128
    out = shaped((count, rows, lanes), BF16)
    return call(functools.partial(blocks_kernel, depth), me, (tokens, kinds, ids), out)


def read_marks(block, depth):
    mark = [block[:, depth + i : depth + i + 1].astype(F32) for i in range(3)]
    return mark[0], mark[1] * DIGIT + mark[2]


def pack_kernel(me_ref, q_ref, up_ref, own_ref, other_ref):
    for i in range(4):
        here = pl.ds(pl.multiple_of((me_ref[0] ^ i) * SPAN, SPAN), SPAN)
        out_ref = other_ref if i % 2 else own_ref
        out_ref[i // 2, 0] = q_ref[:, here]
        out_ref[i // 2, 1] = up_ref[:, here]


def pack_heads(me, queries, upstream):
    out = shaped((2, 2, queries.shape[0], SPAN), BF16)
    return call(pack_kernel, me, (queries, upstream), [out, out])


def place_kernel(me_ref, *refs):
    att_ref, gq_ref = refs[4:]
    for i, ref in enumerate(refs[:4]):
        here = pl.ds(pl.multiple_of((me_ref[0] ^ i) * SPAN, SPAN), SPAN)
        att_ref[:, here] = ref[0]
        gq_ref[:, here] = ref[1]


def place_heads(me, found):
    out = shaped((found[0].shape[1], 4 * SPAN), BF16)
    return call(place_kernel, me, found, [out, out])


def project_kernel(steps, depth, halves, first, last, me_ref, *refs):
    parts, refs = refs[:4], refs[4:]
    weights, refs = refs[: len(steps) + halves], refs[len(steps) + halves :]
    rows, lanes = parts[0].shape[1:]
    sums = [0.0, 0.0]
    for b, by in enumerate(steps):
        owner = owner_at(me_ref[1], by)
        left = jnp.concatenate([ref[owner][:, :depth] for ref in parts], axis=0)
        for e in range(2):
            right = jnp.concatenate([ref[e] for ref in weights], axis=0) if halves else weights[b][e]
            sums[e] = sums[e] + contract(left, right, 1, 0)
    if not first:
        sums = [s + refs[0][:, e * PAIR : (e + 1) * PAIR] for e, s in enumerate(sums)]
        refs = refs[1:]
    if not last:
        for e in range(2):
            refs[-1][:, e * PAIR : (e + 1) * PAIR] = sums[e]
        return
    kv_ref, kind_ref, ids_ref, ids_row_ref = refs[-4:]
    for r in range(4):
        here = pl.ds(pl.multiple_of((me_ref[0] ^ r) * rows, rows), rows)
        kind, ids = read_marks(parts[r][0], depth)
        mine = slice(r * rows, (r + 1) * rows)
        kv_ref[here, :] = jnp.where(kind == 1.0, sums[1][mine], sums[0][mine]).astype(BF16)
        kind_ref[here, :] = kind
        ids_ref[here, :] = ids
    ids_row_ref[...] = jnp.broadcast_to(ids_ref[...], (4 * rows, 128)).T[:1]


def project(me, steps, parts, weights, total, depth, last=False, halves=False, wait=()):
    rows, lanes = parts[0].shape[1:]
    length = 4 * rows
    before = () if total is None else (total,)
    out = shaped((length, 2 * PAIR), F32)
    if last:
        out = [shaped((length, PAIR), BF16)] + [shaped(x, F32) for x in ((length, 1), (length, 1), (1, length))]
    operands = (*parts, *weights, *before, *wait)
    return call(
        functools.partial(project_kernel, steps, depth, int(halves), total is None, last),
        me,
        operands,
        out,
        anywhere=len(wait),
    )


def attend_kernel(me_ref, own_ref, pack_ref, kv_ref, ids_ref, ids_row_ref, *refs):
    mine_ref, other_ref, gkv_ref, bias, scores_all, dp_all, pbs, his, los = refs[-9:]
    rows = own_ref.shape[2]
    heads = [slice(h * HEAD_DIM, (h + 1) * HEAD_DIM) for h in range(GROUP)]
    for i in range(2):
        here = pl.ds(pl.multiple_of((me_ref[0] ^ i) * rows, rows), rows)
        bias[i * rows : (i + 1) * rows, :] = jnp.where(ids_row_ref[...] <= ids_ref[here, :], 0.0, HIDDEN)
    keys = kv_ref[:, :HEAD_DIM]
    values = kv_ref[:, HEAD_DIM:]
    spot = me_ref[2]
    q, up = [
        jnp.concatenate([ref[spot, i, :, cols] for ref in (own_ref, pack_ref) for cols in heads], axis=0)
        for i in range(2)
    ]
    scores_all[...] = contract(q, keys, 1, 1)
    dp_all[...] = contract(up, values, 1, 1).astype(BF16)
    for h in range(2 * GROUP):
        here = slice(h * rows, (h + 1) * rows)
        side = h // GROUP
        scores = scores_all[here, :] * (SCALE * LOG2E) + bias[side * rows : (side + 1) * rows, :]
        expo = jnp.exp2(scores - jnp.max(scores, axis=-1, keepdims=True))
        probs = expo * (1.0 / jnp.sum(expo, axis=-1, keepdims=True))
        pbs[here, :] = probs.astype(BF16)
        dp = dp_all[here, :].astype(F32)
        ds = probs * (dp - jnp.sum(probs * dp, axis=-1, keepdims=True))
        hi = ds.astype(BF16)
        his[here, :] = hi
        los[here, :] = (ds - hi.astype(F32)).astype(BF16)
    att = contract(pbs[...], values, 1, 0).astype(BF16)
    gq = ((contract(his[...], keys, 1, 0) + contract(los[...], keys, 1, 0)) * SCALE).astype(BF16)
    for i, ref in enumerate((mine_ref, other_ref)):
        for h, cols in enumerate(heads):
            here = slice((i * GROUP + h) * rows, (i * GROUP + h + 1) * rows)
            ref[0, :, cols] = att[here]
            ref[1, :, cols] = gq[here]
    dk = (contract(q, his[...], 0, 0) + contract(q, los[...], 0, 0)) * SCALE
    dv = contract(up, pbs[...], 0, 0)
    gkv_ref[:, :HEAD_DIM] = dk.T
    gkv_ref[:, HEAD_DIM:] = dv.T


def attend(me, own, pack, kv, ids, ids_row, wait=()):
    rows = own.shape[2]
    length = kv.shape[0]
    stacked = (2 * GROUP * rows, length)
    side = shaped((2, rows, SPAN), BF16)
    return call(
        attend_kernel,
        me,
        (own, pack, kv, ids, ids_row, *wait),
        [side, side, shaped((length, PAIR), F32)],
        scratch=[pltpu.VMEM((2 * rows, length), F32), pltpu.VMEM(stacked, F32)] + [pltpu.VMEM(stacked, BF16)] * 4,
        anywhere=len(wait),
    )


def by_expert(kind, x):
    return [jnp.where(kind == float(e), x, 0.0).astype(BF16) for e in range(2)]


def hidden_kernel(me_ref, kind_ref, g_ref, gc_ref, w_ref, wc_ref, mine_ref, away_ref):
    rows = mine_ref.shape[0]
    count, _, depth, _ = w_ref.shape
    masked = []
    for ref in (g_ref, gc_ref):
        sides = []
        for i in range(2):
            here = pl.ds(pl.multiple_of((me_ref[0] ^ (2 * i)) * rows, rows), rows)
            sides.append(by_expert(kind_ref[here, :], ref[here, :].astype(F32)))
        masked += [jnp.concatenate([sides[0][e], sides[1][e]], axis=0) for e in range(2)]
    group = count // 4
    for j in range(4):
        total = 0.0
        for k, ref in enumerate((w_ref, wc_ref)):
            for e in range(2):
                w = ref[j * group : (j + 1) * group, e].reshape(group * depth, PAIR)
                total = total + contract(w, masked[2 * k + e], 1, 1)
        total = total.T
        cols = slice(j * group * depth, (j + 1) * group * depth)
        mine_ref[:, cols] = total[:rows]
        away_ref[:, cols] = total[rows:].astype(BF16)


def hidden_grad(me, kind, grad, grad_c, weight, weight_c, rows):
    count, _, depth, _ = weight.shape
    width = count * depth
    return call(
        hidden_kernel,
        me,
        (kind, grad, grad_c, weight, weight_c),
        [shaped((rows, width), F32), shaped((rows, width), BF16)],
    )


def weight_kernel(steps, depth, halves, first, last, me_ref, *refs):
    parts, refs = refs[:4], refs[4:]
    grads, refs = refs[: len(steps) + halves], refs[len(steps) + halves :]
    rows, lanes = parts[0].shape[1:]
    size = grads[0].shape[0]
    total = 0.0
    for b, by in enumerate(steps):
        owner = owner_at(me_ref[1], by)
        left = jnp.concatenate([ref[owner] for ref in parts], axis=0)
        quarter = []
        for r in range(4):
            start = (me_ref[0] ^ r) * rows
            if halves:
                inner = pl.ds(pl.multiple_of(lax.rem(start, size), rows), rows)
                quarter.append(jnp.where(start < size, grads[0][inner, :].astype(F32), grads[1][inner, :].astype(F32)))
            else:
                quarter.append(grads[b][pl.ds(pl.multiple_of(start, rows), rows), :].astype(F32))
        kind = left[:, depth : depth + 1].astype(F32)
        right = jnp.concatenate(by_expert(kind, jnp.concatenate(quarter, axis=0)), axis=-1)
        total = total + contract(left, right, 0, 0)
    if not first:
        total = total + refs[0][...]
    if not last:
        refs[-1][...] = total
        return
    for e in range(2):
        refs[-1][e] = total[:depth, e * PAIR : (e + 1) * PAIR]


def weight_grad(me, steps, parts, grads, total, depth, last=False, halves=False):
    rows, lanes = parts[0].shape[1:]
    before = () if total is None else (total,)
    return call(
        functools.partial(weight_kernel, steps, depth, int(halves), total is None, last),
        me,
        (*parts, *grads, *before),
        shaped((2, depth, PAIR) if last else (lanes, 2 * PAIR), F32),
    )


def gather_kernel(me_ref, *refs):
    blocks, whole_ref = refs[: len(STEPS) + 1], refs[-1]
    size = blocks[-1].shape[1]
    for i, block in enumerate(blocks):
        owner = owner_at(me_ref[1], STEPS[min(i, len(STEPS) - 1)])
        if i < len(STEPS) - 1:
            whole_ref[owner] = block[...]
        else:
            whole_ref[owner, :, (i - len(STEPS) + 1) * size : (i - len(STEPS) + 2) * size, :] = block[...]


def gather_blocks(me, blocks, wait=()):
    out = shaped((len(CYCLE), *blocks[0].shape), blocks[0].dtype)
    return call(gather_kernel, me, (*blocks, *wait), out, anywhere=len(wait))


def in_order(parts, quarters):
    count, rows, lanes = parts[0].shape
    whole = jnp.stack(parts, axis=1)
    return jnp.take(whole, quarters, axis=1).reshape(count, 4 * rows, lanes)


def project_plain(quarters, parts, weights, depth):
    tokens = in_order(parts, quarters)
    kind, ids = read_marks(tokens[0], depth)
    sums = jnp.einsum("jmk,jekn->emn", tokens[:, :, :depth], weights, preferred_element_type=F32)
    return jnp.where(kind == 1.0, sums[1], sums[0]).astype(BF16), kind, ids, ids.reshape(1, -1)


def weight_plain(quarters, parts, grads, depth):
    tokens = in_order(parts, quarters)
    kind = tokens[:, :, depth : depth + 1].astype(F32)
    sums = [
        jnp.einsum("jmk,jmn->kn", tokens[:, :, :depth], g, preferred_element_type=F32)
        for g in by_expert(kind, grads.astype(F32))
    ]
    return jnp.stack(sums)


def per_device(fsdp, seq, tokens, queries, cotangent, modality, block_ids, kv_weight):
    tokens, queries, cotangent = tokens[0], queries[0], cotangent[0]
    me_f = lax.axis_index("fsdp")
    me_s = lax.axis_index("seq")
    rows, width = tokens.shape
    depth = kv_weight.shape[1]
    near_link = fsdp == len(CYCLE)

    def swap(x, bit):
        return lax.ppermute(x, "seq", [(i, i ^ bit) for i in range(seq)])

    def over_seq(x):
        across = swap(x, 2)
        return [x, swap(x, 1), across, swap(across, 1)]

    def turn(x, by):
        return lax.ppermute(x, "fsdp", [(CYCLE[i], CYCLE[(i + by) % fsdp]) for i in range(fsdp)])

    def both_ways(ups, downs):
        return turn(ups, 1), turn(downs, -1)

    def halves(ups, downs, axis):
        size = ups.shape[axis] // 2
        return lax.slice_in_dim(ups, 0, size, axis=axis), lax.slice_in_dim(downs, size, 2 * size, axis=axis)

    def exchange_columns(x):
        return lax.all_to_all(x, "fsdp", split_axis=0, concat_axis=0, tiled=True)

    me = jnp.stack([me_s, me_f, jnp.int32(0)])
    me_far = jnp.stack([me_s, me_f, jnp.int32(1)])
    quarters = me_s ^ jnp.arange(seq, dtype=jnp.int32)
    if near_link:
        weights = [kv_weight, *both_ways(kv_weight, kv_weight)]
        weights += both_ways(*weights[1:])
        weights += both_ways(*weights[3:])
    else:
        weight = lax.all_gather(kv_weight, "fsdp", axis=0)

    blocks = token_blocks(me, tokens, modality, block_ids, fsdp)
    across = swap(blocks, 2)
    held = (weights[3], weights[4]) if near_link else ()
    parts = [blocks, swap(blocks, 1), across, swap(after(across, *held), 1)]
    own, pack = pack_heads(me, queries, cotangent)
    pack = swap(pack, 1)

    if near_link:
        ups, downs = halves(*weights[5:], 1)
        weights += both_ways(after(ups, parts[1], pack), after(downs, parts[1], pack))
        total = project(me, STEPS[:5], parts, weights[:5], None, depth)
        total = project(me, STEPS[5:7], parts, weights[5:7], total, depth)
        kv, kind, ids, ids_row = project(me, STEPS[7:], parts, weights[7:], total, depth, True, True)
        weight = gather_blocks(me, weights, (kv,))
    else:
        kv, kind, ids, ids_row = project_plain(quarters, parts, weight, depth)
    weight_c = swap(weight, 1)

    kv_far = swap(kv, 2)
    columns = exchange_columns(after(blocks, kv))
    far_own, far_other, far = attend(me_far, own, pack, kv_far, ids, ids_row)
    near_own, near_other, near = attend(me, own, pack, kv, ids, ids_row, (far,))
    columns = after(columns, near)
    grad_kv = (after(near, columns) + swap(far, 2)).astype(BF16)
    attended, grad_queries = place_heads(me, (near_own, swap(near_other, 1), far_own, swap(far_other, 1)))

    mine, away = hidden_grad(me, kind, grad_kv, swap(grad_kv, 1), weight, weight_c, rows)
    columns = over_seq(columns)
    if near_link:
        first = after(grad_kv, away)
        grads = [first, *both_ways(first, first)]
        grads += both_ways(*grads[1:])
        grads += both_ways(*grads[3:])
        grads += both_ways(*halves(*grads[5:], 0))
        total = weight_grad(me, STEPS[:5], columns, grads[:5], None, depth)
        total = weight_grad(me, STEPS[5:7], columns, grads[5:7], total, depth)
        grad_weight = weight_grad(me, STEPS[7:], columns, grads[7:], total, depth, True, True)
    else:
        grad_weight = weight_plain(quarters, columns, lax.all_gather(grad_kv, "fsdp", axis=0), depth)
    grad_tokens = (mine + swap(away, 2).astype(F32)).astype(BF16)
    return attended[None], grad_queries[None], grad_tokens[None], grad_weight


def solution(mesh):
    split = P("fsdp", "seq", None)
    weights = P(None, "fsdp", "seq")
    return jax.shard_map(
        functools.partial(per_device, mesh.shape["fsdp"], mesh.shape["seq"]),
        mesh=mesh,
        in_specs=(split, split, split, P("fsdp", "seq"), P("fsdp", "seq"), weights),
        out_specs=(split, split, split, weights),
        check_vma=False,
    )
```

```python
import functools

import jax
import jax.numpy as jnp
from jax import lax
from jax.experimental import pallas as pl
from jax.experimental.pallas import tpu as pltpu
from jax.sharding import PartitionSpec as P

HEAD_DIM = 128
GROUP = 7
SPAN = GROUP * HEAD_DIM
PAIR = 2 * HEAD_DIM
SCALE = HEAD_DIM ** (-0.5)
LOG2E = 1.4426950408889634
HIDDEN = -1e30
DIGIT = 16
F32 = jnp.float32
BF16 = jnp.bfloat16
ANYWHERE = pl.BlockSpec(memory_space=pl.ANY)
CYCLE = (0, 2, 4, 6, 7, 5, 3, 1)
STEPS = (0, -1, 1, -2, 2, -3, 3, 4)


def contract(a, b, da, db):
    return lax.dot_general(a, b, (((da,), (db,)), ((), ())), preferred_element_type=F32)


def shaped(shape, dtype):
    return jax.ShapeDtypeStruct(shape, dtype)


def call(body, me, operands, out_shape, micros, scratch=(), anywhere=0):
    near = pl.BlockSpec(memory_space=pltpu.VMEM)
    return pl.pallas_call(
        body,
        in_specs=[pl.BlockSpec(memory_space=pltpu.SMEM)]
        + [near] * (len(operands) - anywhere)
        + [ANYWHERE] * anywhere,
        out_specs=[near] * len(out_shape) if isinstance(out_shape, list) else near,
        out_shape=out_shape,
        scratch_shapes=scratch,
        compiler_params=pltpu.CompilerParams(vmem_limit_bytes=24 * 1024 * 1024),
        cost_estimate=pl.CostEstimate(flops=0, bytes_accessed=micros * 3000000, transcendentals=0),
    )(me, *operands)


def owner_at(me_f, by):
    size = len(CYCLE)
    half = size // 2
    line, side = lax.div(me_f, 2), lax.rem(me_f, 2)
    spot = jnp.where(side == 1, size - 1 - line, line)
    spot = lax.rem(spot + (size + by), size)
    return jnp.where(spot < half, 2 * spot, 2 * (size - 1 - spot) + 1)


def after(x, *others):
    return pl.pallas_call(
        lambda *refs: None,
        in_specs=[ANYWHERE] * (1 + len(others)),
        out_specs=ANYWHERE,
        out_shape=shaped(x.shape, x.dtype),
        input_output_aliases={0: 0},
        cost_estimate=pl.CostEstimate(flops=0, bytes_accessed=0, transcendentals=0),
    )(x, *others)


def as_column(row):
    return jnp.broadcast_to(row, (128, row.shape[1])).T[:, :1]


def blocks_kernel(depth, me_ref, tok_ref, kind_ref, ids_ref, out_ref):
    count, rows, lanes = out_ref.shape
    base = lanes - 128
    lane = lax.broadcasted_iota(jnp.int32, (rows, 128), 1) - (depth - base)
    ids = ids_ref[...]
    marks = [as_column(x.astype(F32)) for x in (kind_ref[...], lax.div(ids, DIGIT), lax.rem(ids, DIGIT))]
    for j in range(count):
        out_ref[j, :, :depth] = tok_ref[:, j * depth : (j + 1) * depth]
        last = out_ref[j, :, base:].astype(F32)
        last = jnp.where(lane >= 0, 0.0, last)
        for i, mark in enumerate(marks):
            last = jnp.where(lane == i, mark, last)
        out_ref[j, :, base:] = last.astype(BF16)


def token_blocks(me, tokens, kinds, ids, count):
    rows, width = tokens.shape
    depth = width // count
    lanes = -(-(depth + 3) // 128) * 128
    out = shaped((count, rows, lanes), BF16)
    return call(functools.partial(blocks_kernel, depth), me, (tokens, kinds, ids), out, 1)


def read_marks(block, depth):
    mark = [block[:, depth + i : depth + i + 1].astype(F32) for i in range(3)]
    return mark[0], mark[1] * DIGIT + mark[2]


def pack_kernel(me_ref, q_ref, up_ref, own_ref, other_ref):
    for i in range(4):
        here = pl.ds(pl.multiple_of((me_ref[0] ^ i) * SPAN, SPAN), SPAN)
        out_ref = other_ref if i % 2 else own_ref
        out_ref[i // 2, 0] = q_ref[:, here]
        out_ref[i // 2, 1] = up_ref[:, here]


def pack_heads(me, queries, upstream):
    out = shaped((2, 2, queries.shape[0], SPAN), BF16)
    return call(pack_kernel, me, (queries, upstream), [out, out], 2)


def place_kernel(me_ref, *refs):
    att_ref, gq_ref = refs[4:]
    for i, ref in enumerate(refs[:4]):
        here = pl.ds(pl.multiple_of((me_ref[0] ^ i) * SPAN, SPAN), SPAN)
        att_ref[:, here] = ref[0]
        gq_ref[:, here] = ref[1]


def place_heads(me, found):
    out = shaped((found[0].shape[1], 4 * SPAN), BF16)
    return call(place_kernel, me, found, [out, out], 3)


def project_kernel(steps, depth, halves, first, last, me_ref, *refs):
    parts, refs = refs[:4], refs[4:]
    weights, refs = refs[: len(steps) + halves], refs[len(steps) + halves :]
    rows, lanes = parts[0].shape[1:]
    sums = [0.0, 0.0]
    for b, by in enumerate(steps):
        owner = owner_at(me_ref[1], by)
        left = jnp.concatenate([ref[owner][:, :depth] for ref in parts], axis=0)
        for e in range(2):
            right = weights[e][0] if halves else weights[b][e]
            sums[e] = sums[e] + contract(left, right, 1, 0)
    if not first:
        sums = [s + refs[0][:, e * PAIR : (e + 1) * PAIR] for e, s in enumerate(sums)]
        refs = refs[1:]
    if not last:
        for e in range(2):
            refs[-1][:, e * PAIR : (e + 1) * PAIR] = sums[e]
        return
    kv_ref, kind_ref, ids_ref, ids_row_ref = refs[-4:]
    for r in range(4):
        here = pl.ds(pl.multiple_of((me_ref[0] ^ r) * rows, rows), rows)
        kind, ids = read_marks(parts[r][0], depth)
        mine = slice(r * rows, (r + 1) * rows)
        kv_ref[here, :] = jnp.where(kind == 1.0, sums[1][mine], sums[0][mine]).astype(BF16)
        kind_ref[here, :] = kind
        ids_ref[here, :] = ids
    ids_row_ref[...] = jnp.broadcast_to(ids_ref[...], (4 * rows, 128)).T[:1]


def project(me, steps, parts, weights, total, depth, last=False, halves=False, wait=()):
    rows, lanes = parts[0].shape[1:]
    length = 4 * rows
    before = () if total is None else (total,)
    out = shaped((length, 2 * PAIR), F32)
    if last:
        out = [shaped((length, PAIR), BF16)] + [shaped(x, F32) for x in ((length, 1), (length, 1), (1, length))]
    operands = (*parts, *weights, *before, *wait)
    return call(
        functools.partial(project_kernel, steps, depth, int(halves), total is None, last),
        me,
        operands,
        out,
        3,
        anywhere=len(wait),
    )


def attend_kernel(me_ref, own_ref, pack_ref, kv_ref, ids_ref, ids_row_ref, *refs):
    mine_ref, other_ref, gkv_ref, bias, scores_all, dp_all, pbs, his, los = refs[-9:]
    rows = own_ref.shape[2]
    heads = [slice(h * HEAD_DIM, (h + 1) * HEAD_DIM) for h in range(GROUP)]
    for i in range(2):
        here = pl.ds(pl.multiple_of((me_ref[0] ^ i) * rows, rows), rows)
        bias[i * rows : (i + 1) * rows, :] = jnp.where(ids_row_ref[...] <= ids_ref[here, :], 0.0, HIDDEN)
    keys = kv_ref[:, :HEAD_DIM]
    values = kv_ref[:, HEAD_DIM:]
    spot = me_ref[2]
    q, up = [
        jnp.concatenate([ref[spot, i, :, cols] for ref in (own_ref, pack_ref) for cols in heads], axis=0)
        for i in range(2)
    ]
    scores_all[...] = contract(q, keys, 1, 1)
    dp_all[...] = contract(up, values, 1, 1).astype(BF16)
    for h in range(2 * GROUP):
        here = slice(h * rows, (h + 1) * rows)
        side = h // GROUP
        scores = scores_all[here, :] * (SCALE * LOG2E) + bias[side * rows : (side + 1) * rows, :]
        expo = jnp.exp2(scores - jnp.max(scores, axis=-1, keepdims=True))
        probs = expo * (1.0 / jnp.sum(expo, axis=-1, keepdims=True))
        pbs[here, :] = probs.astype(BF16)
        dp = dp_all[here, :].astype(F32)
        ds = probs * (dp - jnp.sum(probs * dp, axis=-1, keepdims=True))
        hi = ds.astype(BF16)
        his[here, :] = hi
        los[here, :] = (ds - hi.astype(F32)).astype(BF16)
    att = contract(pbs[...], values, 1, 0).astype(BF16)
    gq = ((contract(his[...], keys, 1, 0) + contract(los[...], keys, 1, 0)) * SCALE).astype(BF16)
    for i, ref in enumerate((mine_ref, other_ref)):
        for h, cols in enumerate(heads):
            here = slice((i * GROUP + h) * rows, (i * GROUP + h + 1) * rows)
            ref[0, :, cols] = att[here]
            ref[1, :, cols] = gq[here]
    dk = (contract(q, his[...], 0, 0) + contract(q, los[...], 0, 0)) * SCALE
    dv = contract(up, pbs[...], 0, 0)
    gkv_ref[:, :HEAD_DIM] = dk.T
    gkv_ref[:, HEAD_DIM:] = dv.T


def attend(me, own, pack, kv, ids, ids_row, wait=()):
    rows = own.shape[2]
    length = kv.shape[0]
    stacked = (2 * GROUP * rows, length)
    side = shaped((2, rows, SPAN), BF16)
    return call(
        attend_kernel,
        me,
        (own, pack, kv, ids, ids_row, *wait),
        [side, side, shaped((length, PAIR), F32)],
        6,
        scratch=[pltpu.VMEM((2 * rows, length), F32), pltpu.VMEM(stacked, F32)] + [pltpu.VMEM(stacked, BF16)] * 4,
        anywhere=len(wait),
    )


def by_expert(kind, x):
    return [jnp.where(kind == float(e), x, 0.0).astype(BF16) for e in range(2)]


def hidden_kernel(me_ref, kind_ref, g_ref, gc_ref, w_ref, wc_ref, *refs):
    mine_ref, away_ref = refs[-2:]
    rows = mine_ref.shape[0]
    count, _, depth, _ = w_ref.shape
    masked = []
    for ref in (g_ref, gc_ref):
        sides = []
        for i in range(2):
            here = pl.ds(pl.multiple_of((me_ref[0] ^ (2 * i)) * rows, rows), rows)
            sides.append(by_expert(kind_ref[here, :], ref[here, :].astype(F32)))
        masked += [jnp.concatenate([sides[0][e], sides[1][e]], axis=0) for e in range(2)]
    group = count // 4
    for j in range(4):
        total = 0.0
        for k, ref in enumerate((w_ref, wc_ref)):
            for e in range(2):
                w = ref[j * group : (j + 1) * group, e].reshape(group * depth, PAIR)
                total = total + contract(w, masked[2 * k + e], 1, 1)
        total = total.T
        cols = slice(j * group * depth, (j + 1) * group * depth)
        mine_ref[:, cols] = total[:rows]
        away_ref[:, cols] = total[rows:].astype(BF16)


def hidden_grad(me, kind, grad, grad_c, weight, weight_c, rows, wait=()):
    count, _, depth, _ = weight.shape
    width = count * depth
    return call(
        hidden_kernel,
        me,
        (kind, grad, grad_c, weight, weight_c, *wait),
        [shaped((rows, width), F32), shaped((rows, width), BF16)],
        7,
        anywhere=len(wait),
    )


def weight_kernel(steps, depth, halves, first, last, me_ref, *refs):
    parts, refs = refs[:4], refs[4:]
    grads, refs = refs[: len(steps) + halves], refs[len(steps) + halves :]
    rows, lanes = parts[0].shape[1:]
    size = grads[0].shape[0]
    total = 0.0
    for b, by in enumerate(steps):
        owner = owner_at(me_ref[1], by)
        left = jnp.concatenate([ref[owner] for ref in parts], axis=0)
        quarter = []
        for r in range(4):
            start = (me_ref[0] ^ r) * rows
            if halves:
                inner = pl.ds(pl.multiple_of(lax.rem(start, size), rows), rows)
                quarter.append(jnp.where(start < size, grads[0][inner, :].astype(F32), grads[1][inner, :].astype(F32)))
            else:
                quarter.append(grads[b][pl.ds(pl.multiple_of(start, rows), rows), :].astype(F32))
        kind = left[:, depth : depth + 1].astype(F32)
        right = jnp.concatenate(by_expert(kind, jnp.concatenate(quarter, axis=0)), axis=-1)
        total = total + contract(left, right, 0, 0)
    if not first:
        total = total + refs[0][...]
    if not last:
        refs[-1][...] = total
        return
    for e in range(2):
        refs[-1][e] = total[:depth, e * PAIR : (e + 1) * PAIR]


def weight_grad(me, steps, parts, grads, total, depth, last=False, halves=False):
    rows, lanes = parts[0].shape[1:]
    before = () if total is None else (total,)
    return call(
        functools.partial(weight_kernel, steps, depth, int(halves), total is None, last),
        me,
        (*parts, *grads, *before),
        shaped((2, depth, PAIR) if last else (lanes, 2 * PAIR), F32),
        3,
    )


def gather_kernel(me_ref, *refs):
    blocks, whole_ref = refs[: len(STEPS) + 1], refs[-1]
    for i, block in enumerate(blocks):
        owner = owner_at(me_ref[1], STEPS[min(i, len(STEPS) - 1)])
        if i < len(STEPS) - 1:
            whole_ref[owner] = block[...]
        else:
            whole_ref[owner, i - len(STEPS) + 1] = block[0]


def gather_blocks(me, blocks, wait=()):
    out = shaped((len(CYCLE), *blocks[0].shape), blocks[0].dtype)
    return call(gather_kernel, me, (*blocks, *wait), out, 4, anywhere=len(wait))


def in_order(parts, quarters):
    count, rows, lanes = parts[0].shape
    whole = jnp.stack(parts, axis=1)
    return jnp.take(whole, quarters, axis=1).reshape(count, 4 * rows, lanes)


def project_plain(quarters, parts, weights, depth):
    tokens = in_order(parts, quarters)
    kind, ids = read_marks(tokens[0], depth)
    sums = jnp.einsum("jmk,jekn->emn", tokens[:, :, :depth], weights, preferred_element_type=F32)
    return jnp.where(kind == 1.0, sums[1], sums[0]).astype(BF16), kind, ids, ids.reshape(1, -1)


def weight_plain(quarters, parts, grads, depth):
    tokens = in_order(parts, quarters)
    kind = tokens[:, :, depth : depth + 1].astype(F32)
    sums = [
        jnp.einsum("jmk,jmn->kn", tokens[:, :, :depth], g, preferred_element_type=F32)
        for g in by_expert(kind, grads.astype(F32))
    ]
    return jnp.stack(sums)


def per_device(fsdp, seq, tokens, queries, cotangent, modality, block_ids, kv_weight):
    tokens, queries, cotangent = tokens[0], queries[0], cotangent[0]
    me_f = lax.axis_index("fsdp")
    me_s = lax.axis_index("seq")
    rows, width = tokens.shape
    depth = kv_weight.shape[1]
    near_link = fsdp == len(CYCLE)

    def swap(x, bit):
        return lax.ppermute(x, "seq", [(i, i ^ bit) for i in range(seq)])

    def over_seq(x):
        across = swap(x, 2)
        return [x, swap(x, 1), across, swap(across, 1)]

    def turn(x, by):
        return lax.ppermute(x, "fsdp", [(CYCLE[i], CYCLE[(i + by) % fsdp]) for i in range(fsdp)])

    def both_ways(ups, downs):
        return turn(ups, 1), turn(downs, -1)

    def halves(ups, downs, axis):
        size = ups.shape[axis] // 2
        return lax.slice_in_dim(ups, 0, size, axis=axis), lax.slice_in_dim(downs, size, 2 * size, axis=axis)

    def exchange_columns(x):
        return lax.all_to_all(x, "fsdp", split_axis=0, concat_axis=0, tiled=True)

    me = jnp.stack([me_s, me_f, jnp.int32(0)])
    me_far = jnp.stack([me_s, me_f, jnp.int32(1)])
    quarters = me_s ^ jnp.arange(seq, dtype=jnp.int32)
    if near_link:
        weights = [kv_weight, *both_ways(kv_weight, kv_weight)]
        weights += both_ways(*weights[1:])
        weights += both_ways(*weights[3:])
    else:
        weight = lax.all_gather(kv_weight, "fsdp", axis=0)

    blocks = token_blocks(me, tokens, modality, block_ids, fsdp)
    across = swap(blocks, 2)
    held = (weights[3], weights[4]) if near_link else ()
    parts = [blocks, swap(blocks, 1), across, swap(after(across, *held), 1)]
    own, pack = pack_heads(me, queries, cotangent)
    pack = swap(pack, 1)

    if near_link:
        total = project(me, STEPS[:5], parts, weights[:5], None, depth)
        ups, downs = halves(*weights[5:], 0)
        weights += both_ways(after(ups, pack, total), after(downs, pack, total))
        total = project(me, STEPS[5:7], parts, weights[5:7], total, depth)
        kv, kind, ids, ids_row = project(me, STEPS[7:], parts, weights[7:], total, depth, True, True)
    else:
        kv, kind, ids, ids_row = project_plain(quarters, parts, weight, depth)
    kv_far = swap(kv, 2)
    columns = exchange_columns(after(blocks, kv))
    far_own, far_other, far = attend(me_far, own, pack, kv_far, ids, ids_row)
    near_own, near_other, near = attend(me, own, pack, kv, ids, ids_row, (far,))
    grad_kv = (near + swap(far, 2)).astype(BF16)
    if near_link:
        weight = gather_blocks(me, weights, (far,))
    attended, grad_queries = place_heads(me, (near_own, swap(near_other, 1), far_own, swap(far_other, 1)))

    mine, away = hidden_grad(
        me, kind, grad_kv, swap(grad_kv, 1), weight, swap(weight, 1), rows, (columns,)
    )
    columns = over_seq(after(columns, away))
    if near_link:
        first = after(grad_kv, away)
        grads = [first, *both_ways(first, first)]
        grads += both_ways(*grads[1:])
        grads += both_ways(*grads[3:])
        grads += both_ways(*halves(*grads[5:], 0))
        total = weight_grad(me, STEPS[:5], columns, grads[:5], None, depth)
        total = weight_grad(me, STEPS[5:7], columns, grads[5:7], total, depth)
        grad_weight = weight_grad(me, STEPS[7:], columns, grads[7:], total, depth, True, True)
    else:
        grad_weight = weight_plain(quarters, columns, lax.all_gather(grad_kv, "fsdp", axis=0), depth)
    grad_tokens = (mine + swap(away, 2).astype(F32)).astype(BF16)
    return attended[None], grad_queries[None], grad_tokens[None], grad_weight


def solution(mesh):
    split = P("fsdp", "seq", None)
    weights = P(None, "fsdp", "seq")
    return jax.shard_map(
        functools.partial(per_device, mesh.shape["fsdp"], mesh.shape["seq"]),
        mesh=mesh,
        in_specs=(split, split, split, P("fsdp", "seq"), P("fsdp", "seq"), weights),
        out_specs=(split, split, split, weights),
        check_vma=False,
    )
```

```python
import functools

import jax
import jax.numpy as jnp
from jax import lax
from jax.experimental import pallas as pl
from jax.experimental.pallas import tpu as pltpu
from jax.sharding import PartitionSpec as P

HEAD_DIM = 128
GROUP = 7
SPAN = GROUP * HEAD_DIM
PAIR = 2 * HEAD_DIM
SCALE = HEAD_DIM ** (-0.5)
LOG2E = 1.4426950408889634
HIDDEN = -1e30
DIGIT = 16
F32 = jnp.float32
BF16 = jnp.bfloat16
ANYWHERE = pl.BlockSpec(memory_space=pl.ANY)
CYCLE = (0, 2, 4, 6, 7, 5, 3, 1)
STEPS = (0, -1, 1, -2, 2, -3, 3, 4)


def contract(a, b, da, db):
    return lax.dot_general(a, b, (((da,), (db,)), ((), ())), preferred_element_type=F32)


def shaped(shape, dtype):
    return jax.ShapeDtypeStruct(shape, dtype)


def call(body, me, operands, out_shape, micros, scratch=(), far=(), far_out=(), aliases=None):
    near = pl.BlockSpec(memory_space=pltpu.VMEM)
    outs = [ANYWHERE if i in far_out else near for i in range(len(out_shape))] if isinstance(out_shape, list) else near
    return pl.pallas_call(
        body,
        in_specs=[pl.BlockSpec(memory_space=pltpu.SMEM)]
        + [ANYWHERE if i in far else near for i in range(len(operands))],
        out_specs=outs,
        out_shape=out_shape,
        scratch_shapes=scratch,
        input_output_aliases=aliases or {},
        compiler_params=pltpu.CompilerParams(vmem_limit_bytes=24 * 1024 * 1024),
        cost_estimate=pl.CostEstimate(flops=0, bytes_accessed=micros * 3000000, transcendentals=0),
    )(me, *operands)


def run_copies(copies):
    for copy in copies:
        copy.start()
    for copy in copies:
        copy.wait()


def owner_at(me_f, by):
    size = len(CYCLE)
    half = size // 2
    line, side = lax.div(me_f, 2), lax.rem(me_f, 2)
    spot = jnp.where(side == 1, size - 1 - line, line)
    spot = lax.rem(spot + (size + by), size)
    return jnp.where(spot < half, 2 * spot, 2 * (size - 1 - spot) + 1)


def after(x, *others):
    return pl.pallas_call(
        lambda *refs: None,
        in_specs=[ANYWHERE] * (1 + len(others)),
        out_specs=ANYWHERE,
        out_shape=shaped(x.shape, x.dtype),
        input_output_aliases={0: 0},
        cost_estimate=pl.CostEstimate(flops=0, bytes_accessed=0, transcendentals=0),
    )(x, *others)


def as_column(row):
    return jnp.broadcast_to(row, (128, row.shape[1])).T[:, :1]


def blocks_kernel(depth, me_ref, tok_far, kind_far, ids_far, out_ref, tok_ref, kind_ref, ids_ref, sems):
    pairs = ((tok_far, tok_ref), (kind_far, kind_ref), (ids_far, ids_ref))
    run_copies([pltpu.make_async_copy(a, b, sems.at[i]) for i, (a, b) in enumerate(pairs)])
    count, rows, lanes = out_ref.shape
    base = lanes - 128
    lane = lax.broadcasted_iota(jnp.int32, (rows, 128), 1) - (depth - base)
    ids = ids_ref[...]
    marks = [as_column(x.astype(F32)) for x in (kind_ref[...], lax.div(ids, DIGIT), lax.rem(ids, DIGIT))]
    for j in range(count):
        out_ref[j, :, :depth] = tok_ref[:, j * depth : (j + 1) * depth]
        last = out_ref[j, :, base:].astype(F32)
        last = jnp.where(lane >= 0, 0.0, last)
        for i, mark in enumerate(marks):
            last = jnp.where(lane == i, mark, last)
        out_ref[j, :, base:] = last.astype(BF16)


def token_blocks(me, tokens, kinds, ids, count):
    rows, width = tokens.shape
    depth = width // count
    lanes = -(-(depth + 3) // 128) * 128
    out = shaped((count, rows, lanes), BF16)
    return call(
        functools.partial(blocks_kernel, depth),
        me,
        (tokens, kinds, ids),
        out,
        2,
        scratch=[
            pltpu.VMEM((rows, width), BF16),
            pltpu.VMEM((1, rows), jnp.int32),
            pltpu.VMEM((1, rows), jnp.int32),
            pltpu.SemaphoreType.DMA((3,)),
        ],
        far=(0, 1, 2),
    )


def read_marks(block, depth):
    mark = [block[:, depth + i : depth + i + 1].astype(F32) for i in range(3)]
    return mark[0], mark[1] * DIGIT + mark[2]


def pack_kernel(me_ref, q_far, up_far, own_ref, other_ref, sems):
    copies = []
    for i in range(4):
        here = pl.ds(pl.multiple_of((me_ref[0] ^ i) * SPAN, SPAN), SPAN)
        out_ref = other_ref if i % 2 else own_ref
        for k, far in enumerate((q_far, up_far)):
            copies.append(pltpu.make_async_copy(far.at[:, here], out_ref.at[i // 2, k], sems.at[2 * i + k]))
    run_copies(copies)


def pack_heads(me, queries, upstream):
    out = shaped((2, 2, queries.shape[0], SPAN), BF16)
    return call(
        pack_kernel, me, (queries, upstream), [out, out], 2, scratch=[pltpu.SemaphoreType.DMA((8,))], far=(0, 1)
    )


def place_kernel(me_ref, *refs):
    att_ref, gq_ref = refs[4:]
    for i, ref in enumerate(refs[:4]):
        here = pl.ds(pl.multiple_of((me_ref[0] ^ i) * SPAN, SPAN), SPAN)
        att_ref[:, here] = ref[0]
        gq_ref[:, here] = ref[1]


def place_heads(me, found):
    out = shaped((found[0].shape[1], 4 * SPAN), BF16)
    return call(place_kernel, me, found, [out, out], 3)


def project_kernel(steps, depth, halves, first, last, me_ref, *refs):
    parts, refs = refs[:4], refs[4:]
    weights, refs = refs[: len(steps) + halves], refs[len(steps) + halves :]
    whole_ref, sems = refs[-2:]
    rows, lanes = parts[0].shape[1:]
    owners = [owner_at(me_ref[1], by) for by in steps]
    copies = []
    for i, ref in enumerate(weights):
        there = whole_ref.at[owners[0], pl.ds(i, 1)] if halves else whole_ref.at[owners[i]]
        copies.append(pltpu.make_async_copy(ref, there, sems.at[i]))
    for copy in copies:
        copy.start()
    sums = [0.0, 0.0]
    for b, owner in enumerate(owners):
        left = jnp.concatenate([ref[owner][:, :depth] for ref in parts], axis=0)
        for e in range(2):
            right = weights[e][0] if halves else weights[b][e]
            sums[e] = sums[e] + contract(left, right, 1, 0)
    if not first:
        sums = [s + refs[0][:, e * PAIR : (e + 1) * PAIR] for e, s in enumerate(sums)]
    if not last:
        for e in range(2):
            refs[-3][:, e * PAIR : (e + 1) * PAIR] = sums[e]
    else:
        kv_ref, kind_ref, ids_ref, ids_row_ref = refs[-6:-2]
        for r in range(4):
            here = pl.ds(pl.multiple_of((me_ref[0] ^ r) * rows, rows), rows)
            kind, ids = read_marks(parts[r][0], depth)
            mine = slice(r * rows, (r + 1) * rows)
            kv_ref[here, :] = jnp.where(kind == 1.0, sums[1][mine], sums[0][mine]).astype(BF16)
            kind_ref[here, :] = kind
            ids_ref[here, :] = ids
        ids_row_ref[...] = jnp.broadcast_to(ids_ref[...], (4 * rows, 128)).T[:1]
    for copy in copies:
        copy.wait()


def project(me, steps, parts, weights, before, depth, last=False, halves=False):
    rows, lanes = parts[0].shape[1:]
    length = 4 * rows
    outs = [shaped((length, 2 * PAIR), F32)]
    if last:
        outs = [shaped((length, PAIR), BF16)] + [shaped(x, F32) for x in ((length, 1), (length, 1), (1, length))]
    outs.append(shaped((len(CYCLE), 2, depth, PAIR), BF16))
    operands = (*parts, *weights, *before)
    count = len(operands)
    return call(
        functools.partial(project_kernel, steps, depth, int(halves), not before, last),
        me,
        operands,
        outs,
        3,
        scratch=[pltpu.SemaphoreType.DMA((len(weights),))],
        far=(count - 1,) if before else (),
        far_out=(len(outs) - 1,),
        aliases={count: len(outs) - 1} if before else None,
    )


def attend_kernel(me_ref, own_ref, pack_ref, kv_ref, ids_ref, ids_row_ref, *refs):
    mine_ref, other_ref, gkv_ref, bias, scores_all, dp_all, pbs, his, los = refs[-9:]
    rows = own_ref.shape[2]
    heads = [slice(h * HEAD_DIM, (h + 1) * HEAD_DIM) for h in range(GROUP)]
    for i in range(2):
        here = pl.ds(pl.multiple_of((me_ref[0] ^ i) * rows, rows), rows)
        bias[i * rows : (i + 1) * rows, :] = jnp.where(ids_row_ref[...] <= ids_ref[here, :], 0.0, HIDDEN)
    keys = kv_ref[:, :HEAD_DIM]
    values = kv_ref[:, HEAD_DIM:]
    spot = me_ref[2]
    q, up = [
        jnp.concatenate([ref[spot, i, :, cols] for ref in (own_ref, pack_ref) for cols in heads], axis=0)
        for i in range(2)
    ]
    scores_all[...] = contract(q, keys, 1, 1)
    dp_all[...] = contract(up, values, 1, 1).astype(BF16)
    for h in range(2 * GROUP):
        here = slice(h * rows, (h + 1) * rows)
        side = h // GROUP
        scores = scores_all[here, :] * (SCALE * LOG2E) + bias[side * rows : (side + 1) * rows, :]
        expo = jnp.exp2(scores - jnp.max(scores, axis=-1, keepdims=True))
        probs = expo * (1.0 / jnp.sum(expo, axis=-1, keepdims=True))
        pbs[here, :] = probs.astype(BF16)
        dp = dp_all[here, :].astype(F32)
        ds = probs * (dp - jnp.sum(probs * dp, axis=-1, keepdims=True))
        hi = ds.astype(BF16)
        his[here, :] = hi
        los[here, :] = (ds - hi.astype(F32)).astype(BF16)
    att = contract(pbs[...], values, 1, 0).astype(BF16)
    gq = ((contract(his[...], keys, 1, 0) + contract(los[...], keys, 1, 0)) * SCALE).astype(BF16)
    for i, ref in enumerate((mine_ref, other_ref)):
        for h, cols in enumerate(heads):
            here = slice((i * GROUP + h) * rows, (i * GROUP + h + 1) * rows)
            ref[0, :, cols] = att[here]
            ref[1, :, cols] = gq[here]
    dk = (contract(q, his[...], 0, 0) + contract(q, los[...], 0, 0)) * SCALE
    dv = contract(up, pbs[...], 0, 0)
    gkv_ref[:, :HEAD_DIM] = dk.T
    gkv_ref[:, HEAD_DIM:] = dv.T


def attend(me, own, pack, kv, ids, ids_row, wait=()):
    rows = own.shape[2]
    length = kv.shape[0]
    stacked = (2 * GROUP * rows, length)
    side = shaped((2, rows, SPAN), BF16)
    return call(
        attend_kernel,
        me,
        (own, pack, kv, ids, ids_row, *wait),
        [side, side, shaped((length, PAIR), F32)],
        6,
        scratch=[pltpu.VMEM((2 * rows, length), F32), pltpu.VMEM(stacked, F32)] + [pltpu.VMEM(stacked, BF16)] * 4,
        far=tuple(range(5, 5 + len(wait))),
    )


def by_expert(kind, x):
    return [jnp.where(kind == float(e), x, 0.0).astype(BF16) for e in range(2)]


def hidden_kernel(me_ref, kind_ref, g_ref, gc_ref, w_ref, wc_ref, *refs):
    mine_ref, away_ref = refs[-2:]
    rows = mine_ref.shape[0]
    count, _, depth, _ = w_ref.shape
    masked = []
    for ref in (g_ref, gc_ref):
        sides = []
        for i in range(2):
            here = pl.ds(pl.multiple_of((me_ref[0] ^ (2 * i)) * rows, rows), rows)
            sides.append(by_expert(kind_ref[here, :], ref[here, :].astype(F32)))
        masked += [jnp.concatenate([sides[0][e], sides[1][e]], axis=0) for e in range(2)]
    group = count // 4
    for j in range(4):
        total = 0.0
        for k, ref in enumerate((w_ref, wc_ref)):
            for e in range(2):
                w = ref[j * group : (j + 1) * group, e].reshape(group * depth, PAIR)
                total = total + contract(w, masked[2 * k + e], 1, 1)
        total = total.T
        cols = slice(j * group * depth, (j + 1) * group * depth)
        mine_ref[:, cols] = total[:rows]
        away_ref[:, cols] = total[rows:].astype(BF16)


def hidden_grad(me, kind, grad, grad_c, weight, weight_c, rows):
    count, _, depth, _ = weight.shape
    width = count * depth
    return call(
        hidden_kernel,
        me,
        (kind, grad, grad_c, weight, weight_c),
        [shaped((rows, width), F32), shaped((rows, width), BF16)],
        7,
    )


def share_kernel(steps, depth, me_ref, *refs):
    parts, g_ref, outs = refs[:4], refs[4], refs[5:]
    rows, lanes = parts[0].shape[1:]
    quarter = [g_ref[pl.ds(pl.multiple_of((me_ref[0] ^ r) * rows, rows), rows), :].astype(F32) for r in range(4)]
    kind = jnp.concatenate([read_marks(ref[0], depth)[0] for ref in parts], axis=0)
    right = jnp.concatenate(by_expert(kind, jnp.concatenate(quarter, axis=0)), axis=-1)
    for i, by in enumerate(steps):
        owner = owner_at(me_ref[1], by)
        left = jnp.concatenate([ref[owner] for ref in parts], axis=0)
        total = contract(left, right, 0, 0)
        for e in range(2):
            block = total[:depth, e * PAIR : (e + 1) * PAIR]
            if outs[0].dtype == BF16:
                outs[2 * i + e][0] = block.astype(BF16)
            else:
                outs[i][e] = block


def shares(me, steps, parts, grad, depth, split):
    if split:
        out = [shaped((1, depth, PAIR), BF16)] * (2 * len(steps))
    else:
        out = [shaped((2, depth, PAIR), F32)] * len(steps)
    return call(functools.partial(share_kernel, steps, depth), me, (*parts, grad), out, 1 + len(steps))


def in_order(parts, quarters):
    count, rows, lanes = parts[0].shape
    whole = jnp.stack(parts, axis=1)
    return jnp.take(whole, quarters, axis=1).reshape(count, 4 * rows, lanes)


def project_plain(quarters, parts, weights, depth):
    tokens = in_order(parts, quarters)
    kind, ids = read_marks(tokens[0], depth)
    sums = jnp.einsum("jmk,jekn->emn", tokens[:, :, :depth], weights, preferred_element_type=F32)
    return jnp.where(kind == 1.0, sums[1], sums[0]).astype(BF16), kind, ids, ids.reshape(1, -1)


def weight_plain(quarters, parts, grad, depth):
    tokens = in_order(parts, quarters)
    kind = tokens[0, :, depth : depth + 1].astype(F32)
    sums = [
        jnp.einsum("jmk,mn->jkn", tokens[:, :, :depth], g, preferred_element_type=F32)
        for g in by_expert(kind, grad.astype(F32))
    ]
    return lax.psum_scatter(jnp.stack(sums), "fsdp", scatter_dimension=1)


def per_device(fsdp, seq, tokens, queries, cotangent, modality, block_ids, kv_weight):
    tokens, queries, cotangent = tokens[0], queries[0], cotangent[0]
    me_f = lax.axis_index("fsdp")
    me_s = lax.axis_index("seq")
    rows, width = tokens.shape
    depth = kv_weight.shape[1]
    near_link = fsdp == len(CYCLE)

    def swap(x, bit):
        return lax.ppermute(x, "seq", [(i, i ^ bit) for i in range(seq)])

    def turn(x, by):
        return lax.ppermute(x, "fsdp", [(CYCLE[i], CYCLE[(i + by) % fsdp]) for i in range(fsdp)])

    def both_ways(ups, downs):
        return turn(ups, 1), turn(downs, -1)

    def halves(ups, downs, axis):
        size = ups.shape[axis] // 2
        return lax.slice_in_dim(ups, 0, size, axis=axis), lax.slice_in_dim(downs, size, 2 * size, axis=axis)

    me = jnp.stack([me_s, me_f, jnp.int32(0)])
    me_far = jnp.stack([me_s, me_f, jnp.int32(1)])
    quarters = me_s ^ jnp.arange(seq, dtype=jnp.int32)
    if near_link:
        weights = [kv_weight, *both_ways(kv_weight, kv_weight)]
        weights += both_ways(*weights[1:])
        weights += both_ways(*weights[3:])
    else:
        weight = lax.all_gather(kv_weight, "fsdp", axis=0)

    blocks = token_blocks(me, tokens, modality, block_ids, fsdp)
    across = swap(blocks, 2)
    if near_link:
        across = after(across, weights[3], weights[4])
    parts = [blocks, swap(blocks, 1), across, swap(across, 1)]
    own, pack = pack_heads(me, queries, cotangent)
    pack = swap(pack, 1)

    if near_link:
        ups, downs = halves(*weights[5:], 0)
        weights += both_ways(after(ups, pack), after(downs, pack))
        before = project(me, STEPS[:5], parts, weights[:5], (), depth)
        before = project(me, STEPS[5:7], parts, weights[5:7], before, depth)
        kv, kind, ids, ids_row, weight = project(me, STEPS[7:], parts, weights[7:], before, depth, True, True)
    else:
        kv, kind, ids, ids_row = project_plain(quarters, parts, weight, depth)
    kv_far = swap(kv, 2)
    far_own, far_other, far = attend(me_far, own, pack, kv_far, ids, ids_row)
    near_own, near_other, near = attend(me, own, pack, kv, ids, ids_row, (far,))
    grad_kv = (near + swap(far, 2)).astype(BF16)
    attended, grad_queries = place_heads(me, (near_own, swap(near_other, 1), far_own, swap(far_other, 1)))

    if near_link:
        ups, downs = both_ways(*shares(me, STEPS[7:], parts, grad_kv, depth, True))
        terms = shares(me, STEPS[5:7], parts, grad_kv, depth, False)
        terms += shares(me, STEPS[:5], parts, grad_kv, depth, False)
        none = jnp.zeros_like(ups)
        ups, downs = jnp.concatenate([ups, none]), jnp.concatenate([none, downs])
        for i in (0, 5, 3):
            down, up = terms[i : i + 2]
            ups, downs = both_ways((up + ups.astype(F32)).astype(BF16), (down + downs.astype(F32)).astype(BF16))
        grad_weight = terms[2] + ups.astype(F32) + downs.astype(F32)
    else:
        grad_weight = weight_plain(quarters, parts, grad_kv, depth)
    mine, away = hidden_grad(me, kind, grad_kv, swap(grad_kv, 1), weight, swap(weight, 1), rows)
    grad_tokens = (mine + swap(away, 2).astype(F32)).astype(BF16)
    return attended[None], grad_queries[None], grad_tokens[None], grad_weight


def solution(mesh):
    split = P("fsdp", "seq", None)
    weights = P(None, "fsdp", "seq")
    return jax.shard_map(
        functools.partial(per_device, mesh.shape["fsdp"], mesh.shape["seq"]),
        mesh=mesh,
        in_specs=(split, split, split, P("fsdp", "seq"), P("fsdp", "seq"), weights),
        out_specs=(split, split, split, weights),
        check_vma=False,
    )
```

```python
import functools

import jax
import jax.numpy as jnp
from jax import lax
from jax.experimental import pallas as pl
from jax.experimental.pallas import tpu as pltpu
from jax.sharding import PartitionSpec as P

HEAD_DIM = 128
GROUP = 7
SPAN = GROUP * HEAD_DIM
PAIR = 2 * HEAD_DIM
SCALE = HEAD_DIM ** (-0.5)
LOG2E = 1.4426950408889634
HIDDEN = -1e30
DIGIT = 16
F32 = jnp.float32
BF16 = jnp.bfloat16
ANYWHERE = pl.BlockSpec(memory_space=pl.ANY)
IN_HBM = pl.BlockSpec(memory_space=pltpu.HBM)
CYCLE = (0, 2, 4, 6, 7, 5, 3, 1)
STEPS = (0, -1, 1, -2, 2, -3, 3, 4)


def contract(a, b, da, db):
    return lax.dot_general(a, b, (((da,), (db,)), ((), ())), preferred_element_type=F32)


def shaped(shape, dtype):
    return jax.ShapeDtypeStruct(shape, dtype)


def call(body, me, operands, out_shape, micros, scratch=(), far=(), far_out=(), aliases=None, hbm=()):
    near = pl.BlockSpec(memory_space=pltpu.VMEM)
    outs = [ANYWHERE if i in far_out else near for i in range(len(out_shape))] if isinstance(out_shape, list) else near
    return pl.pallas_call(
        body,
        in_specs=[pl.BlockSpec(memory_space=pltpu.SMEM)]
        + [ANYWHERE if i in far else IN_HBM if i in hbm else near for i in range(len(operands))],
        out_specs=outs,
        out_shape=out_shape,
        scratch_shapes=scratch,
        input_output_aliases=aliases or {},
        compiler_params=pltpu.CompilerParams(vmem_limit_bytes=24 * 1024 * 1024),
        cost_estimate=pl.CostEstimate(flops=0, bytes_accessed=micros * 3000000, transcendentals=0),
    )(me, *operands)


def run_copies(copies):
    for copy in copies:
        copy.start()
    for copy in copies:
        copy.wait()


def owner_at(me_f, by):
    size = len(CYCLE)
    half = size // 2
    line, side = lax.div(me_f, 2), lax.rem(me_f, 2)
    spot = jnp.where(side == 1, size - 1 - line, line)
    spot = lax.rem(spot + (size + by), size)
    return jnp.where(spot < half, 2 * spot, 2 * (size - 1 - spot) + 1)


def after(x, *others):
    return pl.pallas_call(
        lambda *refs: None,
        in_specs=[ANYWHERE] * (1 + len(others)),
        out_specs=ANYWHERE,
        out_shape=shaped(x.shape, x.dtype),
        input_output_aliases={0: 0},
        cost_estimate=pl.CostEstimate(flops=0, bytes_accessed=0, transcendentals=0),
    )(x, *others)


def as_column(row):
    return jnp.broadcast_to(row, (128, row.shape[1])).T[:, :1]


def blocks_kernel(depth, me_ref, tok_far, kind_far, ids_far, out_ref, tok_ref, kind_ref, ids_ref, sems):
    pairs = ((tok_far, tok_ref), (kind_far, kind_ref), (ids_far, ids_ref))
    run_copies([pltpu.make_async_copy(a, b, sems.at[i]) for i, (a, b) in enumerate(pairs)])
    count, rows, lanes = out_ref.shape
    base = lanes - 128
    lane = lax.broadcasted_iota(jnp.int32, (rows, 128), 1) - (depth - base)
    ids = ids_ref[...]
    marks = [as_column(x.astype(F32)) for x in (kind_ref[...], lax.div(ids, DIGIT), lax.rem(ids, DIGIT))]
    for j in range(count):
        out_ref[j, :, :depth] = tok_ref[:, j * depth : (j + 1) * depth]
        last = out_ref[j, :, base:].astype(F32)
        last = jnp.where(lane >= 0, 0.0, last)
        for i, mark in enumerate(marks):
            last = jnp.where(lane == i, mark, last)
        out_ref[j, :, base:] = last.astype(BF16)


def token_blocks(me, tokens, kinds, ids, count):
    rows, width = tokens.shape
    depth = width // count
    lanes = -(-(depth + 3) // 128) * 128
    out = shaped((count, rows, lanes), BF16)
    return call(
        functools.partial(blocks_kernel, depth),
        me,
        (tokens, kinds, ids),
        out,
        2,
        scratch=[
            pltpu.VMEM((rows, width), BF16),
            pltpu.VMEM((1, rows), jnp.int32),
            pltpu.VMEM((1, rows), jnp.int32),
            pltpu.SemaphoreType.DMA((3,)),
        ],
        hbm=(0, 1, 2),
    )


def read_marks(block, depth):
    mark = [block[:, depth + i : depth + i + 1].astype(F32) for i in range(3)]
    return mark[0], mark[1] * DIGIT + mark[2]


def pack_kernel(me_ref, q_far, up_far, own_ref, other_ref, sems):
    copies = []
    for i in range(4):
        here = pl.ds(pl.multiple_of((me_ref[0] ^ i) * SPAN, SPAN), SPAN)
        out_ref = other_ref if i % 2 else own_ref
        for k, far in enumerate((q_far, up_far)):
            copies.append(pltpu.make_async_copy(far.at[:, here], out_ref.at[i // 2, k], sems.at[2 * i + k]))
    run_copies(copies)


def pack_heads(me, queries, upstream):
    out = shaped((2, 2, queries.shape[0], SPAN), BF16)
    return call(
        pack_kernel, me, (queries, upstream), [out, out], 2, scratch=[pltpu.SemaphoreType.DMA((8,))], hbm=(0, 1)
    )


def place_kernel(me_ref, *refs):
    att_ref, gq_ref = refs[4:]
    for i, ref in enumerate(refs[:4]):
        here = pl.ds(pl.multiple_of((me_ref[0] ^ i) * SPAN, SPAN), SPAN)
        att_ref[:, here] = ref[0]
        gq_ref[:, here] = ref[1]


def place_heads(me, found):
    out = shaped((found[0].shape[1], 4 * SPAN), BF16)
    return call(place_kernel, me, found, [out, out], 3)


def project_kernel(steps, depth, halves, first, last, me_ref, *refs):
    parts, refs = refs[:4], refs[4:]
    weights, refs = refs[: len(steps) + halves], refs[len(steps) + halves :]
    whole_ref, sems = refs[-2:]
    rows, lanes = parts[0].shape[1:]
    owners = [owner_at(me_ref[1], by) for by in steps]
    copies = []
    for i, ref in enumerate(weights):
        there = whole_ref.at[owners[0], pl.ds(i, 1)] if halves else whole_ref.at[owners[i]]
        copies.append(pltpu.make_async_copy(ref, there, sems.at[i]))
    for copy in copies:
        copy.start()
    sums = [0.0, 0.0]
    for b, owner in enumerate(owners):
        left = jnp.concatenate([ref[owner][:, :depth] for ref in parts], axis=0)
        for e in range(2):
            right = weights[e][0] if halves else weights[b][e]
            sums[e] = sums[e] + contract(left, right, 1, 0)
    if not first:
        sums = [s + refs[0][:, e * PAIR : (e + 1) * PAIR] for e, s in enumerate(sums)]
    if not last:
        for e in range(2):
            refs[-3][:, e * PAIR : (e + 1) * PAIR] = sums[e]
    else:
        kv_ref, kind_ref, ids_ref, ids_row_ref = refs[-6:-2]
        for r in range(4):
            here = pl.ds(pl.multiple_of((me_ref[0] ^ r) * rows, rows), rows)
            kind, ids = read_marks(parts[r][0], depth)
            mine = slice(r * rows, (r + 1) * rows)
            kv_ref[here, :] = jnp.where(kind == 1.0, sums[1][mine], sums[0][mine]).astype(BF16)
            kind_ref[here, :] = kind
            ids_ref[here, :] = ids
        ids_row_ref[...] = jnp.broadcast_to(ids_ref[...], (4 * rows, 128)).T[:1]
    for copy in copies:
        copy.wait()


def project(me, steps, parts, weights, before, depth, last=False, halves=False):
    rows, lanes = parts[0].shape[1:]
    length = 4 * rows
    outs = [shaped((length, 2 * PAIR), F32)]
    if last:
        outs = [shaped((length, PAIR), BF16)] + [shaped(x, F32) for x in ((length, 1), (length, 1), (1, length))]
    outs.append(shaped((len(CYCLE), 2, depth, PAIR), BF16))
    operands = (*parts, *weights, *before)
    count = len(operands)
    return call(
        functools.partial(project_kernel, steps, depth, int(halves), not before, last),
        me,
        operands,
        outs,
        3,
        scratch=[pltpu.SemaphoreType.DMA((len(weights),))],
        far=(count - 1,) if before else (),
        far_out=(len(outs) - 1,),
        aliases={count: len(outs) - 1} if before else None,
    )


def halve_kernel(me_ref, ups_ref, downs_ref, *refs):
    refs[-2][...] = ups_ref[:1]
    refs[-1][...] = downs_ref[1:]


def halve(me, ups, downs, wait):
    out = [shaped((1, *ups.shape[1:]), ups.dtype)] * 2
    return call(halve_kernel, me, (ups, downs, *wait), out, 1, far=tuple(range(2, 2 + len(wait))))


def attend_kernel(me_ref, own_ref, pack_ref, kv_ref, ids_ref, ids_row_ref, *refs):
    mine_ref, other_ref, gkv_ref, bias, scores_all, dp_all, pbs, his, los = refs[-9:]
    rows = own_ref.shape[2]
    heads = [slice(h * HEAD_DIM, (h + 1) * HEAD_DIM) for h in range(GROUP)]
    for i in range(2):
        here = pl.ds(pl.multiple_of((me_ref[0] ^ i) * rows, rows), rows)
        bias[i * rows : (i + 1) * rows, :] = jnp.where(ids_row_ref[...] <= ids_ref[here, :], 0.0, HIDDEN)
    keys = kv_ref[:, :HEAD_DIM]
    values = kv_ref[:, HEAD_DIM:]
    spot = me_ref[2]
    q, up = [
        jnp.concatenate([ref[spot, i, :, cols] for ref in (own_ref, pack_ref) for cols in heads], axis=0)
        for i in range(2)
    ]
    scores_all[...] = contract(q, keys, 1, 1)
    dp_all[...] = contract(up, values, 1, 1).astype(BF16)
    for h in range(2 * GROUP):
        here = slice(h * rows, (h + 1) * rows)
        side = h // GROUP
        scores = scores_all[here, :] * (SCALE * LOG2E) + bias[side * rows : (side + 1) * rows, :]
        expo = jnp.exp2(scores - jnp.max(scores, axis=-1, keepdims=True))
        probs = expo * (1.0 / jnp.sum(expo, axis=-1, keepdims=True))
        pbs[here, :] = probs.astype(BF16)
        dp = dp_all[here, :].astype(F32)
        ds = probs * (dp - jnp.sum(probs * dp, axis=-1, keepdims=True))
        hi = ds.astype(BF16)
        his[here, :] = hi
        los[here, :] = (ds - hi.astype(F32)).astype(BF16)
    att = contract(pbs[...], values, 1, 0).astype(BF16)
    gq = ((contract(his[...], keys, 1, 0) + contract(los[...], keys, 1, 0)) * SCALE).astype(BF16)
    for i, ref in enumerate((mine_ref, other_ref)):
        for h, cols in enumerate(heads):
            here = slice((i * GROUP + h) * rows, (i * GROUP + h + 1) * rows)
            ref[0, :, cols] = att[here]
            ref[1, :, cols] = gq[here]
    dk = (contract(q, his[...], 0, 0) + contract(q, los[...], 0, 0)) * SCALE
    dv = contract(up, pbs[...], 0, 0)
    gkv_ref[:, :HEAD_DIM] = dk.T
    gkv_ref[:, HEAD_DIM:] = dv.T


def attend(me, own, pack, kv, ids, ids_row, wait=()):
    rows = own.shape[2]
    length = kv.shape[0]
    stacked = (2 * GROUP * rows, length)
    side = shaped((2, rows, SPAN), BF16)
    return call(
        attend_kernel,
        me,
        (own, pack, kv, ids, ids_row, *wait),
        [side, side, shaped((length, PAIR), F32)],
        6,
        scratch=[pltpu.VMEM((2 * rows, length), F32), pltpu.VMEM(stacked, F32)] + [pltpu.VMEM(stacked, BF16)] * 4,
        far=tuple(range(5, 5 + len(wait))),
    )


def by_expert(kind, x):
    return [jnp.where(kind == float(e), x, 0.0).astype(BF16) for e in range(2)]


def hidden_kernel(me_ref, kind_ref, g_ref, gc_ref, w_ref, wc_ref, *refs):
    mine_ref, away_ref = refs[-2:]
    rows = mine_ref.shape[0]
    count, _, depth, _ = w_ref.shape
    masked = []
    for ref in (g_ref, gc_ref):
        sides = []
        for i in range(2):
            here = pl.ds(pl.multiple_of((me_ref[0] ^ (2 * i)) * rows, rows), rows)
            sides.append(by_expert(kind_ref[here, :], ref[here, :].astype(F32)))
        masked += [jnp.concatenate([sides[0][e], sides[1][e]], axis=0) for e in range(2)]
    group = count // 4
    for j in range(4):
        total = 0.0
        for k, ref in enumerate((w_ref, wc_ref)):
            for e in range(2):
                w = ref[j * group : (j + 1) * group, e].reshape(group * depth, PAIR)
                total = total + contract(w, masked[2 * k + e], 1, 1)
        total = total.T
        cols = slice(j * group * depth, (j + 1) * group * depth)
        mine_ref[:, cols] = total[:rows]
        away_ref[:, cols] = total[rows:].astype(BF16)


def hidden_grad(me, kind, grad, grad_c, weight, weight_c, rows):
    count, _, depth, _ = weight.shape
    width = count * depth
    return call(
        hidden_kernel,
        me,
        (kind, grad, grad_c, weight, weight_c),
        [shaped((rows, width), F32), shaped((rows, width), BF16)],
        7,
    )


def share_kernel(steps, depth, split, me_ref, *refs):
    parts, g_ref, outs = refs[:4], refs[4], refs[-(2 if split else 1) * len(steps) :]
    rows, lanes = parts[0].shape[1:]
    quarter = [g_ref[pl.ds(pl.multiple_of((me_ref[0] ^ r) * rows, rows), rows), :].astype(F32) for r in range(4)]
    kind = jnp.concatenate([read_marks(ref[0], depth)[0] for ref in parts], axis=0)
    right = jnp.concatenate(by_expert(kind, jnp.concatenate(quarter, axis=0)), axis=-1)
    for i, by in enumerate(steps):
        owner = owner_at(me_ref[1], by)
        left = jnp.concatenate([ref[owner] for ref in parts], axis=0)
        total = contract(left, right, 0, 0)
        for e in range(2):
            block = total[:depth, e * PAIR : (e + 1) * PAIR]
            if split:
                outs[2 * i + e][0] = block.astype(BF16)
            else:
                outs[i][e] = block


def shares(me, steps, parts, grad, depth, split=False, wait=()):
    if split:
        out = [shaped((1, depth, PAIR), BF16)] * (2 * len(steps))
    else:
        out = [shaped((2, depth, PAIR), F32)] * len(steps)
    far = tuple(range(5, 5 + len(wait)))
    return call(functools.partial(share_kernel, steps, depth, split), me, (*parts, grad, *wait), out, 1 + len(steps), far=far)


def in_order(parts, quarters):
    count, rows, lanes = parts[0].shape
    whole = jnp.stack(parts, axis=1)
    return jnp.take(whole, quarters, axis=1).reshape(count, 4 * rows, lanes)


def project_plain(quarters, parts, weights, depth):
    tokens = in_order(parts, quarters)
    kind, ids = read_marks(tokens[0], depth)
    sums = jnp.einsum("jmk,jekn->emn", tokens[:, :, :depth], weights, preferred_element_type=F32)
    return jnp.where(kind == 1.0, sums[1], sums[0]).astype(BF16), kind, ids, ids.reshape(1, -1)


def weight_plain(quarters, parts, grad, depth):
    tokens = in_order(parts, quarters)
    kind = tokens[0, :, depth : depth + 1].astype(F32)
    sums = [
        jnp.einsum("jmk,mn->jkn", tokens[:, :, :depth], g, preferred_element_type=F32)
        for g in by_expert(kind, grad.astype(F32))
    ]
    return lax.psum_scatter(jnp.stack(sums), "fsdp", scatter_dimension=1)


def per_device(fsdp, seq, tokens, queries, cotangent, modality, block_ids, kv_weight):
    tokens, queries, cotangent = tokens[0], queries[0], cotangent[0]
    me_f = lax.axis_index("fsdp")
    me_s = lax.axis_index("seq")
    rows, width = tokens.shape
    depth = kv_weight.shape[1]
    near_link = fsdp == len(CYCLE)

    def swap(x, bit):
        return lax.ppermute(x, "seq", [(i, i ^ bit) for i in range(seq)])

    def turn(x, by):
        return lax.ppermute(x, "fsdp", [(CYCLE[i], CYCLE[(i + by) % fsdp]) for i in range(fsdp)])

    def both_ways(ups, downs):
        return turn(ups, 1), turn(downs, -1)

    me = jnp.stack([me_s, me_f, jnp.int32(0)])
    me_far = jnp.stack([me_s, me_f, jnp.int32(1)])
    quarters = me_s ^ jnp.arange(seq, dtype=jnp.int32)
    if near_link:
        weights = [kv_weight, *both_ways(kv_weight, kv_weight)]
        weights += both_ways(*weights[1:])
        weights += both_ways(*weights[3:])
    else:
        weight = lax.all_gather(kv_weight, "fsdp", axis=0)

    blocks = token_blocks(me, tokens, modality, block_ids, fsdp)
    across = swap(blocks, 2)
    if near_link:
        across = after(across, weights[3], weights[4])
    parts = [blocks, swap(blocks, 1), across, swap(across, 1)]
    own, pack = pack_heads(me, queries, cotangent)
    pack = swap(pack, 1)

    if near_link:
        before = project(me, STEPS[:5], parts, weights[:5], (), depth)
        weights += both_ways(*halve(me, *weights[5:], (pack, before[0])))
        before = project(me, STEPS[5:7], parts, weights[5:7], before, depth)
        kv, kind, ids, ids_row, weight = project(me, STEPS[7:], parts, weights[7:], before, depth, True, True)
    else:
        kv, kind, ids, ids_row = project_plain(quarters, parts, weight, depth)
    kv_far = swap(kv, 2)
    far_own, far_other, far = attend(me_far, own, pack, kv_far, ids, ids_row)
    near_own, near_other, near = attend(me, own, pack, kv, ids, ids_row, (far,))
    grad_kv = (near + swap(far, 2)).astype(BF16)
    attended, grad_queries = place_heads(me, (near_own, swap(near_other, 1), far_own, swap(far_other, 1)))

    grad_c = swap(grad_kv, 1)
    if near_link:
        ups, downs = both_ways(*shares(me, STEPS[7:], parts, grad_kv, depth, True))
    mine, away = hidden_grad(me, kind, grad_kv, grad_c, weight, swap(weight, 1), rows)
    if near_link:
        terms = shares(me, STEPS[5:7], parts, grad_kv, depth, wait=(away,))
        terms += shares(me, STEPS[:5], parts, grad_kv, depth)
        none = jnp.zeros_like(ups)
        ups, downs = jnp.concatenate([ups, none]), jnp.concatenate([none, downs])
        for i in (0, 5, 3):
            down, up = terms[i : i + 2]
            ups, downs = both_ways((up + ups.astype(F32)).astype(BF16), (down + downs.astype(F32)).astype(BF16))
        grad_weight = terms[2] + ups.astype(F32) + downs.astype(F32)
    else:
        grad_weight = weight_plain(quarters, parts, grad_kv, depth)
    grad_tokens = (mine + swap(away, 2).astype(F32)).astype(BF16)
    return attended[None], grad_queries[None], grad_tokens[None], grad_weight


def solution(mesh):
    split = P("fsdp", "seq", None)
    weights = P(None, "fsdp", "seq")
    return jax.shard_map(
        functools.partial(per_device, mesh.shape["fsdp"], mesh.shape["seq"]),
        mesh=mesh,
        in_specs=(split, split, split, P("fsdp", "seq"), P("fsdp", "seq"), weights),
        out_specs=(split, split, split, weights),
        check_vma=False,
    )
```

```python
import functools

import jax
import jax.numpy as jnp
from jax import lax
from jax.experimental import pallas as pl
from jax.experimental.pallas import tpu as pltpu
from jax.sharding import PartitionSpec as P

HEAD_DIM = 128
GROUP = 7
SPAN = GROUP * HEAD_DIM
PAIR = 2 * HEAD_DIM
SCALE = HEAD_DIM ** (-0.5)
LOG2E = 1.4426950408889634
HIDDEN = -1e30
DIGIT = 16
F32 = jnp.float32
BF16 = jnp.bfloat16
ANYWHERE = pl.BlockSpec(memory_space=pl.ANY)
CYCLE = (0, 2, 4, 6, 7, 5, 3, 1)
STEPS = (0, -1, 1, -2, 2, -3, 3, 4)


def contract(a, b, da, db):
    return lax.dot_general(a, b, (((da,), (db,)), ((), ())), preferred_element_type=F32)


def shaped(shape, dtype):
    return jax.ShapeDtypeStruct(shape, dtype)


def call(body, me, operands, out_shape, micros, scratch=(), far=(), far_out=(), aliases=None):
    near = pl.BlockSpec(memory_space=pltpu.VMEM)
    outs = [ANYWHERE if i in far_out else near for i in range(len(out_shape))] if isinstance(out_shape, list) else near
    return pl.pallas_call(
        body,
        in_specs=[pl.BlockSpec(memory_space=pltpu.SMEM)]
        + [ANYWHERE if i in far else near for i in range(len(operands))],
        out_specs=outs,
        out_shape=out_shape,
        scratch_shapes=scratch,
        input_output_aliases=aliases or {},
        compiler_params=pltpu.CompilerParams(vmem_limit_bytes=24 * 1024 * 1024),
        cost_estimate=pl.CostEstimate(flops=0, bytes_accessed=micros * 3000000, transcendentals=0),
    )(me, *operands)


def owner_at(me_f, by):
    size = len(CYCLE)
    half = size // 2
    line, side = lax.div(me_f, 2), lax.rem(me_f, 2)
    spot = jnp.where(side == 1, size - 1 - line, line)
    spot = lax.rem(spot + (size + by), size)
    return jnp.where(spot < half, 2 * spot, 2 * (size - 1 - spot) + 1)


def after_kernel(x_ref, other_ref, out_ref):
    out_ref[...] = x_ref[...]


def after(x, other):
    near = pl.BlockSpec(memory_space=pltpu.VMEM)
    return pl.pallas_call(
        after_kernel,
        in_specs=[near, ANYWHERE],
        out_specs=near,
        out_shape=shaped(x.shape, x.dtype),
        cost_estimate=pl.CostEstimate(flops=0, bytes_accessed=3000000, transcendentals=0),
    )(x, other)


def as_column(row):
    return jnp.broadcast_to(row, (128, row.shape[1])).T[:, :1]


def blocks_kernel(depth, me_ref, tok_ref, ids_ref, out_ref):
    count, rows, lanes = out_ref.shape
    base = lanes - 128
    lane = lax.broadcasted_iota(jnp.int32, (rows, 128), 1) - (depth - base)
    ids = lax.div(ids_ref[...], 2)
    marks = (lax.rem(ids_ref[...], 2), lax.div(ids, DIGIT), lax.rem(ids, DIGIT))
    marks = [as_column(x.astype(F32)) for x in marks]
    for j in range(count):
        out_ref[j, :, :depth] = tok_ref[:, j * depth : (j + 1) * depth]
        last = out_ref[j, :, base:].astype(F32)
        last = jnp.where(lane >= 0, 0.0, last)
        for i, mark in enumerate(marks):
            last = jnp.where(lane == i, mark, last)
        out_ref[j, :, base:] = last.astype(BF16)


def token_blocks(me, tokens, ids, count):
    rows, width = tokens.shape
    depth = width // count
    lanes = -(-(depth + 3) // 128) * 128
    out = shaped((count, rows, lanes), BF16)
    return call(functools.partial(blocks_kernel, depth), me, (tokens, ids), out, 2)


def read_marks(block, depth):
    mark = [block[:, depth + i : depth + i + 1].astype(F32) for i in range(3)]
    return mark[0], mark[1] * DIGIT + mark[2]


def place_kernel(me_ref, *refs):
    att_ref, gq_ref = refs[4:]
    for i, ref in enumerate(refs[:4]):
        here = pl.ds(pl.multiple_of((me_ref[0] ^ i) * SPAN, SPAN), SPAN)
        att_ref[:, here] = ref[0]
        gq_ref[:, here] = ref[1]


def place_heads(me, found):
    out = shaped((found[0].shape[1], 4 * SPAN), BF16)
    return call(place_kernel, me, found, [out, out], 3)


def project_kernel(steps, depth, halves, first, last, me_ref, *refs):
    parts, refs = refs[:4], refs[4:]
    weights, refs = refs[: len(steps) + halves], refs[len(steps) + halves :]
    whole_ref, sems = refs[-2:]
    rows, lanes = parts[0].shape[1:]
    owners = [owner_at(me_ref[1], by) for by in steps]
    copies = []
    for i, ref in enumerate(weights):
        there = whole_ref.at[owners[0], pl.ds(i, 1)] if halves else whole_ref.at[owners[i]]
        copies.append(pltpu.make_async_copy(ref, there, sems.at[i]))
    for copy in copies:
        copy.start()
    sums = [0.0, 0.0]
    for b, owner in enumerate(owners):
        left = jnp.concatenate([ref[owner][:, :depth] for ref in parts], axis=0)
        for e in range(2):
            right = weights[e][0] if halves else weights[b][e]
            sums[e] = sums[e] + contract(left, right, 1, 0)
    if not first:
        sums = [s + refs[0][:, e * PAIR : (e + 1) * PAIR] for e, s in enumerate(sums)]
    if not last:
        for e in range(2):
            refs[-3][:, e * PAIR : (e + 1) * PAIR] = sums[e]
    else:
        kv_ref, kind_ref, ids_ref, ids_row_ref = refs[-6:-2]
        for r in range(4):
            here = pl.ds(pl.multiple_of((me_ref[0] ^ r) * rows, rows), rows)
            kind, ids = read_marks(parts[r][0], depth)
            mine = slice(r * rows, (r + 1) * rows)
            kv_ref[here, :] = jnp.where(kind == 1.0, sums[1][mine], sums[0][mine]).astype(BF16)
            kind_ref[here, :] = kind
            ids_ref[here, :] = ids
        ids_row_ref[...] = jnp.broadcast_to(ids_ref[...], (4 * rows, 128)).T[:1]
    for copy in copies:
        copy.wait()


def project(me, steps, parts, weights, before, depth, last=False, halves=False):
    rows, lanes = parts[0].shape[1:]
    length = 4 * rows
    outs = [shaped((length, 2 * PAIR), F32)]
    if last:
        outs = [shaped((length, PAIR), BF16)] + [shaped(x, F32) for x in ((length, 1), (length, 1), (1, length))]
    outs.append(shaped((len(CYCLE), 2, depth, PAIR), BF16))
    operands = (*parts, *weights, *before)
    count = len(operands)
    return call(
        functools.partial(project_kernel, steps, depth, int(halves), not before, last),
        me,
        operands,
        outs,
        3,
        scratch=[pltpu.SemaphoreType.DMA((len(weights),))],
        far=(count - 1,) if before else (),
        far_out=(len(outs) - 1,),
        aliases={count: len(outs) - 1} if before else None,
    )


def halve_kernel(me_ref, ups_ref, downs_ref, *refs):
    refs[-2][...] = ups_ref[:1]
    refs[-1][...] = downs_ref[1:]


def halve(me, ups, downs, wait):
    out = [shaped((1, *ups.shape[1:]), ups.dtype)] * 2
    return call(halve_kernel, me, (ups, downs, *wait), out, 1, far=tuple(range(2, 2 + len(wait))))


def attend_kernel(me_ref, q_ref, up_ref, q_other, up_other, kv_ref, ids_ref, ids_row_ref, *refs):
    mine_ref, other_ref, early_ref, late_ref, bias, scores_all, dp_all, pbs, his, los = refs[-10:]
    rows = q_ref.shape[0]
    heads = [slice(h * HEAD_DIM, (h + 1) * HEAD_DIM) for h in range(GROUP)]
    for i in range(2):
        here = pl.ds(pl.multiple_of((me_ref[0] ^ i) * rows, rows), rows)
        bias[i * rows : (i + 1) * rows, :] = jnp.where(ids_row_ref[...] <= ids_ref[here, :], 0.0, HIDDEN)
    keys = kv_ref[:, :HEAD_DIM]
    values = kv_ref[:, HEAD_DIM:]
    start = me_ref[2] * SPAN
    places = [pl.ds(pl.multiple_of(start + h * HEAD_DIM, HEAD_DIM), HEAD_DIM) for h in range(GROUP)]
    q, up = [
        jnp.concatenate([ref[:, place] for ref in pair for place in places], axis=0)
        for pair in ((q_ref, q_other), (up_ref, up_other))
    ]
    scores_all[...] = contract(q, keys, 1, 1)
    dp_all[...] = contract(up, values, 1, 1).astype(BF16)
    for h in range(2 * GROUP):
        here = slice(h * rows, (h + 1) * rows)
        side = h // GROUP
        scores = scores_all[here, :] * (SCALE * LOG2E) + bias[side * rows : (side + 1) * rows, :]
        expo = jnp.exp2(scores - jnp.max(scores, axis=-1, keepdims=True))
        probs = expo * (1.0 / jnp.sum(expo, axis=-1, keepdims=True))
        pbs[here, :] = probs.astype(BF16)
        dp = dp_all[here, :].astype(F32)
        ds = probs * (dp - jnp.sum(probs * dp, axis=-1, keepdims=True))
        hi = ds.astype(BF16)
        his[here, :] = hi
        los[here, :] = (ds - hi.astype(F32)).astype(BF16)
    att = contract(pbs[...], values, 1, 0).astype(BF16)
    gq = ((contract(his[...], keys, 1, 0) + contract(los[...], keys, 1, 0)) * SCALE).astype(BF16)
    for i, ref in enumerate((mine_ref, other_ref)):
        for h, cols in enumerate(heads):
            here = slice((i * GROUP + h) * rows, (i * GROUP + h + 1) * rows)
            ref[0, :, cols] = att[here]
            ref[1, :, cols] = gq[here]
    dk = (contract(q, his[...], 0, 0) + contract(q, los[...], 0, 0)) * SCALE
    dv = contract(up, pbs[...], 0, 0)
    half = early_ref.shape[0]
    for i, x in enumerate((dk.T, dv.T)):
        cols = slice(i * HEAD_DIM, (i + 1) * HEAD_DIM)
        early_ref[:, cols] = x[:half]
        late_ref[:, cols] = x[half:].astype(late_ref.dtype)


def attend(me, sides, kv, ids, ids_row, late, wait=()):
    rows = sides[0].shape[0]
    length = kv.shape[0]
    stacked = (2 * GROUP * rows, length)
    side = shaped((2, rows, SPAN), BF16)
    return call(
        attend_kernel,
        me,
        (*sides, kv, ids, ids_row, *wait),
        [side, side, shaped((length // 2, PAIR), F32), shaped((length // 2, PAIR), late)],
        6,
        scratch=[pltpu.VMEM((2 * rows, length), F32), pltpu.VMEM(stacked, F32)] + [pltpu.VMEM(stacked, BF16)] * 4,
        far=tuple(range(7, 7 + len(wait))),
    )


def by_expert(kind, x):
    return [jnp.where(kind == float(e), x, 0.0).astype(BF16) for e in range(2)]


def hidden_kernel(me_ref, kind_ref, g_ref, gc_ref, w_ref, wc_ref, *refs):
    mine_ref, away_ref = refs[-2:]
    rows = mine_ref.shape[0]
    count, _, depth, _ = w_ref.shape
    masked = []
    for ref in (g_ref, gc_ref):
        sides = []
        for i in range(2):
            here = pl.ds(pl.multiple_of((me_ref[0] ^ (2 * i)) * rows, rows), rows)
            sides.append(by_expert(kind_ref[here, :], ref[here, :].astype(F32)))
        masked += [jnp.concatenate([sides[0][e], sides[1][e]], axis=0) for e in range(2)]
    group = count // 4
    for j in range(4):
        total = 0.0
        for k, ref in enumerate((w_ref, wc_ref)):
            for e in range(2):
                w = ref[j * group : (j + 1) * group, e].reshape(group * depth, PAIR)
                total = total + contract(w, masked[2 * k + e], 1, 1)
        total = total.T
        cols = slice(j * group * depth, (j + 1) * group * depth)
        mine_ref[:, cols] = total[:rows]
        away_ref[:, cols] = total[rows:].astype(BF16)


def hidden_grad(me, kind, grad, grad_c, weight, weight_c, rows):
    count, _, depth, _ = weight.shape
    width = count * depth
    return call(
        hidden_kernel,
        me,
        (kind, grad, grad_c, weight, weight_c),
        [shaped((rows, width), F32), shaped((rows, width), BF16)],
        7,
    )


def share_kernel(steps, depth, split, me_ref, *refs):
    parts, g_ref, outs = refs[:4], refs[4], refs[-(2 if split else 1) * len(steps) :]
    rows, lanes = parts[0].shape[1:]
    quarter = [g_ref[pl.ds(pl.multiple_of((me_ref[0] ^ r) * rows, rows), rows), :].astype(F32) for r in range(4)]
    kind = jnp.concatenate([read_marks(ref[0], depth)[0] for ref in parts], axis=0)
    right = jnp.concatenate(by_expert(kind, jnp.concatenate(quarter, axis=0)), axis=-1)
    for i, by in enumerate(steps):
        owner = owner_at(me_ref[1], by)
        left = jnp.concatenate([ref[owner] for ref in parts], axis=0)
        total = contract(left, right, 0, 0)
        for e in range(2):
            block = total[:depth, e * PAIR : (e + 1) * PAIR]
            if split:
                outs[2 * i + e][0] = block.astype(BF16)
            else:
                outs[i][e] = block


def shares(me, steps, parts, grad, depth, split=False, wait=()):
    if split:
        out = [shaped((1, depth, PAIR), BF16)] * (2 * len(steps))
    else:
        out = [shaped((2, depth, PAIR), F32)] * len(steps)
    far = tuple(range(5, 5 + len(wait)))
    return call(functools.partial(share_kernel, steps, depth, split), me, (*parts, grad, *wait), out, 1 + len(steps), far=far)


def in_order(parts, quarters):
    count, rows, lanes = parts[0].shape
    whole = jnp.stack(parts, axis=1)
    return jnp.take(whole, quarters, axis=1).reshape(count, 4 * rows, lanes)


def project_plain(quarters, parts, weights, depth):
    tokens = in_order(parts, quarters)
    kind, ids = read_marks(tokens[0], depth)
    sums = jnp.einsum("jmk,jekn->emn", tokens[:, :, :depth], weights, preferred_element_type=F32)
    return jnp.where(kind == 1.0, sums[1], sums[0]).astype(BF16), kind, ids, ids.reshape(1, -1)


def weight_plain(quarters, parts, grad, depth):
    tokens = in_order(parts, quarters)
    kind = tokens[0, :, depth : depth + 1].astype(F32)
    sums = [
        jnp.einsum("jmk,mn->jkn", tokens[:, :, :depth], g, preferred_element_type=F32)
        for g in by_expert(kind, grad.astype(F32))
    ]
    return lax.psum_scatter(jnp.stack(sums), "fsdp", scatter_dimension=1)


def per_device(fsdp, seq, tokens, queries, cotangent, modality, block_ids, kv_weight):
    tokens, queries, cotangent = tokens[0], queries[0], cotangent[0]
    me_f = lax.axis_index("fsdp")
    me_s = lax.axis_index("seq")
    rows, width = tokens.shape
    depth = kv_weight.shape[1]
    near_link = fsdp == len(CYCLE)

    def swap(x, bit):
        return lax.ppermute(x, "seq", [(i, i ^ bit) for i in range(seq)])

    def turn(x, by):
        return lax.ppermute(x, "fsdp", [(CYCLE[i], CYCLE[(i + by) % fsdp]) for i in range(fsdp)])

    def both_ways(ups, downs):
        return turn(ups, 1), turn(downs, -1)

    me = jnp.stack([me_s, me_f, me_s])
    me_far = jnp.stack([me_s, me_f, me_s ^ 2])
    quarters = me_s ^ jnp.arange(seq, dtype=jnp.int32)
    if near_link:
        weights = [kv_weight, *both_ways(kv_weight, kv_weight)]
        weights += both_ways(*weights[1:])
        weights += both_ways(*weights[3:])
    else:
        weight = lax.all_gather(kv_weight, "fsdp", axis=0)

    blocks = token_blocks(me, tokens, block_ids * 2 + modality, fsdp)
    across = swap(blocks, 2)
    if near_link:
        across = after(across, weights[3][0, :16, :128])
    parts = [blocks, swap(blocks, 1), across, swap(across, 1)]
    sides = (queries, cotangent, swap(queries, 1), swap(cotangent, 1))

    if near_link:
        before = project(me, STEPS[:5], parts, weights[:5], (), depth)
        weights += both_ways(*halve(me, *weights[5:], (before[0], sides[2][:16, :128], sides[3][:16, :128])))
        before = project(me, STEPS[5:7], parts, weights[5:7], before, depth)
        kv, kind, ids, ids_row, weight = project(me, STEPS[7:], parts, weights[7:], before, depth, True, True)
    else:
        kv, kind, ids, ids_row = project_plain(quarters, parts, weight, depth)
    kv_far = swap(kv, 2)
    far_own, far_other, early, late = attend(me_far, sides, kv_far, ids, ids_row, BF16)
    near_own, near_other, *near = attend(me, sides, kv, ids, ids_row, F32, (early,))
    grad_kv = jnp.concatenate([near[0] + swap(early, 2), near[1] + swap(late, 2).astype(F32)]).astype(BF16)
    attended, grad_queries = place_heads(me, (near_own, swap(near_other, 1), far_own, swap(far_other, 1)))

    grad_c = swap(grad_kv, 1)
    if near_link:
        ups, downs = both_ways(*shares(me, STEPS[7:], parts, grad_kv, depth, True))
    mine, away = hidden_grad(me, kind, grad_kv, grad_c, weight, swap(weight, 1), rows)
    if near_link:
        terms = shares(me, STEPS[5:7], parts, grad_kv, depth, wait=(away,))
        terms += shares(me, STEPS[:5], parts, grad_kv, depth)
        none = jnp.zeros_like(ups)
        ups, downs = jnp.concatenate([ups, none]), jnp.concatenate([none, downs])
        for i in (0, 5, 3):
            down, up = terms[i : i + 2]
            ups, downs = both_ways((up + ups.astype(F32)).astype(BF16), (down + downs.astype(F32)).astype(BF16))
        grad_weight = terms[2] + ups.astype(F32) + downs.astype(F32)
    else:
        grad_weight = weight_plain(quarters, parts, grad_kv, depth)
    grad_tokens = (mine + swap(away, 2).astype(F32)).astype(BF16)
    return attended[None], grad_queries[None], grad_tokens[None], grad_weight


def solution(mesh):
    split = P("fsdp", "seq", None)
    weights = P(None, "fsdp", "seq")
    return jax.shard_map(
        functools.partial(per_device, mesh.shape["fsdp"], mesh.shape["seq"]),
        mesh=mesh,
        in_specs=(split, split, split, P("fsdp", "seq"), P("fsdp", "seq"), weights),
        out_specs=(split, split, split, weights),
        check_vma=False,
    )
```

```python
import functools

import jax
import jax.numpy as jnp
from jax import lax
from jax.experimental import pallas as pl
from jax.experimental.pallas import tpu as pltpu
from jax.sharding import PartitionSpec as P

HEAD_DIM = 128
GROUP = 7
SPAN = GROUP * HEAD_DIM
PAIR = 2 * HEAD_DIM
SCALE = HEAD_DIM ** (-0.5)
LOG2E = 1.4426950408889634
HIDDEN = -1e30
DIGIT = 16
F32 = jnp.float32
BF16 = jnp.bfloat16
ANYWHERE = pl.BlockSpec(memory_space=pl.ANY)
CYCLE = (0, 2, 4, 6, 7, 5, 3, 1)
STEPS = (0, -1, 1, -2, 2, -3, 3, 4)


def contract(a, b, da, db):
    return lax.dot_general(a, b, (((da,), (db,)), ((), ())), preferred_element_type=F32)


def shaped(shape, dtype):
    return jax.ShapeDtypeStruct(shape, dtype)


def call(body, me, operands, out_shape, micros, scratch=(), far=(), far_out=(), aliases=None):
    near = pl.BlockSpec(memory_space=pltpu.VMEM)
    outs = [ANYWHERE if i in far_out else near for i in range(len(out_shape))] if isinstance(out_shape, list) else near
    return pl.pallas_call(
        body,
        in_specs=[pl.BlockSpec(memory_space=pltpu.SMEM)]
        + [ANYWHERE if i in far else near for i in range(len(operands))],
        out_specs=outs,
        out_shape=out_shape,
        scratch_shapes=scratch,
        input_output_aliases=aliases or {},
        compiler_params=pltpu.CompilerParams(vmem_limit_bytes=24 * 1024 * 1024),
        cost_estimate=pl.CostEstimate(flops=0, bytes_accessed=micros * 3000000, transcendentals=0),
    )(me, *operands)


def owner_at(me_f, by):
    size = len(CYCLE)
    half = size // 2
    line, side = lax.div(me_f, 2), lax.rem(me_f, 2)
    spot = jnp.where(side == 1, size - 1 - line, line)
    spot = lax.rem(spot + (size + by), size)
    return jnp.where(spot < half, 2 * spot, 2 * (size - 1 - spot) + 1)


def after(x, *others):
    return pl.pallas_call(
        lambda *refs: None,
        in_specs=[ANYWHERE] + [pl.BlockSpec(memory_space=pltpu.VMEM)] * len(others),
        out_specs=ANYWHERE,
        out_shape=shaped(x.shape, x.dtype),
        input_output_aliases={0: 0},
        cost_estimate=pl.CostEstimate(flops=0, bytes_accessed=0, transcendentals=0),
    )(x, *others)


def as_column(row):
    return jnp.broadcast_to(row, (128, row.shape[1])).T[:, :1]


def blocks_kernel(depth, me_ref, tok_ref, ids_ref, out_ref):
    count, rows, lanes = out_ref.shape
    base = lanes - 128
    lane = lax.broadcasted_iota(jnp.int32, (rows, 128), 1) - (depth - base)
    ids = lax.div(ids_ref[...], 2)
    marks = (lax.rem(ids_ref[...], 2), lax.div(ids, DIGIT), lax.rem(ids, DIGIT))
    marks = [as_column(x.astype(F32)) for x in marks]
    for j in range(count):
        out_ref[j, :, :depth] = tok_ref[:, j * depth : (j + 1) * depth]
        last = out_ref[j, :, base:].astype(F32)
        last = jnp.where(lane >= 0, 0.0, last)
        for i, mark in enumerate(marks):
            last = jnp.where(lane == i, mark, last)
        out_ref[j, :, base:] = last.astype(BF16)


def token_blocks(me, tokens, ids, count):
    rows, width = tokens.shape
    depth = width // count
    lanes = -(-(depth + 3) // 128) * 128
    out = shaped((count, rows, lanes), BF16)
    return call(functools.partial(blocks_kernel, depth), me, (tokens, ids), out, 2)


def read_marks(block, depth):
    mark = [block[:, depth + i : depth + i + 1].astype(F32) for i in range(3)]
    return mark[0], mark[1] * DIGIT + mark[2]


def pack_kernel(me_ref, q_ref, up_ref, own_ref, *other_refs):
    for i in range(4):
        here = pl.ds(pl.multiple_of((me_ref[0] ^ i) * SPAN, SPAN), SPAN)
        for k, ref in enumerate((q_ref, up_ref)):
            if i % 2:
                other_refs[i // 2 * 2 + k][...] = ref[:, here]
            else:
                own_ref[i // 2, k] = ref[:, here]


def pack_heads(me, queries, upstream):
    rows = queries.shape[0]
    out = [shaped((2, 2, rows, SPAN), BF16)] + [shaped((rows, SPAN), BF16)] * 4
    return call(pack_kernel, me, (queries, upstream), out, 2)


def place_kernel(me_ref, *refs):
    att_ref, gq_ref = refs[4:]
    for i, ref in enumerate(refs[:4]):
        here = pl.ds(pl.multiple_of((me_ref[0] ^ i) * SPAN, SPAN), SPAN)
        att_ref[:, here] = ref[0]
        gq_ref[:, here] = ref[1]


def place_heads(me, found):
    out = shaped((found[0].shape[1], 4 * SPAN), BF16)
    return call(place_kernel, me, found, [out, out], 3)


def project_kernel(steps, depth, halves, first, last, me_ref, *refs):
    parts, refs = refs[:4], refs[4:]
    weights, refs = refs[: len(steps) + halves], refs[len(steps) + halves :]
    whole_ref, sems = refs[-2:]
    rows, lanes = parts[0].shape[1:]
    owners = [owner_at(me_ref[1], by) for by in steps]
    copies = []
    for i, ref in enumerate(weights):
        there = whole_ref.at[owners[0], pl.ds(i, 1)] if halves else whole_ref.at[owners[i]]
        copies.append(pltpu.make_async_copy(ref, there, sems.at[i]))
    for copy in copies:
        copy.start()
    sums = [0.0, 0.0]
    for b, owner in enumerate(owners):
        left = jnp.concatenate([ref[owner][:, :depth] for ref in parts], axis=0)
        for e in range(2):
            right = weights[e][0] if halves else weights[b][e]
            sums[e] = sums[e] + contract(left, right, 1, 0)
    if not first:
        sums = [s + refs[0][:, e * PAIR : (e + 1) * PAIR] for e, s in enumerate(sums)]
    if not last:
        for e in range(2):
            refs[-3][:, e * PAIR : (e + 1) * PAIR] = sums[e]
    else:
        kv_ref, kind_ref, ids_ref, ids_row_ref = refs[-6:-2]
        for r in range(4):
            here = pl.ds(pl.multiple_of((me_ref[0] ^ r) * rows, rows), rows)
            kind, ids = read_marks(parts[r][0], depth)
            mine = slice(r * rows, (r + 1) * rows)
            kv_ref[here, :] = jnp.where(kind == 1.0, sums[1][mine], sums[0][mine]).astype(BF16)
            kind_ref[here, :] = kind
            ids_ref[here, :] = ids
        ids_row_ref[...] = jnp.broadcast_to(ids_ref[...], (4 * rows, 128)).T[:1]
    for copy in copies:
        copy.wait()


def project(me, steps, parts, weights, before, depth, last=False, halves=False):
    rows, lanes = parts[0].shape[1:]
    length = 4 * rows
    outs = [shaped((length, 2 * PAIR), F32)]
    if last:
        outs = [shaped((length, PAIR), BF16)] + [shaped(x, F32) for x in ((length, 1), (length, 1), (1, length))]
    outs.append(shaped((len(CYCLE), 2, depth, PAIR), BF16))
    operands = (*parts, *weights, *before)
    count = len(operands)
    return call(
        functools.partial(project_kernel, steps, depth, int(halves), not before, last),
        me,
        operands,
        outs,
        3,
        scratch=[pltpu.SemaphoreType.DMA((len(weights),))],
        far=(count - 1,) if before else (),
        far_out=(len(outs) - 1,),
        aliases={count: len(outs) - 1} if before else None,
    )


def halve_kernel(me_ref, ups_ref, downs_ref, *refs):
    refs[-2][...] = ups_ref[:1]
    refs[-1][...] = downs_ref[1:]


def halve(me, ups, downs, wait):
    out = [shaped((1, *ups.shape[1:]), ups.dtype)] * 2
    return call(halve_kernel, me, (ups, downs, *wait), out, 1, far=tuple(range(2, 2 + len(wait))))


def attend_kernel(spot, me_ref, own_ref, q_other, up_other, kv_ref, ids_ref, ids_row_ref, *refs):
    mine_ref, other_ref, early_ref, late_ref, bias, scores_all, dp_all, pbs, his, los = refs[-10:]
    rows = q_other.shape[0]
    heads = [slice(h * HEAD_DIM, (h + 1) * HEAD_DIM) for h in range(GROUP)]
    for i in range(2):
        here = pl.ds(pl.multiple_of((me_ref[0] ^ i) * rows, rows), rows)
        bias[i * rows : (i + 1) * rows, :] = jnp.where(ids_row_ref[...] <= ids_ref[here, :], 0.0, HIDDEN)
    keys = kv_ref[:, :HEAD_DIM]
    values = kv_ref[:, HEAD_DIM:]
    q, up = [
        jnp.concatenate([own_ref[spot, i, :, cols] for cols in heads] + [ref[:, cols] for cols in heads], axis=0)
        for i, ref in enumerate((q_other, up_other))
    ]
    scores_all[...] = contract(q, keys, 1, 1)
    dp_all[...] = contract(up, values, 1, 1).astype(BF16)
    for h in range(2 * GROUP):
        here = slice(h * rows, (h + 1) * rows)
        side = h // GROUP
        scores = scores_all[here, :] * (SCALE * LOG2E) + bias[side * rows : (side + 1) * rows, :]
        expo = jnp.exp2(scores - jnp.max(scores, axis=-1, keepdims=True))
        probs = expo * (1.0 / jnp.sum(expo, axis=-1, keepdims=True))
        pbs[here, :] = probs.astype(BF16)
        dp = dp_all[here, :].astype(F32)
        ds = probs * (dp - jnp.sum(probs * dp, axis=-1, keepdims=True))
        hi = ds.astype(BF16)
        his[here, :] = hi
        los[here, :] = (ds - hi.astype(F32)).astype(BF16)
    att = contract(pbs[...], values, 1, 0).astype(BF16)
    gq = ((contract(his[...], keys, 1, 0) + contract(los[...], keys, 1, 0)) * SCALE).astype(BF16)
    for i, ref in enumerate((mine_ref, other_ref)):
        for h, cols in enumerate(heads):
            here = slice((i * GROUP + h) * rows, (i * GROUP + h + 1) * rows)
            ref[0, :, cols] = att[here]
            ref[1, :, cols] = gq[here]
    dk = (contract(q, his[...], 0, 0) + contract(q, los[...], 0, 0)) * SCALE
    dv = contract(up, pbs[...], 0, 0)
    half = early_ref.shape[0]
    for i, x in enumerate((dk.T, dv.T)):
        cols = slice(i * HEAD_DIM, (i + 1) * HEAD_DIM)
        early_ref[:, cols] = x[:half]
        late_ref[:, cols] = x[half:].astype(late_ref.dtype)


def attend(spot, me, own, others, kv, ids, ids_row, late, wait=()):
    rows = own.shape[2]
    length = kv.shape[0]
    stacked = (2 * GROUP * rows, length)
    side = shaped((2, rows, SPAN), BF16)
    return call(
        functools.partial(attend_kernel, spot),
        me,
        (own, *others, kv, ids, ids_row, *wait),
        [side, side, shaped((length // 2, PAIR), F32), shaped((length // 2, PAIR), late)],
        6,
        scratch=[pltpu.VMEM((2 * rows, length), F32), pltpu.VMEM(stacked, F32)] + [pltpu.VMEM(stacked, BF16)] * 4,
        far=tuple(range(6, 6 + len(wait))),
    )


def by_expert(kind, x):
    return [jnp.where(kind == float(e), x, 0.0).astype(BF16) for e in range(2)]


def hidden_kernel(me_ref, kind_ref, g_ref, gc_ref, w_ref, wc_ref, *refs):
    mine_ref, away_ref = refs[-2:]
    rows = mine_ref.shape[0]
    count, _, depth, _ = w_ref.shape
    masked = []
    for ref in (g_ref, gc_ref):
        sides = []
        for i in range(2):
            here = pl.ds(pl.multiple_of((me_ref[0] ^ (2 * i)) * rows, rows), rows)
            sides.append(by_expert(kind_ref[here, :], ref[here, :].astype(F32)))
        masked += [jnp.concatenate([sides[0][e], sides[1][e]], axis=0) for e in range(2)]
    group = count // 4
    for j in range(4):
        total = 0.0
        for k, ref in enumerate((w_ref, wc_ref)):
            for e in range(2):
                w = ref[j * group : (j + 1) * group, e].reshape(group * depth, PAIR)
                total = total + contract(w, masked[2 * k + e], 1, 1)
        total = total.T
        cols = slice(j * group * depth, (j + 1) * group * depth)
        mine_ref[:, cols] = total[:rows]
        away_ref[:, cols] = total[rows:].astype(BF16)


def hidden_grad(me, kind, grad, grad_c, weight, weight_c, rows):
    count, _, depth, _ = weight.shape
    width = count * depth
    return call(
        hidden_kernel,
        me,
        (kind, grad, grad_c, weight, weight_c),
        [shaped((rows, width), F32), shaped((rows, width), BF16)],
        7,
    )


def share_kernel(steps, depth, split, me_ref, *refs):
    parts, g_ref, outs = refs[:4], refs[4], refs[-(2 if split else 1) * len(steps) :]
    rows, lanes = parts[0].shape[1:]
    quarter = [g_ref[pl.ds(pl.multiple_of((me_ref[0] ^ r) * rows, rows), rows), :].astype(F32) for r in range(4)]
    kind = jnp.concatenate([read_marks(ref[0], depth)[0] for ref in parts], axis=0)
    right = jnp.concatenate(by_expert(kind, jnp.concatenate(quarter, axis=0)), axis=-1)
    for i, by in enumerate(steps):
        owner = owner_at(me_ref[1], by)
        left = jnp.concatenate([ref[owner] for ref in parts], axis=0)
        total = contract(left, right, 0, 0)
        for e in range(2):
            block = total[:depth, e * PAIR : (e + 1) * PAIR]
            if split:
                outs[2 * i + e][0] = block.astype(BF16)
            else:
                outs[i][e] = block


def shares(me, steps, parts, grad, depth, split=False, wait=()):
    if split:
        out = [shaped((1, depth, PAIR), BF16)] * (2 * len(steps))
    else:
        out = [shaped((2, depth, PAIR), F32)] * len(steps)
    far = tuple(range(5, 5 + len(wait)))
    return call(functools.partial(share_kernel, steps, depth, split), me, (*parts, grad, *wait), out, 1 + len(steps), far=far)


def in_order(parts, quarters):
    count, rows, lanes = parts[0].shape
    whole = jnp.stack(parts, axis=1)
    return jnp.take(whole, quarters, axis=1).reshape(count, 4 * rows, lanes)


def project_plain(quarters, parts, weights, depth):
    tokens = in_order(parts, quarters)
    kind, ids = read_marks(tokens[0], depth)
    sums = jnp.einsum("jmk,jekn->emn", tokens[:, :, :depth], weights, preferred_element_type=F32)
    return jnp.where(kind == 1.0, sums[1], sums[0]).astype(BF16), kind, ids, ids.reshape(1, -1)


def weight_plain(quarters, parts, grad, depth):
    tokens = in_order(parts, quarters)
    kind = tokens[0, :, depth : depth + 1].astype(F32)
    sums = [
        jnp.einsum("jmk,mn->jkn", tokens[:, :, :depth], g, preferred_element_type=F32)
        for g in by_expert(kind, grad.astype(F32))
    ]
    return lax.psum_scatter(jnp.stack(sums), "fsdp", scatter_dimension=1)


def per_device(fsdp, seq, tokens, queries, cotangent, modality, block_ids, kv_weight):
    tokens, queries, cotangent = tokens[0], queries[0], cotangent[0]
    me_f = lax.axis_index("fsdp")
    me_s = lax.axis_index("seq")
    rows, width = tokens.shape
    depth = kv_weight.shape[1]
    near_link = fsdp == len(CYCLE)

    def swap(x, bit):
        return lax.ppermute(x, "seq", [(i, i ^ bit) for i in range(seq)])

    def turn(x, by):
        return lax.ppermute(x, "fsdp", [(CYCLE[i], CYCLE[(i + by) % fsdp]) for i in range(fsdp)])

    def both_ways(ups, downs):
        return turn(ups, 1), turn(downs, -1)

    me = jnp.stack([me_s, me_f])
    quarters = me_s ^ jnp.arange(seq, dtype=jnp.int32)
    if near_link:
        weights = [kv_weight, *both_ways(kv_weight, kv_weight)]
        weights += both_ways(*weights[1:])
        weights += both_ways(*weights[3:])
    else:
        weight = lax.all_gather(kv_weight, "fsdp", axis=0)

    blocks = token_blocks(me, tokens, block_ids * 2 + modality, fsdp)
    across = swap(blocks, 2)
    own, *others = pack_heads(me, queries, cotangent)
    others = [swap(x, 1) for x in others]
    if near_link:
        across = after(across, weights[3], weights[4], *others)
    parts = [blocks, swap(blocks, 1), across, swap(across, 1)]

    if near_link:
        before = project(me, STEPS[:5], parts, weights[:5], (), depth)
        weights += both_ways(*halve(me, *weights[5:], (before[0],)))
        before = project(me, STEPS[5:7], parts, weights[5:7], before, depth)
        kv, kind, ids, ids_row, weight = project(me, STEPS[7:], parts, weights[7:], before, depth, True, True)
    else:
        kv, kind, ids, ids_row = project_plain(quarters, parts, weight, depth)
    kv_far = swap(kv, 2)
    far_own, far_other, early, late = attend(1, me, own, others[2:], kv_far, ids, ids_row, BF16)
    near_own, near_other, *near = attend(0, me, own, others[:2], kv, ids, ids_row, F32, (early,))
    grad_kv = jnp.concatenate([near[0] + swap(early, 2), near[1] + swap(late, 2).astype(F32)]).astype(BF16)
    attended, grad_queries = place_heads(me, (near_own, swap(near_other, 1), far_own, swap(far_other, 1)))

    grad_c = swap(grad_kv, 1)
    if near_link:
        ups, downs = both_ways(*shares(me, STEPS[7:], parts, grad_kv, depth, True))
    mine, away = hidden_grad(me, kind, grad_kv, grad_c, weight, swap(weight, 1), rows)
    if near_link:
        terms = shares(me, STEPS[5:7], parts, grad_kv, depth, wait=(away,))
        terms += shares(me, STEPS[:5], parts, grad_kv, depth)
        none = jnp.zeros_like(ups)
        ups, downs = jnp.concatenate([ups, none]), jnp.concatenate([none, downs])
        for i in (0, 5, 3):
            down, up = terms[i : i + 2]
            ups, downs = both_ways((up + ups.astype(F32)).astype(BF16), (down + downs.astype(F32)).astype(BF16))
        grad_weight = terms[2] + ups.astype(F32) + downs.astype(F32)
    else:
        grad_weight = weight_plain(quarters, parts, grad_kv, depth)
    grad_tokens = (mine + swap(away, 2).astype(F32)).astype(BF16)
    return attended[None], grad_queries[None], grad_tokens[None], grad_weight


def solution(mesh):
    split = P("fsdp", "seq", None)
    weights = P(None, "fsdp", "seq")
    return jax.shard_map(
        functools.partial(per_device, mesh.shape["fsdp"], mesh.shape["seq"]),
        mesh=mesh,
        in_specs=(split, split, split, P("fsdp", "seq"), P("fsdp", "seq"), weights),
        out_specs=(split, split, split, weights),
        check_vma=False,
    )
```

```python
import functools

import jax
import jax.numpy as jnp
from jax import lax
from jax.experimental import pallas as pl
from jax.experimental.pallas import tpu as pltpu
from jax.sharding import PartitionSpec as P

HEAD_DIM = 128
GROUP = 7
SPAN = GROUP * HEAD_DIM
PAIR = 2 * HEAD_DIM
SCALE = HEAD_DIM ** (-0.5)
LOG2E = 1.4426950408889634
HIDDEN = -1e30
DIGIT = 16
F32 = jnp.float32
BF16 = jnp.bfloat16
ANYWHERE = pl.BlockSpec(memory_space=pl.ANY)
CYCLE = (0, 2, 4, 6, 7, 5, 3, 1)
STEPS = (0, -1, 1, -2, 2, -3, 3, 4)


def contract(a, b, da, db):
    return lax.dot_general(a, b, (((da,), (db,)), ((), ())), preferred_element_type=F32)


def shaped(shape, dtype):
    return jax.ShapeDtypeStruct(shape, dtype)


def call(body, me, operands, out_shape, micros, scratch=(), far=(), far_out=(), aliases=None):
    near = pl.BlockSpec(memory_space=pltpu.VMEM)
    outs = [ANYWHERE if i in far_out else near for i in range(len(out_shape))] if isinstance(out_shape, list) else near
    return pl.pallas_call(
        body,
        in_specs=[pl.BlockSpec(memory_space=pltpu.SMEM)]
        + [ANYWHERE if i in far else near for i in range(len(operands))],
        out_specs=outs,
        out_shape=out_shape,
        scratch_shapes=scratch,
        input_output_aliases=aliases or {},
        compiler_params=pltpu.CompilerParams(vmem_limit_bytes=24 * 1024 * 1024),
        cost_estimate=pl.CostEstimate(flops=0, bytes_accessed=micros * 3000000, transcendentals=0),
    )(me, *operands)


def owner_at(me_f, by):
    size = len(CYCLE)
    half = size // 2
    line, side = lax.div(me_f, 2), lax.rem(me_f, 2)
    spot = jnp.where(side == 1, size - 1 - line, line)
    spot = lax.rem(spot + (size + by), size)
    return jnp.where(spot < half, 2 * spot, 2 * (size - 1 - spot) + 1)


def after(x, *others):
    return pl.pallas_call(
        lambda *refs: None,
        in_specs=[ANYWHERE] + [pl.BlockSpec(memory_space=pltpu.VMEM)] * len(others),
        out_specs=ANYWHERE,
        out_shape=shaped(x.shape, x.dtype),
        input_output_aliases={0: 0},
        cost_estimate=pl.CostEstimate(flops=0, bytes_accessed=0, transcendentals=0),
    )(x, *others)


def as_column(row):
    return jnp.broadcast_to(row, (128, row.shape[1])).T[:, :1]


def blocks_kernel(depth, me_ref, tok_ref, ids_ref, out_ref):
    count, rows, lanes = out_ref.shape
    base = lanes - 128
    lane = lax.broadcasted_iota(jnp.int32, (rows, 128), 1) - (depth - base)
    ids = lax.div(ids_ref[...], 2)
    marks = (lax.rem(ids_ref[...], 2), lax.div(ids, DIGIT), lax.rem(ids, DIGIT))
    marks = [as_column(x.astype(F32)) for x in marks]
    for j in range(count):
        out_ref[j, :, :depth] = tok_ref[:, j * depth : (j + 1) * depth]
        last = out_ref[j, :, base:].astype(F32)
        last = jnp.where(lane >= 0, 0.0, last)
        for i, mark in enumerate(marks):
            last = jnp.where(lane == i, mark, last)
        out_ref[j, :, base:] = last.astype(BF16)


def token_blocks(me, tokens, ids, count):
    rows, width = tokens.shape
    depth = width // count
    lanes = -(-(depth + 3) // 128) * 128
    out = shaped((count, rows, lanes), BF16)
    return call(functools.partial(blocks_kernel, depth), me, (tokens, ids), out, 2)


def read_marks(block, depth):
    mark = [block[:, depth + i : depth + i + 1].astype(F32) for i in range(3)]
    return mark[0], mark[1] * DIGIT + mark[2]


def pack_kernel(me_ref, q_ref, up_ref, *refs):
    own_ref, other_refs = refs[-5], refs[-4:]
    for i in range(4):
        here = pl.ds(pl.multiple_of((me_ref[0] ^ i) * SPAN, SPAN), SPAN)
        for k, ref in enumerate((q_ref, up_ref)):
            if i % 2:
                other_refs[i // 2 * 2 + k][...] = ref[:, here]
            else:
                own_ref[i // 2, k] = ref[:, here]


def pack_heads(me, queries, upstream, wait):
    rows = queries.shape[0]
    out = [shaped((2, 2, rows, SPAN), BF16)] + [shaped((rows, SPAN), BF16)] * 4
    return call(pack_kernel, me, (queries, upstream, *wait), out, 2)


def place_kernel(me_ref, *refs):
    att_ref, gq_ref = refs[4:]
    for i, ref in enumerate(refs[:4]):
        here = pl.ds(pl.multiple_of((me_ref[0] ^ i) * SPAN, SPAN), SPAN)
        att_ref[:, here] = ref[0]
        gq_ref[:, here] = ref[1]


def place_heads(me, found):
    out = shaped((found[0].shape[1], 4 * SPAN), BF16)
    return call(place_kernel, me, found, [out, out], 3)


def project_kernel(steps, depth, first, last, me_ref, *refs):
    parts, refs = refs[:4], refs[4:]
    weights, refs = refs[: 2 * len(steps)], refs[2 * len(steps) :]
    whole_ref, sems = refs[-2:]
    rows, lanes = parts[0].shape[1:]
    owners = [owner_at(me_ref[1], by) for by in steps]
    copies = [
        pltpu.make_async_copy(ref, whole_ref.at[owners[i // 2], i % 2], sems.at[i]) for i, ref in enumerate(weights)
    ]
    for copy in copies:
        copy.start()
    sums = [0.0, 0.0]
    for b, owner in enumerate(owners):
        left = jnp.concatenate([ref[owner][:, :depth] for ref in parts], axis=0)
        for e in range(2):
            sums[e] = sums[e] + contract(left, weights[2 * b + e][...], 1, 0)
    if not first:
        sums = [s + refs[0][:, e * PAIR : (e + 1) * PAIR] for e, s in enumerate(sums)]
    if not last:
        for e in range(2):
            refs[-3][:, e * PAIR : (e + 1) * PAIR] = sums[e]
    else:
        kv_ref, kind_ref, ids_ref, ids_row_ref = refs[-6:-2]
        for r in range(4):
            here = pl.ds(pl.multiple_of((me_ref[0] ^ r) * rows, rows), rows)
            kind, ids = read_marks(parts[r][0], depth)
            mine = slice(r * rows, (r + 1) * rows)
            kv_ref[here, :] = jnp.where(kind == 1.0, sums[1][mine], sums[0][mine]).astype(BF16)
            kind_ref[here, :] = kind
            ids_ref[here, :] = ids
        ids_row_ref[...] = jnp.broadcast_to(ids_ref[...], (4 * rows, 128)).T[:1]
    for copy in copies:
        copy.wait()


def project(me, steps, parts, weights, before, depth, last=False):
    rows, lanes = parts[0].shape[1:]
    length = 4 * rows
    outs = [shaped((length, 2 * PAIR), F32)]
    if last:
        outs = [shaped((length, PAIR), BF16)] + [shaped(x, F32) for x in ((length, 1), (length, 1), (1, length))]
    outs.append(shaped((len(CYCLE), 2, depth, PAIR), BF16))
    operands = (*parts, *weights, *before)
    count = len(operands)
    return call(
        functools.partial(project_kernel, steps, depth, not before, last),
        me,
        operands,
        outs,
        3,
        scratch=[pltpu.SemaphoreType.DMA((len(weights),))],
        far=(count - 1,) if before else (),
        far_out=(len(outs) - 1,),
        aliases={count: len(outs) - 1} if before else None,
    )


def hold_kernel(count, me_ref, *refs):
    for i in range(count):
        refs[i - count][...] = refs[i][...]


def hold(me, arrays, wait):
    out = [shaped(x.shape, x.dtype) for x in arrays]
    far = tuple(range(len(arrays), len(arrays) + len(wait)))
    return call(functools.partial(hold_kernel, len(arrays)), me, (*arrays, *wait), out, 1, far=far)


def finish_kernel(me_ref, *refs):
    for e in range(2):
        own, ups, downs = refs[3 * e : 3 * e + 3]
        refs[-1][e] = own[...] + ups[...].astype(F32) + downs[...].astype(F32)


def finish(me, terms):
    return call(finish_kernel, me, terms, shaped((2, *terms[0].shape), F32), 1)


def attend_kernel(spot, me_ref, own_ref, q_other, up_other, kv_ref, ids_ref, ids_row_ref, *refs):
    mine_ref, other_ref, early_ref, late_ref, bias, scores_all, dp_all, pbs, his, los = refs[-10:]
    rows = q_other.shape[0]
    heads = [slice(h * HEAD_DIM, (h + 1) * HEAD_DIM) for h in range(GROUP)]
    for i in range(2):
        here = pl.ds(pl.multiple_of((me_ref[0] ^ i) * rows, rows), rows)
        bias[i * rows : (i + 1) * rows, :] = jnp.where(ids_row_ref[...] <= ids_ref[here, :], 0.0, HIDDEN)
    keys = kv_ref[:, :HEAD_DIM]
    values = kv_ref[:, HEAD_DIM:]
    q, up = [
        jnp.concatenate([own_ref[spot, i, :, cols] for cols in heads] + [ref[:, cols] for cols in heads], axis=0)
        for i, ref in enumerate((q_other, up_other))
    ]
    scores_all[...] = contract(q, keys, 1, 1)
    dp_all[...] = contract(up, values, 1, 1).astype(BF16)
    for h in range(2 * GROUP):
        here = slice(h * rows, (h + 1) * rows)
        side = h // GROUP
        scores = scores_all[here, :] * (SCALE * LOG2E) + bias[side * rows : (side + 1) * rows, :]
        expo = jnp.exp2(scores - jnp.max(scores, axis=-1, keepdims=True))
        probs = expo * (1.0 / jnp.sum(expo, axis=-1, keepdims=True))
        pbs[here, :] = probs.astype(BF16)
        dp = dp_all[here, :].astype(F32)
        ds = probs * (dp - jnp.sum(probs * dp, axis=-1, keepdims=True))
        hi = ds.astype(BF16)
        his[here, :] = hi
        los[here, :] = (ds - hi.astype(F32)).astype(BF16)
    att = contract(pbs[...], values, 1, 0).astype(BF16)
    gq = ((contract(his[...], keys, 1, 0) + contract(los[...], keys, 1, 0)) * SCALE).astype(BF16)
    for i, ref in enumerate((mine_ref, other_ref)):
        for h, cols in enumerate(heads):
            here = slice((i * GROUP + h) * rows, (i * GROUP + h + 1) * rows)
            ref[0, :, cols] = att[here]
            ref[1, :, cols] = gq[here]
    dk = (contract(q, his[...], 0, 0) + contract(q, los[...], 0, 0)) * SCALE
    dv = contract(up, pbs[...], 0, 0)
    half = early_ref.shape[0]
    for i, x in enumerate((dk.T, dv.T)):
        cols = slice(i * HEAD_DIM, (i + 1) * HEAD_DIM)
        early_ref[:, cols] = x[:half]
        late_ref[:, cols] = x[half:].astype(late_ref.dtype)


def attend(spot, me, own, others, kv, ids, ids_row, late, wait=()):
    rows = own.shape[2]
    length = kv.shape[0]
    stacked = (2 * GROUP * rows, length)
    side = shaped((2, rows, SPAN), BF16)
    return call(
        functools.partial(attend_kernel, spot),
        me,
        (own, *others, kv, ids, ids_row, *wait),
        [side, side, shaped((length // 2, PAIR), F32), shaped((length // 2, PAIR), late)],
        6,
        scratch=[pltpu.VMEM((2 * rows, length), F32), pltpu.VMEM(stacked, F32)] + [pltpu.VMEM(stacked, BF16)] * 4,
        far=tuple(range(6, 6 + len(wait))),
    )


def by_expert(kind, x):
    return [jnp.where(kind == float(e), x, 0.0).astype(BF16) for e in range(2)]


def hidden_kernel(me_ref, kind_ref, g_ref, gc_ref, w_ref, wc_ref, *refs):
    mine_ref, away_ref = refs[-2:]
    rows = mine_ref.shape[0]
    count, _, depth, _ = w_ref.shape
    masked = []
    for ref in (g_ref, gc_ref):
        sides = []
        for i in range(2):
            here = pl.ds(pl.multiple_of((me_ref[0] ^ (2 * i)) * rows, rows), rows)
            sides.append(by_expert(kind_ref[here, :], ref[here, :].astype(F32)))
        masked += [jnp.concatenate([sides[0][e], sides[1][e]], axis=0) for e in range(2)]
    group = count // 4
    for j in range(4):
        total = 0.0
        for k, ref in enumerate((w_ref, wc_ref)):
            for e in range(2):
                w = ref[j * group : (j + 1) * group, e].reshape(group * depth, PAIR)
                total = total + contract(w, masked[2 * k + e], 1, 1)
        total = total.T
        cols = slice(j * group * depth, (j + 1) * group * depth)
        mine_ref[:, cols] = total[:rows]
        away_ref[:, cols] = total[rows:].astype(BF16)


def hidden_grad(me, kind, grad, grad_c, weight, weight_c, rows):
    count, _, depth, _ = weight.shape
    width = count * depth
    return call(
        hidden_kernel,
        me,
        (kind, grad, grad_c, weight, weight_c),
        [shaped((rows, width), F32), shaped((rows, width), BF16)],
        7,
    )


def share_kernel(steps, depth, me_ref, *refs):
    parts, g_ref, outs = refs[:4], refs[4], refs[-2 * len(steps) :]
    rows, lanes = parts[0].shape[1:]
    quarter = [g_ref[pl.ds(pl.multiple_of((me_ref[0] ^ r) * rows, rows), rows), :].astype(F32) for r in range(4)]
    kind = jnp.concatenate([read_marks(ref[0], depth)[0] for ref in parts], axis=0)
    right = jnp.concatenate(by_expert(kind, jnp.concatenate(quarter, axis=0)), axis=-1)
    for i, by in enumerate(steps):
        owner = owner_at(me_ref[1], by)
        left = jnp.concatenate([ref[owner] for ref in parts], axis=0)
        total = contract(left, right, 0, 0)
        for e in range(2):
            ref = outs[2 * i + e]
            ref[...] = total[:depth, e * PAIR : (e + 1) * PAIR].astype(ref.dtype)


def shares(me, steps, parts, grad, depth, dtype=F32, wait=()):
    out = [shaped((depth, PAIR), dtype)] * (2 * len(steps))
    far = tuple(range(5, 5 + len(wait)))
    return call(functools.partial(share_kernel, steps, depth), me, (*parts, grad, *wait), out, 1 + len(steps), far=far)


def in_order(parts, quarters):
    count, rows, lanes = parts[0].shape
    whole = jnp.stack(parts, axis=1)
    return jnp.take(whole, quarters, axis=1).reshape(count, 4 * rows, lanes)


def project_plain(quarters, parts, weights, depth):
    tokens = in_order(parts, quarters)
    kind, ids = read_marks(tokens[0], depth)
    sums = jnp.einsum("jmk,jekn->emn", tokens[:, :, :depth], weights, preferred_element_type=F32)
    return jnp.where(kind == 1.0, sums[1], sums[0]).astype(BF16), kind, ids, ids.reshape(1, -1)


def weight_plain(quarters, parts, grad, depth):
    tokens = in_order(parts, quarters)
    kind = tokens[0, :, depth : depth + 1].astype(F32)
    sums = [
        jnp.einsum("jmk,mn->jkn", tokens[:, :, :depth], g, preferred_element_type=F32)
        for g in by_expert(kind, grad.astype(F32))
    ]
    return lax.psum_scatter(jnp.stack(sums), "fsdp", scatter_dimension=1)


def per_device(fsdp, seq, tokens, queries, cotangent, modality, block_ids, kv_weight):
    tokens, queries, cotangent = tokens[0], queries[0], cotangent[0]
    me_f = lax.axis_index("fsdp")
    me_s = lax.axis_index("seq")
    rows, width = tokens.shape
    depth = kv_weight.shape[1]
    near_link = fsdp == len(CYCLE)

    def swap(x, bit):
        return lax.ppermute(x, "seq", [(i, i ^ bit) for i in range(seq)])

    def turn(x, by):
        return lax.ppermute(x, "fsdp", [(CYCLE[i], CYCLE[(i + by) % fsdp]) for i in range(fsdp)])

    me = jnp.stack([me_s, me_f])
    quarters = me_s ^ jnp.arange(seq, dtype=jnp.int32)
    if near_link:
        pair = [kv_weight[0], kv_weight[1]]
        ups, downs = [pair], [pair]
        for _ in range(3):
            ups.append([turn(x, 1) for x in ups[-1]])
            downs.append([turn(x, -1) for x in downs[-1]])
    else:
        weight = lax.all_gather(kv_weight, "fsdp", axis=0)

    blocks = token_blocks(me, tokens, block_ids * 2 + modality, fsdp)
    across = swap(blocks, 2)
    own, *others = pack_heads(me, queries, cotangent, ups[1][:1] if near_link else ())
    others = [swap(x, 1) for x in others]
    if near_link:
        across = after(across, *ups[2], *downs[2], *others)
    parts = [blocks, swap(blocks, 1), across, swap(across, 1)]

    if near_link:
        before = project(me, STEPS[:5], parts, pair + ups[1] + downs[1] + ups[2] + downs[2], (), depth)
        last = hold(me, (ups[3][0], downs[3][1]), before[:1])
        last = [turn(last[0], 1), turn(last[1], -1)]
        before = project(me, STEPS[5:7], parts, ups[3] + downs[3], before, depth)
        kv, kind, ids, ids_row, weight = project(me, STEPS[7:], parts, last, before, depth, True)
    else:
        kv, kind, ids, ids_row = project_plain(quarters, parts, weight, depth)
    kv_far = swap(kv, 2)
    far_own, far_other, early, late = attend(1, me, own, others[2:], kv_far, ids, ids_row, BF16)
    near_own, near_other, *near = attend(0, me, own, others[:2], kv, ids, ids_row, F32, (early,))
    grad_kv = jnp.concatenate([near[0] + swap(early, 2), near[1] + swap(late, 2).astype(F32)]).astype(BF16)
    attended, grad_queries = place_heads(me, (near_own, swap(near_other, 1), far_own, swap(far_other, 1)))

    grad_c = swap(grad_kv, 1)
    if near_link:
        first = shares(me, STEPS[7:], parts, grad_kv, depth, BF16)
        ups, downs = [turn(first[0], 1), None], [None, turn(first[1], -1)]
    mine, away = hidden_grad(me, kind, grad_kv, grad_c, weight, swap(weight, 1), rows)
    if near_link:
        terms = shares(me, STEPS[5:7], parts, grad_kv, depth, wait=(away,))
        terms += shares(me, STEPS[:5], parts, grad_kv, depth)

        def added(term, x):
            return (term if x is None else term + x.astype(F32)).astype(BF16)

        for i in (0, 10, 6):
            down, up = terms[i : i + 2], terms[i + 2 : i + 4]
            ups = [turn(added(up[e], ups[e]), 1) for e in range(2)]
            downs = [turn(added(down[e], downs[e]), -1) for e in range(2)]
        grad_weight = finish(me, (terms[4], ups[0], downs[0], terms[5], ups[1], downs[1]))
    else:
        grad_weight = weight_plain(quarters, parts, grad_kv, depth)
    grad_tokens = (mine + swap(away, 2).astype(F32)).astype(BF16)
    return attended[None], grad_queries[None], grad_tokens[None], grad_weight


def solution(mesh):
    split = P("fsdp", "seq", None)
    weights = P(None, "fsdp", "seq")
    return jax.shard_map(
        functools.partial(per_device, mesh.shape["fsdp"], mesh.shape["seq"]),
        mesh=mesh,
        in_specs=(split, split, split, P("fsdp", "seq"), P("fsdp", "seq"), weights),
        out_specs=(split, split, split, weights),
        check_vma=False,
    )
```

```python
import functools

import jax
import jax.numpy as jnp
from jax import lax
from jax.experimental import pallas as pl
from jax.experimental.pallas import tpu as pltpu
from jax.sharding import PartitionSpec as P

HEAD_DIM = 128
GROUP = 7
SPAN = GROUP * HEAD_DIM
PAIR = 2 * HEAD_DIM
SCALE = HEAD_DIM ** (-0.5)
LOG2E = 1.4426950408889634
HIDDEN = -1e30
DIGIT = 16
F32 = jnp.float32
BF16 = jnp.bfloat16
ANYWHERE = pl.BlockSpec(memory_space=pl.ANY)
CYCLE = (0, 2, 4, 6, 7, 5, 3, 1)
STEPS = (0, -1, 1, -2, 2, -3, 3, 4)


def contract(a, b, da, db):
    return lax.dot_general(a, b, (((da,), (db,)), ((), ())), preferred_element_type=F32)


def shaped(shape, dtype):
    return jax.ShapeDtypeStruct(shape, dtype)


def call(body, me, operands, out_shape, micros, scratch=(), far=(), far_out=(), aliases=None):
    near = pl.BlockSpec(memory_space=pltpu.VMEM)
    outs = [ANYWHERE if i in far_out else near for i in range(len(out_shape))] if isinstance(out_shape, list) else near
    return pl.pallas_call(
        body,
        in_specs=[pl.BlockSpec(memory_space=pltpu.SMEM)]
        + [ANYWHERE if i in far else near for i in range(len(operands))],
        out_specs=outs,
        out_shape=out_shape,
        scratch_shapes=scratch,
        input_output_aliases=aliases or {},
        compiler_params=pltpu.CompilerParams(vmem_limit_bytes=24 * 1024 * 1024),
        cost_estimate=pl.CostEstimate(flops=0, bytes_accessed=micros * 3000000, transcendentals=0),
    )(me, *operands)


def owner_at(me_f, by):
    size = len(CYCLE)
    half = size // 2
    line, side = lax.div(me_f, 2), lax.rem(me_f, 2)
    spot = jnp.where(side == 1, size - 1 - line, line)
    spot = lax.rem(spot + (size + by), size)
    return jnp.where(spot < half, 2 * spot, 2 * (size - 1 - spot) + 1)


def as_column(row):
    return jnp.broadcast_to(row, (128, row.shape[1])).T[:, :1]


def blocks_kernel(depth, me_ref, tok_ref, ids_ref, *out_refs):
    count, rows, lanes = out_refs[0].shape
    base = lanes - 128
    lane = lax.broadcasted_iota(jnp.int32, (rows, 128), 1) - (depth - base)
    ids = lax.div(ids_ref[...], 2)
    marks = (lax.rem(ids_ref[...], 2), lax.div(ids, DIGIT), lax.rem(ids, DIGIT))
    marks = [as_column(x.astype(F32)) for x in marks]
    for h, out_ref in enumerate(out_refs):
        here = slice(h * rows, (h + 1) * rows)
        for j in range(count):
            out_ref[j, :, :depth] = tok_ref[here, j * depth : (j + 1) * depth]
            last = out_ref[j, :, base:].astype(F32)
            last = jnp.where(lane >= 0, 0.0, last)
            for i, mark in enumerate(marks):
                last = jnp.where(lane == i, mark[here], last)
            out_ref[j, :, base:] = last.astype(BF16)


def token_blocks(me, tokens, ids, count):
    rows, width = tokens.shape
    depth = width // count
    lanes = -(-(depth + 3) // 128) * 128
    out = [shaped((count, rows // 2, lanes), BF16)] * 2
    return call(functools.partial(blocks_kernel, depth), me, (tokens, ids), out, 1)


def piece_start(me, i, rows):
    return pl.multiple_of((me ^ (i // 2)) * (2 * rows) + i % 2 * rows, rows)


def read_marks(block, depth):
    mark = [block[:, depth + i : depth + i + 1].astype(F32) for i in range(3)]
    return mark[0], mark[1] * DIGIT + mark[2]


def pack_kernel(me_ref, q_ref, up_ref, *refs):
    own_ref, other_refs = refs[-5], refs[-4:]
    for i in range(4):
        here = pl.ds(pl.multiple_of((me_ref[0] ^ i) * SPAN, SPAN), SPAN)
        for k, ref in enumerate((q_ref, up_ref)):
            if i % 2:
                other_refs[i // 2 * 2 + k][...] = ref[:, here]
            else:
                own_ref[i // 2, k] = ref[:, here]


def pack_heads(me, queries, upstream, wait):
    rows = queries.shape[0]
    out = [shaped((2, 2, rows, SPAN), BF16)] + [shaped((rows, SPAN), BF16)] * 4
    return call(pack_kernel, me, (queries, upstream, *wait), out, 2)


def place_kernel(me_ref, *refs):
    att_ref, gq_ref = refs[4:]
    for i, ref in enumerate(refs[:4]):
        here = pl.ds(pl.multiple_of((me_ref[0] ^ i) * SPAN, SPAN), SPAN)
        att_ref[:, here] = ref[0]
        gq_ref[:, here] = ref[1]


def place_heads(me, found):
    out = shaped((found[0].shape[1], 4 * SPAN), BF16)
    return call(place_kernel, me, found, [out, out], 3)


def project_kernel(steps, depth, halves, first, last, me_ref, *refs):
    parts, refs = refs[:8], refs[8:]
    weights, refs = refs[: len(steps) + halves], refs[len(steps) + halves :]
    whole_ref, sems = refs[-2:]
    rows, lanes = parts[0].shape[1:]
    owners = [owner_at(me_ref[1], by) for by in steps]
    copies = []
    for i, ref in enumerate(weights):
        there = whole_ref.at[owners[0], pl.ds(i, 1)] if halves else whole_ref.at[owners[i]]
        copies.append(pltpu.make_async_copy(ref, there, sems.at[i]))
    for copy in copies:
        copy.start()
    sums = [0.0, 0.0]
    for b, owner in enumerate(owners):
        left = jnp.concatenate([ref[owner][:, :depth] for ref in parts], axis=0)
        for e in range(2):
            right = weights[e][0] if halves else weights[b][e]
            sums[e] = sums[e] + contract(left, right, 1, 0)
    if not first:
        sums = [s + refs[0][:, e * PAIR : (e + 1) * PAIR] for e, s in enumerate(sums)]
    if not last:
        for e in range(2):
            refs[-3][:, e * PAIR : (e + 1) * PAIR] = sums[e]
    else:
        kv_ref, kind_ref, ids_ref, ids_row_ref = refs[-6:-2]
        for i, ref in enumerate(parts):
            here = pl.ds(piece_start(me_ref[0], i, rows), rows)
            kind, ids = read_marks(ref[0], depth)
            mine = slice(i * rows, (i + 1) * rows)
            kv_ref[here, :] = jnp.where(kind == 1.0, sums[1][mine], sums[0][mine]).astype(BF16)
            kind_ref[here, :] = kind
            ids_ref[here, :] = ids
        ids_row_ref[...] = jnp.broadcast_to(ids_ref[...], (8 * rows, 128)).T[:1]
    for copy in copies:
        copy.wait()


def project(me, steps, parts, weights, before, depth, last=False, halves=False):
    length = 8 * parts[0].shape[1]
    outs = [shaped((length, 2 * PAIR), F32)]
    if last:
        outs = [shaped((length, PAIR), BF16)] + [shaped(x, F32) for x in ((length, 1), (length, 1), (1, length))]
    outs.append(shaped((len(CYCLE), 2, depth, PAIR), BF16))
    operands = (*parts, *weights, *before)
    count = len(operands)
    return call(
        functools.partial(project_kernel, steps, depth, int(halves), not before, last),
        me,
        operands,
        outs,
        3,
        scratch=[pltpu.SemaphoreType.DMA((len(weights),))],
        far=(count - 1,) if before else (),
        far_out=(len(outs) - 1,),
        aliases={count: len(outs) - 1} if before else None,
    )


def halve_kernel(me_ref, ups_ref, downs_ref, *refs):
    refs[-2][...] = ups_ref[:1]
    refs[-1][...] = downs_ref[1:]


def halve(me, ups, downs, near, wait):
    out = [shaped((1, *ups.shape[1:]), ups.dtype)] * 2
    first = 2 + len(near)
    return call(halve_kernel, me, (ups, downs, *near, *wait), out, 1, far=tuple(range(first, first + len(wait))))


def attend_kernel(spot, me_ref, own_ref, q_other, up_other, kv_ref, ids_ref, ids_row_ref, *refs):
    mine_ref, other_ref, early_ref, late_ref, bias, scores_all, dp_all, pbs, his, los = refs[-10:]
    rows = q_other.shape[0]
    heads = [slice(h * HEAD_DIM, (h + 1) * HEAD_DIM) for h in range(GROUP)]
    for i in range(2):
        here = pl.ds(pl.multiple_of((me_ref[0] ^ i) * rows, rows), rows)
        bias[i * rows : (i + 1) * rows, :] = jnp.where(ids_row_ref[...] <= ids_ref[here, :], 0.0, HIDDEN)
    keys = kv_ref[:, :HEAD_DIM]
    values = kv_ref[:, HEAD_DIM:]
    q, up = [
        jnp.concatenate([own_ref[spot, i, :, cols] for cols in heads] + [ref[:, cols] for cols in heads], axis=0)
        for i, ref in enumerate((q_other, up_other))
    ]
    scores_all[...] = contract(q, keys, 1, 1)
    dp_all[...] = contract(up, values, 1, 1).astype(BF16)
    for h in range(2 * GROUP):
        here = slice(h * rows, (h + 1) * rows)
        side = h // GROUP
        scores = scores_all[here, :] * (SCALE * LOG2E) + bias[side * rows : (side + 1) * rows, :]
        expo = jnp.exp2(scores - jnp.max(scores, axis=-1, keepdims=True))
        probs = expo * (1.0 / jnp.sum(expo, axis=-1, keepdims=True))
        pbs[here, :] = probs.astype(BF16)
        dp = dp_all[here, :].astype(F32)
        ds = probs * (dp - jnp.sum(probs * dp, axis=-1, keepdims=True))
        hi = ds.astype(BF16)
        his[here, :] = hi
        los[here, :] = (ds - hi.astype(F32)).astype(BF16)
    att = contract(pbs[...], values, 1, 0).astype(BF16)
    gq = ((contract(his[...], keys, 1, 0) + contract(los[...], keys, 1, 0)) * SCALE).astype(BF16)
    for i, ref in enumerate((mine_ref, other_ref)):
        for h, cols in enumerate(heads):
            here = slice((i * GROUP + h) * rows, (i * GROUP + h + 1) * rows)
            ref[0, :, cols] = att[here]
            ref[1, :, cols] = gq[here]
    dk = (contract(q, his[...], 0, 0) + contract(q, los[...], 0, 0)) * SCALE
    dv = contract(up, pbs[...], 0, 0)
    half = early_ref.shape[0]
    for i, x in enumerate((dk.T, dv.T)):
        cols = slice(i * HEAD_DIM, (i + 1) * HEAD_DIM)
        early_ref[:, cols] = x[:half]
        late_ref[:, cols] = x[half:].astype(late_ref.dtype)


def attend(spot, me, own, others, kv, ids, ids_row, late, wait=()):
    rows = own.shape[2]
    length = kv.shape[0]
    stacked = (2 * GROUP * rows, length)
    side = shaped((2, rows, SPAN), BF16)
    return call(
        functools.partial(attend_kernel, spot),
        me,
        (own, *others, kv, ids, ids_row, *wait),
        [side, side, shaped((length // 2, PAIR), F32), shaped((length // 2, PAIR), late)],
        6,
        scratch=[pltpu.VMEM((2 * rows, length), F32), pltpu.VMEM(stacked, F32)] + [pltpu.VMEM(stacked, BF16)] * 4,
        far=tuple(range(6, 6 + len(wait))),
    )


def by_expert(kind, x):
    return [jnp.where(kind == float(e), x, 0.0).astype(BF16) for e in range(2)]


def hidden_kernel(me_ref, kind_ref, g_ref, gc_ref, w_ref, wc_ref, *refs):
    mine_ref, away_ref = refs[-2:]
    rows = mine_ref.shape[0]
    count, _, depth, _ = w_ref.shape
    masked = []
    for ref in (g_ref, gc_ref):
        sides = []
        for i in range(2):
            here = pl.ds(pl.multiple_of((me_ref[0] ^ (2 * i)) * rows, rows), rows)
            sides.append(by_expert(kind_ref[here, :], ref[here, :].astype(F32)))
        masked += [jnp.concatenate([sides[0][e], sides[1][e]], axis=0) for e in range(2)]
    group = count // 4
    for j in range(4):
        total = 0.0
        for k, ref in enumerate((w_ref, wc_ref)):
            for e in range(2):
                w = ref[j * group : (j + 1) * group, e].reshape(group * depth, PAIR)
                total = total + contract(w, masked[2 * k + e], 1, 1)
        total = total.T
        cols = slice(j * group * depth, (j + 1) * group * depth)
        mine_ref[:, cols] = total[:rows]
        away_ref[:, cols] = total[rows:].astype(BF16)


def hidden_grad(me, kind, grad, grad_c, weight, weight_c, rows):
    count, _, depth, _ = weight.shape
    width = count * depth
    return call(
        hidden_kernel,
        me,
        (kind, grad, grad_c, weight, weight_c),
        [shaped((rows, width), F32), shaped((rows, width), BF16)],
        7,
    )


def share_kernel(steps, depth, split, me_ref, *refs):
    parts, g_ref, outs = refs[:8], refs[8], refs[-(2 if split else 1) * len(steps) :]
    rows, lanes = parts[0].shape[1:]
    pieces = [g_ref[pl.ds(piece_start(me_ref[0], i, rows), rows), :].astype(F32) for i in range(8)]
    kind = jnp.concatenate([read_marks(ref[0], depth)[0] for ref in parts], axis=0)
    right = jnp.concatenate(by_expert(kind, jnp.concatenate(pieces, axis=0)), axis=-1)
    for i, by in enumerate(steps):
        owner = owner_at(me_ref[1], by)
        left = jnp.concatenate([ref[owner] for ref in parts], axis=0)
        total = contract(left, right, 0, 0)
        for e in range(2):
            block = total[:depth, e * PAIR : (e + 1) * PAIR]
            if split:
                outs[2 * i + e][0] = block.astype(BF16)
            else:
                outs[i][e] = block


def shares(me, steps, parts, grad, depth, split=False, wait=()):
    if split:
        out = [shaped((1, depth, PAIR), BF16)] * (2 * len(steps))
    else:
        out = [shaped((2, depth, PAIR), F32)] * len(steps)
    far = tuple(range(9, 9 + len(wait)))
    return call(functools.partial(share_kernel, steps, depth, split), me, (*parts, grad, *wait), out, 1 + len(steps), far=far)


def in_order(parts, quarters):
    count, rows, lanes = parts[0].shape
    whole = jnp.stack(parts, axis=1).reshape(count, 4, 2 * rows, lanes)
    return jnp.take(whole, quarters, axis=1).reshape(count, 8 * rows, lanes)


def project_plain(quarters, parts, weights, depth):
    tokens = in_order(parts, quarters)
    kind, ids = read_marks(tokens[0], depth)
    sums = jnp.einsum("jmk,jekn->emn", tokens[:, :, :depth], weights, preferred_element_type=F32)
    return jnp.where(kind == 1.0, sums[1], sums[0]).astype(BF16), kind, ids, ids.reshape(1, -1)


def weight_plain(quarters, parts, grad, depth):
    tokens = in_order(parts, quarters)
    kind = tokens[0, :, depth : depth + 1].astype(F32)
    sums = [
        jnp.einsum("jmk,mn->jkn", tokens[:, :, :depth], g, preferred_element_type=F32)
        for g in by_expert(kind, grad.astype(F32))
    ]
    return lax.psum_scatter(jnp.stack(sums), "fsdp", scatter_dimension=1)


def per_device(fsdp, seq, tokens, queries, cotangent, modality, block_ids, kv_weight):
    tokens, queries, cotangent = tokens[0], queries[0], cotangent[0]
    me_f = lax.axis_index("fsdp")
    me_s = lax.axis_index("seq")
    rows, width = tokens.shape
    depth = kv_weight.shape[1]
    near_link = fsdp == len(CYCLE)

    def swap(x, bit):
        return lax.ppermute(x, "seq", [(i, i ^ bit) for i in range(seq)])

    def turn(x, by):
        return lax.ppermute(x, "fsdp", [(CYCLE[i], CYCLE[(i + by) % fsdp]) for i in range(fsdp)])

    def both_ways(ups, downs):
        return turn(ups, 1), turn(downs, -1)

    me = jnp.stack([me_s, me_f])
    quarters = me_s ^ jnp.arange(seq, dtype=jnp.int32)
    if near_link:
        weights = [kv_weight, *both_ways(kv_weight, kv_weight)]
        weights += both_ways(*weights[1:])
        weights += both_ways(*weights[3:])
    else:
        weight = lax.all_gather(kv_weight, "fsdp", axis=0)

    blocks = token_blocks(me, tokens, block_ids * 2 + modality, fsdp)
    across = [swap(x, 2) for x in blocks]
    parts = [*blocks, *[swap(x, 1) for x in blocks], *across, *[swap(x, 1) for x in across]]
    own, *others = pack_heads(me, queries, cotangent, weights[1:3] if near_link else ())
    others = [swap(x, 1) for x in others]

    if near_link:
        before = project(me, STEPS[:5], parts, weights[:5], (), depth)
        weights += both_ways(*halve(me, *weights[5:], others, (before[0],)))
        before = project(me, STEPS[5:7], parts, weights[5:7], before, depth)
        kv, kind, ids, ids_row, weight = project(me, STEPS[7:], parts, weights[7:], before, depth, True, True)
    else:
        kv, kind, ids, ids_row = project_plain(quarters, parts, weight, depth)
    kv_far = swap(kv, 2)
    far_own, far_other, early, late = attend(1, me, own, others[2:], kv_far, ids, ids_row, BF16)
    near_own, near_other, *near = attend(0, me, own, others[:2], kv, ids, ids_row, F32, (early,))
    grad_kv = jnp.concatenate([near[0] + swap(early, 2), near[1] + swap(late, 2).astype(F32)]).astype(BF16)
    attended, grad_queries = place_heads(me, (near_own, swap(near_other, 1), far_own, swap(far_other, 1)))

    grad_c = swap(grad_kv, 1)
    if near_link:
        ups, downs = both_ways(*shares(me, STEPS[7:], parts, grad_kv, depth, True))
    mine, away = hidden_grad(me, kind, grad_kv, grad_c, weight, swap(weight, 1), rows)
    if near_link:
        terms = shares(me, STEPS[5:7], parts, grad_kv, depth, wait=(away,))
        terms += shares(me, STEPS[:5], parts, grad_kv, depth)
        none = jnp.zeros_like(ups)
        ups, downs = jnp.concatenate([ups, none]), jnp.concatenate([none, downs])
        for i in (0, 5, 3):
            down, up = terms[i : i + 2]
            ups, downs = both_ways((up + ups.astype(F32)).astype(BF16), (down + downs.astype(F32)).astype(BF16))
        grad_weight = terms[2] + ups.astype(F32) + downs.astype(F32)
    else:
        grad_weight = weight_plain(quarters, parts, grad_kv, depth)
    grad_tokens = (mine + swap(away, 2).astype(F32)).astype(BF16)
    return attended[None], grad_queries[None], grad_tokens[None], grad_weight


def solution(mesh):
    split = P("fsdp", "seq", None)
    weights = P(None, "fsdp", "seq")
    return jax.shard_map(
        functools.partial(per_device, mesh.shape["fsdp"], mesh.shape["seq"]),
        mesh=mesh,
        in_specs=(split, split, split, P("fsdp", "seq"), P("fsdp", "seq"), weights),
        out_specs=(split, split, split, weights),
        check_vma=False,
    )
```

```python
import functools

import jax
import jax.numpy as jnp
from jax import lax
from jax.experimental import pallas as pl
from jax.experimental.pallas import tpu as pltpu
from jax.sharding import PartitionSpec as P

HEAD_DIM = 128
GROUP = 7
SPAN = GROUP * HEAD_DIM
PAIR = 2 * HEAD_DIM
SCALE = HEAD_DIM ** (-0.5)
LOG2E = 1.4426950408889634
HIDDEN = -1e30
DIGIT = 16
F32 = jnp.float32
BF16 = jnp.bfloat16
ANYWHERE = pl.BlockSpec(memory_space=pl.ANY)
CYCLE = (0, 2, 4, 6, 7, 5, 3, 1)
STEPS = (0, -1, 1, -2, 2, -3, 3, 4)


def contract(a, b, da, db):
    return lax.dot_general(a, b, (((da,), (db,)), ((), ())), preferred_element_type=F32)


def shaped(shape, dtype):
    return jax.ShapeDtypeStruct(shape, dtype)


def call(body, me, operands, out_shape, micros, scratch=(), far=(), far_out=(), aliases=None):
    near = pl.BlockSpec(memory_space=pltpu.VMEM)
    outs = [ANYWHERE if i in far_out else near for i in range(len(out_shape))] if isinstance(out_shape, list) else near
    return pl.pallas_call(
        body,
        in_specs=[pl.BlockSpec(memory_space=pltpu.SMEM)]
        + [ANYWHERE if i in far else near for i in range(len(operands))],
        out_specs=outs,
        out_shape=out_shape,
        scratch_shapes=scratch,
        input_output_aliases=aliases or {},
        compiler_params=pltpu.CompilerParams(vmem_limit_bytes=24 * 1024 * 1024),
        cost_estimate=pl.CostEstimate(flops=0, bytes_accessed=micros * 3000000, transcendentals=0),
    )(me, *operands)


def owner_at(me_f, by):
    size = len(CYCLE)
    half = size // 2
    line, side = lax.div(me_f, 2), lax.rem(me_f, 2)
    spot = jnp.where(side == 1, size - 1 - line, line)
    spot = lax.rem(spot + (size + by), size)
    return jnp.where(spot < half, 2 * spot, 2 * (size - 1 - spot) + 1)


def as_column(row):
    return jnp.broadcast_to(row, (128, row.shape[1])).T[:, :1]


def blocks_kernel(depth, me_ref, tok_ref, ids_ref, *out_refs):
    count, rows, lanes = out_refs[0].shape
    base = lanes - 128
    lane = lax.broadcasted_iota(jnp.int32, (rows, 128), 1) - (depth - base)
    ids = lax.div(ids_ref[...], 2)
    marks = (lax.rem(ids_ref[...], 2), lax.div(ids, DIGIT), lax.rem(ids, DIGIT))
    marks = [as_column(x.astype(F32)) for x in marks]
    for h, out_ref in enumerate(out_refs):
        here = slice(h * rows, (h + 1) * rows)
        for j in range(count):
            out_ref[j, :, :depth] = tok_ref[here, j * depth : (j + 1) * depth]
            last = out_ref[j, :, base:].astype(F32)
            last = jnp.where(lane >= 0, 0.0, last)
            for i, mark in enumerate(marks):
                last = jnp.where(lane == i, mark[here], last)
            out_ref[j, :, base:] = last.astype(BF16)


def token_blocks(me, tokens, ids, count):
    rows, width = tokens.shape
    depth = width // count
    lanes = -(-(depth + 3) // 128) * 128
    out = [shaped((count, rows // 2, lanes), BF16)] * 2
    return call(functools.partial(blocks_kernel, depth), me, (tokens, ids), out, 1)


def piece_start(me, i, rows):
    return pl.multiple_of((me ^ (i // 2)) * (2 * rows) + i % 2 * rows, rows)


def read_marks(block, depth):
    mark = [block[:, depth + i : depth + i + 1].astype(F32) for i in range(3)]
    return mark[0], mark[1] * DIGIT + mark[2]


def pack_kernel(me_ref, q_ref, up_ref, *refs):
    own_ref, other_refs = refs[-3], refs[-2:]
    for i in range(4):
        here = pl.ds(pl.multiple_of((me_ref[0] ^ i) * SPAN, SPAN), SPAN)
        for k, ref in enumerate((q_ref, up_ref)):
            if i % 2:
                other_refs[i // 2][k] = ref[:, here]
            else:
                own_ref[i // 2, k] = ref[:, here]


def pack_heads(me, queries, upstream):
    rows = queries.shape[0]
    out = [shaped((2, 2, rows, SPAN), BF16)] + [shaped((2, rows, SPAN), BF16)] * 2
    return call(pack_kernel, me, (queries, upstream), out, 2)


def place_kernel(me_ref, *refs):
    att_ref, gq_ref = refs[4:]
    for i, ref in enumerate(refs[:4]):
        here = pl.ds(pl.multiple_of((me_ref[0] ^ i) * SPAN, SPAN), SPAN)
        att_ref[:, here] = ref[0]
        gq_ref[:, here] = ref[1]


def place_heads(me, found):
    out = shaped((found[0].shape[1], 4 * SPAN), BF16)
    return call(place_kernel, me, found, [out, out], 3)


def project_kernel(steps, depth, halves, first, last, me_ref, *refs):
    parts, refs = refs[:8], refs[8:]
    weights, refs = refs[: len(steps) + halves], refs[len(steps) + halves :]
    whole_ref, sems = refs[-2:]
    rows, lanes = parts[0].shape[1:]
    owners = [owner_at(me_ref[1], by) for by in steps]
    copies = []
    for i, ref in enumerate(weights):
        there = whole_ref.at[owners[0], pl.ds(i, 1)] if halves else whole_ref.at[owners[i]]
        copies.append(pltpu.make_async_copy(ref, there, sems.at[i]))
    for copy in copies:
        copy.start()
    sums = [0.0, 0.0]
    for b, owner in enumerate(owners):
        left = jnp.concatenate([ref[owner][:, :depth] for ref in parts], axis=0)
        for e in range(2):
            right = weights[e][0] if halves else weights[b][e]
            sums[e] = sums[e] + contract(left, right, 1, 0)
    if not first:
        sums = [s + refs[0][:, e * PAIR : (e + 1) * PAIR] for e, s in enumerate(sums)]
    if not last:
        for e in range(2):
            refs[-3][:, e * PAIR : (e + 1) * PAIR] = sums[e]
    else:
        kv_ref, kind_ref, ids_ref, ids_row_ref = refs[-6:-2]
        for i, ref in enumerate(parts):
            here = pl.ds(piece_start(me_ref[0], i, rows), rows)
            kind, ids = read_marks(ref[0], depth)
            mine = slice(i * rows, (i + 1) * rows)
            kv_ref[here, :] = jnp.where(kind == 1.0, sums[1][mine], sums[0][mine]).astype(BF16)
            kind_ref[here, :] = kind
            ids_ref[here, :] = ids
        ids_row_ref[...] = jnp.broadcast_to(ids_ref[...], (8 * rows, 128)).T[:1]
    for copy in copies:
        copy.wait()


def project(me, steps, parts, weights, before, depth, last=False, halves=False):
    length = 8 * parts[0].shape[1]
    outs = [shaped((length, 2 * PAIR), F32)]
    if last:
        outs = [shaped((length, PAIR), BF16)] + [shaped(x, F32) for x in ((length, 1), (length, 1), (1, length))]
    outs.append(shaped((len(CYCLE), 2, depth, PAIR), BF16))
    operands = (*parts, *weights, *before)
    count = len(operands)
    return call(
        functools.partial(project_kernel, steps, depth, int(halves), not before, last),
        me,
        operands,
        outs,
        1,
        scratch=[pltpu.SemaphoreType.DMA((len(weights),))],
        far=(count - 1,) if before else (),
        far_out=(len(outs) - 1,),
        aliases={count: len(outs) - 1} if before else None,
    )


def hold_kernel(count, me_ref, *refs):
    for i in range(count):
        refs[i - count][...] = refs[i][...]


def hold(me, arrays, others):
    out = [shaped(x.shape, x.dtype) for x in arrays]
    return call(functools.partial(hold_kernel, len(arrays)), me, (*arrays, *others), out, 1)


def halve_kernel(me_ref, ups_ref, downs_ref, *refs):
    refs[-2][...] = ups_ref[:1]
    refs[-1][...] = downs_ref[1:]


def halve(me, ups, downs, wait):
    out = [shaped((1, *ups.shape[1:]), ups.dtype)] * 2
    return call(halve_kernel, me, (ups, downs, *wait), out, 1, far=tuple(range(2, 2 + len(wait))))


def attend_kernel(spot, me_ref, own_ref, sibling_ref, kv_ref, ids_ref, ids_row_ref, *refs):
    mine_ref, other_ref, early_ref, late_ref, bias, scores_all, dp_all, pbs, his, los = refs[-10:]
    rows = own_ref.shape[2]
    heads = [slice(h * HEAD_DIM, (h + 1) * HEAD_DIM) for h in range(GROUP)]
    for i in range(2):
        here = pl.ds(pl.multiple_of((me_ref[0] ^ i) * rows, rows), rows)
        bias[i * rows : (i + 1) * rows, :] = jnp.where(ids_row_ref[...] <= ids_ref[here, :], 0.0, HIDDEN)
    keys = kv_ref[:, :HEAD_DIM]
    values = kv_ref[:, HEAD_DIM:]
    q, up = [
        jnp.concatenate([own_ref[spot, i, :, c] for c in heads] + [sibling_ref[i, :, c] for c in heads], axis=0)
        for i in range(2)
    ]
    scores_all[...] = contract(q, keys, 1, 1)
    dp_all[...] = contract(up, values, 1, 1).astype(BF16)
    for h in range(2 * GROUP):
        here = slice(h * rows, (h + 1) * rows)
        side = h // GROUP
        scores = scores_all[here, :] * (SCALE * LOG2E) + bias[side * rows : (side + 1) * rows, :]
        expo = jnp.exp2(scores - jnp.max(scores, axis=-1, keepdims=True))
        probs = expo * (1.0 / jnp.sum(expo, axis=-1, keepdims=True))
        pbs[here, :] = probs.astype(BF16)
        dp = dp_all[here, :].astype(F32)
        ds = probs * (dp - jnp.sum(probs * dp, axis=-1, keepdims=True))
        hi = ds.astype(BF16)
        his[here, :] = hi
        los[here, :] = (ds - hi.astype(F32)).astype(BF16)
    att = contract(pbs[...], values, 1, 0).astype(BF16)
    gq = ((contract(his[...], keys, 1, 0) + contract(los[...], keys, 1, 0)) * SCALE).astype(BF16)
    for i, ref in enumerate((mine_ref, other_ref)):
        for h, cols in enumerate(heads):
            here = slice((i * GROUP + h) * rows, (i * GROUP + h + 1) * rows)
            ref[0, :, cols] = att[here]
            ref[1, :, cols] = gq[here]
    dk = (contract(q, his[...], 0, 0) + contract(q, los[...], 0, 0)) * SCALE
    dv = contract(up, pbs[...], 0, 0)
    half = early_ref.shape[0]
    for i, x in enumerate((dk.T, dv.T)):
        cols = slice(i * HEAD_DIM, (i + 1) * HEAD_DIM)
        early_ref[:, cols] = x[:half]
        late_ref[:, cols] = x[half:].astype(late_ref.dtype)


def attend(spot, me, own, other, kv, ids, ids_row, late, wait=()):
    rows = own.shape[2]
    length = kv.shape[0]
    stacked = (2 * GROUP * rows, length)
    side = shaped((2, rows, SPAN), BF16)
    return call(
        functools.partial(attend_kernel, spot),
        me,
        (own, other, kv, ids, ids_row, *wait),
        [side, side, shaped((length // 2, PAIR), F32), shaped((length // 2, PAIR), late)],
        6,
        scratch=[pltpu.VMEM((2 * rows, length), F32), pltpu.VMEM(stacked, F32)] + [pltpu.VMEM(stacked, BF16)] * 4,
        far=tuple(range(5, 5 + len(wait))),
    )


def by_expert(kind, x):
    return [jnp.where(kind == float(e), x, 0.0).astype(BF16) for e in range(2)]


def hidden_kernel(me_ref, kind_ref, g_ref, gc_ref, w_ref, wc_ref, *refs):
    mine_ref, away_ref = refs[-2:]
    rows = mine_ref.shape[0]
    count, _, depth, _ = w_ref.shape
    masked = []
    for ref in (g_ref, gc_ref):
        sides = []
        for i in range(2):
            here = pl.ds(pl.multiple_of((me_ref[0] ^ (2 * i)) * rows, rows), rows)
            sides.append(by_expert(kind_ref[here, :], ref[here, :].astype(F32)))
        masked += [jnp.concatenate([sides[0][e], sides[1][e]], axis=0) for e in range(2)]
    group = count // 4
    for j in range(4):
        total = 0.0
        for k, ref in enumerate((w_ref, wc_ref)):
            for e in range(2):
                w = ref[j * group : (j + 1) * group, e].reshape(group * depth, PAIR)
                total = total + contract(w, masked[2 * k + e], 1, 1)
        total = total.T
        cols = slice(j * group * depth, (j + 1) * group * depth)
        mine_ref[:, cols] = total[:rows]
        away_ref[:, cols] = total[rows:].astype(BF16)


def hidden_grad(me, kind, grad, grad_c, weight, weight_c, rows):
    count, _, depth, _ = weight.shape
    width = count * depth
    return call(
        hidden_kernel,
        me,
        (kind, grad, grad_c, weight, weight_c),
        [shaped((rows, width), F32), shaped((rows, width), BF16)],
        7,
    )


def share_kernel(steps, depth, split, me_ref, *refs):
    parts, g_ref, outs = refs[:8], refs[8], refs[-(2 if split else 1) * len(steps) :]
    rows, lanes = parts[0].shape[1:]
    pieces = [g_ref[pl.ds(piece_start(me_ref[0], i, rows), rows), :].astype(F32) for i in range(8)]
    kind = jnp.concatenate([read_marks(ref[0], depth)[0] for ref in parts], axis=0)
    right = jnp.concatenate(by_expert(kind, jnp.concatenate(pieces, axis=0)), axis=-1)
    for i, by in enumerate(steps):
        owner = owner_at(me_ref[1], by)
        left = jnp.concatenate([ref[owner] for ref in parts], axis=0)
        total = contract(left, right, 0, 0)
        for e in range(2):
            block = total[:depth, e * PAIR : (e + 1) * PAIR]
            if split:
                outs[2 * i + e][0] = block.astype(BF16)
            else:
                outs[i][e] = block


def shares(me, steps, parts, grad, depth, split=False, wait=()):
    if split:
        out = [shaped((1, depth, PAIR), BF16)] * (2 * len(steps))
    else:
        out = [shaped((2, depth, PAIR), F32)] * len(steps)
    far = tuple(range(9, 9 + len(wait)))
    return call(functools.partial(share_kernel, steps, depth, split), me, (*parts, grad, *wait), out, 1 + len(steps), far=far)


def in_order(parts, quarters):
    count, rows, lanes = parts[0].shape
    whole = jnp.stack(parts, axis=1).reshape(count, 4, 2 * rows, lanes)
    return jnp.take(whole, quarters, axis=1).reshape(count, 8 * rows, lanes)


def project_plain(quarters, parts, weights, depth):
    tokens = in_order(parts, quarters)
    kind, ids = read_marks(tokens[0], depth)
    sums = jnp.einsum("jmk,jekn->emn", tokens[:, :, :depth], weights, preferred_element_type=F32)
    return jnp.where(kind == 1.0, sums[1], sums[0]).astype(BF16), kind, ids, ids.reshape(1, -1)


def weight_plain(quarters, parts, grad, depth):
    tokens = in_order(parts, quarters)
    kind = tokens[0, :, depth : depth + 1].astype(F32)
    sums = [
        jnp.einsum("jmk,mn->jkn", tokens[:, :, :depth], g, preferred_element_type=F32)
        for g in by_expert(kind, grad.astype(F32))
    ]
    return lax.psum_scatter(jnp.stack(sums), "fsdp", scatter_dimension=1)


def per_device(fsdp, seq, tokens, queries, cotangent, modality, block_ids, kv_weight):
    tokens, queries, cotangent = tokens[0], queries[0], cotangent[0]
    me_f = lax.axis_index("fsdp")
    me_s = lax.axis_index("seq")
    rows, width = tokens.shape
    depth = kv_weight.shape[1]
    near_link = fsdp == len(CYCLE)

    def swap(x, bit):
        return lax.ppermute(x, "seq", [(i, i ^ bit) for i in range(seq)])

    def turn(x, by):
        return lax.ppermute(x, "fsdp", [(CYCLE[i], CYCLE[(i + by) % fsdp]) for i in range(fsdp)])

    def both_ways(ups, downs):
        return turn(ups, 1), turn(downs, -1)

    me = jnp.stack([me_s, me_f])
    quarters = me_s ^ jnp.arange(seq, dtype=jnp.int32)
    if near_link:
        weights = [kv_weight, *both_ways(kv_weight, kv_weight)]
        weights += both_ways(*weights[1:])
        weights += both_ways(*weights[3:])
    else:
        weight = lax.all_gather(kv_weight, "fsdp", axis=0)

    blocks = token_blocks(me, tokens, block_ids * 2 + modality, fsdp)
    across = [swap(x, 2) for x in blocks]
    own, *others = pack_heads(me, queries, cotangent)
    others = [swap(x, 1) for x in others]
    here = hold(me, blocks, (*weights[1:3], *others)) if near_link else blocks
    parts = [*here, *[swap(x, 1) for x in here], *across, *[swap(x, 1) for x in across]]

    if near_link:
        before = project(me, STEPS[:5], parts, weights[:5], (), depth)
        weights += both_ways(*halve(me, *weights[5:], (before[0],)))
        before = project(me, STEPS[5:7], parts, weights[5:7], before, depth)
        kv, kind, ids, ids_row, weight = project(me, STEPS[7:], parts, weights[7:], before, depth, True, True)
    else:
        kv, kind, ids, ids_row = project_plain(quarters, parts, weight, depth)
    kv_far = swap(kv, 2)
    far_own, far_other, early, late = attend(1, me, own, others[1], kv_far, ids, ids_row, BF16)
    near_own, near_other, *near = attend(0, me, own, others[0], kv, ids, ids_row, F32, (early,))
    grad_kv = jnp.concatenate([near[0] + swap(early, 2), near[1] + swap(late, 2).astype(F32)]).astype(BF16)
    attended, grad_queries = place_heads(me, (near_own, swap(near_other, 1), far_own, swap(far_other, 1)))

    grad_c = swap(grad_kv, 1)
    if near_link:
        ups, downs = both_ways(*shares(me, STEPS[7:], parts, grad_kv, depth, True))
    mine, away = hidden_grad(me, kind, grad_kv, grad_c, weight, swap(weight, 1), rows)
    if near_link:
        terms = shares(me, STEPS[5:7], parts, grad_kv, depth, wait=(away,))
        terms += shares(me, STEPS[:5], parts, grad_kv, depth)
        none = jnp.zeros_like(ups)
        ups, downs = jnp.concatenate([ups, none]), jnp.concatenate([none, downs])
        for i in (0, 5, 3):
            down, up = terms[i : i + 2]
            ups, downs = both_ways((up + ups.astype(F32)).astype(BF16), (down + downs.astype(F32)).astype(BF16))
        grad_weight = terms[2] + ups.astype(F32) + downs.astype(F32)
    else:
        grad_weight = weight_plain(quarters, parts, grad_kv, depth)
    grad_tokens = (mine + swap(away, 2).astype(F32)).astype(BF16)
    return attended[None], grad_queries[None], grad_tokens[None], grad_weight


def solution(mesh):
    split = P("fsdp", "seq", None)
    weights = P(None, "fsdp", "seq")
    return jax.shard_map(
        functools.partial(per_device, mesh.shape["fsdp"], mesh.shape["seq"]),
        mesh=mesh,
        in_specs=(split, split, split, P("fsdp", "seq"), P("fsdp", "seq"), weights),
        out_specs=(split, split, split, weights),
        check_vma=False,
    )
```

```python
import functools

import jax
import jax.numpy as jnp
from jax import lax
from jax.experimental import pallas as pl
from jax.experimental.pallas import tpu as pltpu
from jax.sharding import PartitionSpec as P

HEAD_DIM = 128
GROUP = 7
SPAN = GROUP * HEAD_DIM
PAIR = 2 * HEAD_DIM
SCALE = HEAD_DIM ** (-0.5)
LOG2E = 1.4426950408889634
HIDDEN = -1e30
DIGIT = 16
F32 = jnp.float32
BF16 = jnp.bfloat16
ANYWHERE = pl.BlockSpec(memory_space=pl.ANY)
CYCLE = (0, 2, 4, 6, 7, 5, 3, 1)
STEPS = (0, -1, 1, -2, 2, -3, 3, 4)


def contract(a, b, da, db):
    return lax.dot_general(a, b, (((da,), (db,)), ((), ())), preferred_element_type=F32)


def shaped(shape, dtype):
    return jax.ShapeDtypeStruct(shape, dtype)


def call(body, me, operands, out_shape, micros, scratch=(), far=(), far_out=(), aliases=None):
    near = pl.BlockSpec(memory_space=pltpu.VMEM)
    outs = [ANYWHERE if i in far_out else near for i in range(len(out_shape))] if isinstance(out_shape, list) else near
    return pl.pallas_call(
        body,
        in_specs=[pl.BlockSpec(memory_space=pltpu.SMEM)]
        + [ANYWHERE if i in far else near for i in range(len(operands))],
        out_specs=outs,
        out_shape=out_shape,
        scratch_shapes=scratch,
        input_output_aliases=aliases or {},
        compiler_params=pltpu.CompilerParams(vmem_limit_bytes=24 * 1024 * 1024),
        cost_estimate=pl.CostEstimate(flops=0, bytes_accessed=micros * 3000000, transcendentals=0),
    )(me, *operands)


def owner_at(me_f, by):
    size = len(CYCLE)
    half = size // 2
    line, side = lax.div(me_f, 2), lax.rem(me_f, 2)
    spot = jnp.where(side == 1, size - 1 - line, line)
    spot = lax.rem(spot + (size + by), size)
    return jnp.where(spot < half, 2 * spot, 2 * (size - 1 - spot) + 1)


def as_column(row):
    return jnp.broadcast_to(row, (128, row.shape[1])).T[:, :1]


def blocks_kernel(depth, me_ref, tok_ref, ids_ref, whole_ref, *out_refs):
    count, rows, lanes = out_refs[0].shape
    base = lanes - 128
    lane = lax.broadcasted_iota(jnp.int32, (rows, 128), 1) - (depth - base)
    ids = lax.div(ids_ref[...], 2)
    marks = (lax.rem(ids_ref[...], 2), lax.div(ids, DIGIT), lax.rem(ids, DIGIT))
    marks = [as_column(x.astype(F32)) for x in marks]
    for h, out_ref in enumerate(out_refs):
        here = slice(h * rows, (h + 1) * rows)
        for j in range(count):
            out_ref[j, :, :depth] = tok_ref[here, j * depth : (j + 1) * depth]
            last = out_ref[j, :, base:].astype(F32)
            last = jnp.where(lane >= 0, 0.0, last)
            for i, mark in enumerate(marks):
                last = jnp.where(lane == i, mark[here], last)
            out_ref[j, :, base:] = last.astype(BF16)
        whole_ref[h] = out_ref[...]


def token_blocks(me, tokens, ids, count):
    rows, width = tokens.shape
    depth = width // count
    lanes = -(-(depth + 3) // 128) * 128
    out = [shaped((2, count, rows // 2, lanes), BF16)] + [shaped((count, rows // 2, lanes), BF16)] * 2
    return call(functools.partial(blocks_kernel, depth), me, (tokens, ids), out, 1)


def piece_start(me, i, rows):
    return pl.multiple_of((me ^ (i // 2)) * (2 * rows) + i % 2 * rows, rows)


def read_marks(block, depth):
    mark = [block[:, depth + i : depth + i + 1].astype(F32) for i in range(3)]
    return mark[0], mark[1] * DIGIT + mark[2]


def pack_kernel(me_ref, q_ref, up_ref, *refs):
    own_ref, other_refs = refs[-3], refs[-2:]
    for i in range(4):
        here = pl.ds(pl.multiple_of((me_ref[0] ^ i) * SPAN, SPAN), SPAN)
        for k, ref in enumerate((q_ref, up_ref)):
            if i % 2:
                other_refs[i // 2][k] = ref[:, here]
            else:
                own_ref[i // 2, k] = ref[:, here]


def pack_heads(me, queries, upstream):
    rows = queries.shape[0]
    out = [shaped((2, 2, rows, SPAN), BF16)] + [shaped((2, rows, SPAN), BF16)] * 2
    return call(pack_kernel, me, (queries, upstream), out, 1)


def place_kernel(me_ref, *refs):
    att_ref, gq_ref = refs[4:]
    for i, ref in enumerate(refs[:4]):
        here = pl.ds(pl.multiple_of((me_ref[0] ^ i) * SPAN, SPAN), SPAN)
        att_ref[:, here] = ref[0]
        gq_ref[:, here] = ref[1]


def place_heads(me, found):
    out = shaped((found[0].shape[1], 4 * SPAN), BF16)
    return call(place_kernel, me, found, [out, out], 3)


def project_kernel(steps, depth, halves, first, last, me_ref, *refs):
    parts, refs = refs[:8], refs[8:]
    weights, refs = refs[: len(steps) + halves], refs[len(steps) + halves :]
    whole_ref, sems = refs[-2:]
    rows, lanes = parts[0].shape[1:]
    owners = [owner_at(me_ref[1], by) for by in steps]
    copies = []
    for i, ref in enumerate(weights):
        there = whole_ref.at[owners[0], pl.ds(i, 1)] if halves else whole_ref.at[owners[i]]
        copies.append(pltpu.make_async_copy(ref, there, sems.at[i]))
    for copy in copies:
        copy.start()
    sums = [0.0, 0.0]
    for b, owner in enumerate(owners):
        left = jnp.concatenate([ref[owner][:, :depth] for ref in parts], axis=0)
        for e in range(2):
            right = weights[e][0] if halves else weights[b][e]
            sums[e] = sums[e] + contract(left, right, 1, 0)
    if not first:
        sums = [s + refs[0][:, e * PAIR : (e + 1) * PAIR] for e, s in enumerate(sums)]
    if not last:
        for e in range(2):
            refs[-3][:, e * PAIR : (e + 1) * PAIR] = sums[e]
    else:
        kv_ref, kind_ref, ids_ref, ids_row_ref = refs[-6:-2]
        for i, ref in enumerate(parts):
            here = pl.ds(piece_start(me_ref[0], i, rows), rows)
            kind, ids = read_marks(ref[0], depth)
            mine = slice(i * rows, (i + 1) * rows)
            kv_ref[here, :] = jnp.where(kind == 1.0, sums[1][mine], sums[0][mine]).astype(BF16)
            kind_ref[here, :] = kind
            ids_ref[here, :] = ids
        ids_row_ref[...] = jnp.broadcast_to(ids_ref[...], (8 * rows, 128)).T[:1]
    for copy in copies:
        copy.wait()


def project(me, steps, parts, weights, before, depth, last=False, halves=False):
    length = 8 * parts[0].shape[1]
    outs = [shaped((length, 2 * PAIR), F32)]
    if last:
        outs = [shaped((length, PAIR), BF16)] + [shaped(x, F32) for x in ((length, 1), (length, 1), (1, length))]
    outs.append(shaped((len(CYCLE), 2, depth, PAIR), BF16))
    operands = (*parts, *weights, *before)
    count = len(operands)
    return call(
        functools.partial(project_kernel, steps, depth, int(halves), not before, last),
        me,
        operands,
        outs,
        1,
        scratch=[pltpu.SemaphoreType.DMA((len(weights),))],
        far=(count - 1,) if before else (),
        far_out=(len(outs) - 1,),
        aliases={count: len(outs) - 1} if before else None,
    )


def hold_kernel(count, me_ref, *refs):
    for i in range(count):
        refs[i - count][...] = refs[i][...]


def hold(me, arrays, others):
    out = [shaped(x.shape, x.dtype) for x in arrays]
    return call(functools.partial(hold_kernel, len(arrays)), me, (*arrays, *others), out, 1)


def split_kernel(me_ref, x_ref, *out_refs):
    for h, ref in enumerate(out_refs):
        ref[...] = x_ref[h]


def split(me, x):
    return call(split_kernel, me, (x,), [shaped(x.shape[1:], x.dtype)] * 2, 1)


def halve_kernel(me_ref, ups_ref, downs_ref, *refs):
    refs[-2][...] = ups_ref[:1]
    refs[-1][...] = downs_ref[1:]


def halve(me, ups, downs, wait):
    out = [shaped((1, *ups.shape[1:]), ups.dtype)] * 2
    return call(halve_kernel, me, (ups, downs, *wait), out, 1, far=tuple(range(2, 2 + len(wait))))


def attend_kernel(spot, me_ref, own_ref, sibling_ref, kv_ref, ids_ref, ids_row_ref, *refs):
    mine_ref, other_ref, early_ref, late_ref, bias, scores_all, dp_all, pbs, his, los = refs[-10:]
    rows = own_ref.shape[2]
    heads = [slice(h * HEAD_DIM, (h + 1) * HEAD_DIM) for h in range(GROUP)]
    for i in range(2):
        here = pl.ds(pl.multiple_of((me_ref[0] ^ i) * rows, rows), rows)
        bias[i * rows : (i + 1) * rows, :] = jnp.where(ids_row_ref[...] <= ids_ref[here, :], 0.0, HIDDEN)
    keys = kv_ref[:, :HEAD_DIM]
    values = kv_ref[:, HEAD_DIM:]
    q, up = [
        jnp.concatenate([own_ref[spot, i, :, c] for c in heads] + [sibling_ref[i, :, c] for c in heads], axis=0)
        for i in range(2)
    ]
    scores_all[...] = contract(q, keys, 1, 1)
    dp_all[...] = contract(up, values, 1, 1).astype(BF16)
    for h in range(2 * GROUP):
        here = slice(h * rows, (h + 1) * rows)
        side = h // GROUP
        scores = scores_all[here, :] * (SCALE * LOG2E) + bias[side * rows : (side + 1) * rows, :]
        expo = jnp.exp2(scores - jnp.max(scores, axis=-1, keepdims=True))
        probs = expo * (1.0 / jnp.sum(expo, axis=-1, keepdims=True))
        pbs[here, :] = probs.astype(BF16)
        dp = dp_all[here, :].astype(F32)
        ds = probs * (dp - jnp.sum(probs * dp, axis=-1, keepdims=True))
        hi = ds.astype(BF16)
        his[here, :] = hi
        los[here, :] = (ds - hi.astype(F32)).astype(BF16)
    att = contract(pbs[...], values, 1, 0).astype(BF16)
    gq = ((contract(his[...], keys, 1, 0) + contract(los[...], keys, 1, 0)) * SCALE).astype(BF16)
    for i, ref in enumerate((mine_ref, other_ref)):
        for h, cols in enumerate(heads):
            here = slice((i * GROUP + h) * rows, (i * GROUP + h + 1) * rows)
            ref[0, :, cols] = att[here]
            ref[1, :, cols] = gq[here]
    dk = (contract(q, his[...], 0, 0) + contract(q, los[...], 0, 0)) * SCALE
    dv = contract(up, pbs[...], 0, 0)
    half = early_ref.shape[0]
    for i, x in enumerate((dk.T, dv.T)):
        cols = slice(i * HEAD_DIM, (i + 1) * HEAD_DIM)
        early_ref[:, cols] = x[:half]
        late_ref[:, cols] = x[half:].astype(late_ref.dtype)


def attend(spot, me, own, other, kv, ids, ids_row, late, wait=()):
    rows = own.shape[2]
    length = kv.shape[0]
    stacked = (2 * GROUP * rows, length)
    side = shaped((2, rows, SPAN), BF16)
    return call(
        functools.partial(attend_kernel, spot),
        me,
        (own, other, kv, ids, ids_row, *wait),
        [side, side, shaped((length // 2, PAIR), F32), shaped((length // 2, PAIR), late)],
        6,
        scratch=[pltpu.VMEM((2 * rows, length), F32), pltpu.VMEM(stacked, F32)] + [pltpu.VMEM(stacked, BF16)] * 4,
        far=tuple(range(5, 5 + len(wait))),
    )


def by_expert(kind, x):
    return [jnp.where(kind == float(e), x, 0.0).astype(BF16) for e in range(2)]


def hidden_kernel(me_ref, kind_ref, g_ref, gc_ref, w_ref, wc_ref, *refs):
    mine_ref, away_ref = refs[-2:]
    rows = mine_ref.shape[0]
    count, _, depth, _ = w_ref.shape
    masked = []
    for ref in (g_ref, gc_ref):
        sides = []
        for i in range(2):
            here = pl.ds(pl.multiple_of((me_ref[0] ^ (2 * i)) * rows, rows), rows)
            sides.append(by_expert(kind_ref[here, :], ref[here, :].astype(F32)))
        masked += [jnp.concatenate([sides[0][e], sides[1][e]], axis=0) for e in range(2)]
    group = count // 4
    for j in range(4):
        total = 0.0
        for k, ref in enumerate((w_ref, wc_ref)):
            for e in range(2):
                w = ref[j * group : (j + 1) * group, e].reshape(group * depth, PAIR)
                total = total + contract(w, masked[2 * k + e], 1, 1)
        total = total.T
        cols = slice(j * group * depth, (j + 1) * group * depth)
        mine_ref[:, cols] = total[:rows]
        away_ref[:, cols] = total[rows:].astype(BF16)


def hidden_grad(me, kind, grad, grad_c, weight, weight_c, rows):
    count, _, depth, _ = weight.shape
    width = count * depth
    return call(
        hidden_kernel,
        me,
        (kind, grad, grad_c, weight, weight_c),
        [shaped((rows, width), F32), shaped((rows, width), BF16)],
        7,
    )


def share_kernel(steps, depth, split, me_ref, *refs):
    parts, g_ref, outs = refs[:8], refs[8], refs[-(2 if split else 1) * len(steps) :]
    rows, lanes = parts[0].shape[1:]
    pieces = [g_ref[pl.ds(piece_start(me_ref[0], i, rows), rows), :].astype(F32) for i in range(8)]
    kind = jnp.concatenate([read_marks(ref[0], depth)[0] for ref in parts], axis=0)
    right = jnp.concatenate(by_expert(kind, jnp.concatenate(pieces, axis=0)), axis=-1)
    for i, by in enumerate(steps):
        owner = owner_at(me_ref[1], by)
        left = jnp.concatenate([ref[owner] for ref in parts], axis=0)
        total = contract(left, right, 0, 0)
        for e in range(2):
            block = total[:depth, e * PAIR : (e + 1) * PAIR]
            if split:
                outs[2 * i + e][0] = block.astype(BF16)
            else:
                outs[i][e] = block


def shares(me, steps, parts, grad, depth, split=False, wait=()):
    if split:
        out = [shaped((1, depth, PAIR), BF16)] * (2 * len(steps))
    else:
        out = [shaped((2, depth, PAIR), F32)] * len(steps)
    far = tuple(range(9, 9 + len(wait)))
    return call(functools.partial(share_kernel, steps, depth, split), me, (*parts, grad, *wait), out, 1 + len(steps), far=far)


def in_order(parts, quarters):
    count, rows, lanes = parts[0].shape
    whole = jnp.stack(parts, axis=1).reshape(count, 4, 2 * rows, lanes)
    return jnp.take(whole, quarters, axis=1).reshape(count, 8 * rows, lanes)


def project_plain(quarters, parts, weights, depth):
    tokens = in_order(parts, quarters)
    kind, ids = read_marks(tokens[0], depth)
    sums = jnp.einsum("jmk,jekn->emn", tokens[:, :, :depth], weights, preferred_element_type=F32)
    return jnp.where(kind == 1.0, sums[1], sums[0]).astype(BF16), kind, ids, ids.reshape(1, -1)


def weight_plain(quarters, parts, grad, depth):
    tokens = in_order(parts, quarters)
    kind = tokens[0, :, depth : depth + 1].astype(F32)
    sums = [
        jnp.einsum("jmk,mn->jkn", tokens[:, :, :depth], g, preferred_element_type=F32)
        for g in by_expert(kind, grad.astype(F32))
    ]
    return lax.psum_scatter(jnp.stack(sums), "fsdp", scatter_dimension=1)


def per_device(fsdp, seq, tokens, queries, cotangent, modality, block_ids, kv_weight):
    tokens, queries, cotangent = tokens[0], queries[0], cotangent[0]
    me_f = lax.axis_index("fsdp")
    me_s = lax.axis_index("seq")
    rows, width = tokens.shape
    depth = kv_weight.shape[1]
    near_link = fsdp == len(CYCLE)

    def swap(x, bit):
        return lax.ppermute(x, "seq", [(i, i ^ bit) for i in range(seq)])

    def turn(x, by):
        return lax.ppermute(x, "fsdp", [(CYCLE[i], CYCLE[(i + by) % fsdp]) for i in range(fsdp)])

    def both_ways(ups, downs):
        return turn(ups, 1), turn(downs, -1)

    me = jnp.stack([me_s, me_f])
    quarters = me_s ^ jnp.arange(seq, dtype=jnp.int32)
    if near_link:
        weights = [kv_weight, *both_ways(kv_weight, kv_weight)]
        weights += both_ways(*weights[1:])
        weights += both_ways(*weights[3:])
    else:
        weight = lax.all_gather(kv_weight, "fsdp", axis=0)

    whole, *blocks = token_blocks(me, tokens, block_ids * 2 + modality, fsdp)
    across = split(me, swap(whole, 2))
    own, *others = pack_heads(me, queries, cotangent)
    others = [swap(x, 1) for x in others]
    here = hold(me, blocks, (*weights[1:3], *others)) if near_link else blocks
    parts = [*here, *[swap(x, 1) for x in here], *across, *[swap(x, 1) for x in across]]

    if near_link:
        before = project(me, STEPS[:5], parts, weights[:5], (), depth)
        weights += both_ways(*halve(me, *weights[5:], (before[0],)))
        before = project(me, STEPS[5:7], parts, weights[5:7], before, depth)
        kv, kind, ids, ids_row, weight = project(me, STEPS[7:], parts, weights[7:], before, depth, True, True)
    else:
        kv, kind, ids, ids_row = project_plain(quarters, parts, weight, depth)
    kv_far = swap(kv, 2)
    far_own, far_other, early, late = attend(1, me, own, others[1], kv_far, ids, ids_row, BF16)
    near_own, near_other, *near = attend(0, me, own, others[0], kv, ids, ids_row, F32, (early,))
    grad_kv = jnp.concatenate([near[0] + swap(early, 2), near[1] + swap(late, 2).astype(F32)]).astype(BF16)
    attended, grad_queries = place_heads(me, (near_own, swap(near_other, 1), far_own, swap(far_other, 1)))

    grad_c = swap(grad_kv, 1)
    if near_link:
        ups, downs = both_ways(*shares(me, STEPS[7:], parts, grad_kv, depth, True))
    mine, away = hidden_grad(me, kind, grad_kv, grad_c, weight, swap(weight, 1), rows)
    if near_link:
        terms = shares(me, STEPS[5:7], parts, grad_kv, depth, wait=(away,))
        terms += shares(me, STEPS[:5], parts, grad_kv, depth)
        none = jnp.zeros_like(ups)
        ups, downs = jnp.concatenate([ups, none]), jnp.concatenate([none, downs])
        for i in (0, 5, 3):
            down, up = terms[i : i + 2]
            ups, downs = both_ways((up + ups.astype(F32)).astype(BF16), (down + downs.astype(F32)).astype(BF16))
        grad_weight = terms[2] + ups.astype(F32) + downs.astype(F32)
    else:
        grad_weight = weight_plain(quarters, parts, grad_kv, depth)
    grad_tokens = (mine + swap(away, 2).astype(F32)).astype(BF16)
    return attended[None], grad_queries[None], grad_tokens[None], grad_weight


def solution(mesh):
    split = P("fsdp", "seq", None)
    weights = P(None, "fsdp", "seq")
    return jax.shard_map(
        functools.partial(per_device, mesh.shape["fsdp"], mesh.shape["seq"]),
        mesh=mesh,
        in_specs=(split, split, split, P("fsdp", "seq"), P("fsdp", "seq"), weights),
        out_specs=(split, split, split, weights),
        check_vma=False,
    )
```

```python
import functools

import jax
import jax.numpy as jnp
from jax import lax
from jax.experimental import pallas as pl
from jax.experimental.pallas import tpu as pltpu
from jax.sharding import PartitionSpec as P

HEAD_DIM = 128
GROUP = 7
SPAN = GROUP * HEAD_DIM
PAIR = 2 * HEAD_DIM
SCALE = HEAD_DIM ** (-0.5)
LOG2E = 1.4426950408889634
HIDDEN = -1e30
DIGIT = 16
F32 = jnp.float32
BF16 = jnp.bfloat16
ANYWHERE = pl.BlockSpec(memory_space=pl.ANY)
CYCLE = (0, 2, 4, 6, 7, 5, 3, 1)
STEPS = (0, -1, 1, -2, 2, -3, 3, 4)


def contract(a, b, da, db):
    return lax.dot_general(a, b, (((da,), (db,)), ((), ())), preferred_element_type=F32)


def shaped(shape, dtype):
    return jax.ShapeDtypeStruct(shape, dtype)


def call(body, me, operands, out_shape, micros, scratch=(), far=(), far_out=(), aliases=None):
    near = pl.BlockSpec(memory_space=pltpu.VMEM)
    outs = [ANYWHERE if i in far_out else near for i in range(len(out_shape))] if isinstance(out_shape, list) else near
    return pl.pallas_call(
        body,
        in_specs=[pl.BlockSpec(memory_space=pltpu.SMEM)]
        + [ANYWHERE if i in far else near for i in range(len(operands))],
        out_specs=outs,
        out_shape=out_shape,
        scratch_shapes=scratch,
        input_output_aliases=aliases or {},
        compiler_params=pltpu.CompilerParams(vmem_limit_bytes=24 * 1024 * 1024),
        cost_estimate=pl.CostEstimate(flops=0, bytes_accessed=micros * 3000000, transcendentals=0),
    )(me, *operands)


def owner_at(me_f, by):
    size = len(CYCLE)
    half = size // 2
    line, side = lax.div(me_f, 2), lax.rem(me_f, 2)
    spot = jnp.where(side == 1, size - 1 - line, line)
    spot = lax.rem(spot + (size + by), size)
    return jnp.where(spot < half, 2 * spot, 2 * (size - 1 - spot) + 1)


def as_column(row):
    return jnp.broadcast_to(row, (128, row.shape[1])).T[:, :1]


def blocks_kernel(depth, me_ref, tok_ref, ids_ref, *out_refs):
    count, rows, lanes = out_refs[0].shape
    base = lanes - 128
    lane = lax.broadcasted_iota(jnp.int32, (rows, 128), 1) - (depth - base)
    ids = lax.div(ids_ref[...], 2)
    marks = (lax.rem(ids_ref[...], 2), lax.div(ids, DIGIT), lax.rem(ids, DIGIT))
    marks = [as_column(x.astype(F32)) for x in marks]
    for h, out_ref in enumerate(out_refs):
        here = slice(h * rows, (h + 1) * rows)
        for j in range(count):
            out_ref[j, :, :depth] = tok_ref[here, j * depth : (j + 1) * depth]
            last = out_ref[j, :, base:].astype(F32)
            last = jnp.where(lane >= 0, 0.0, last)
            for i, mark in enumerate(marks):
                last = jnp.where(lane == i, mark[here], last)
            out_ref[j, :, base:] = last.astype(BF16)


def token_blocks(me, tokens, ids, count):
    rows, width = tokens.shape
    depth = width // count
    lanes = -(-(depth + 3) // 128) * 128
    out = [shaped((count, rows // 2, lanes), BF16)] * 2
    return call(functools.partial(blocks_kernel, depth), me, (tokens, ids), out, 1)


def piece_start(me, i, rows):
    return pl.multiple_of((me ^ (i // 2)) * (2 * rows) + i % 2 * rows, rows)


def read_marks(block, depth):
    mark = [block[:, depth + i : depth + i + 1].astype(F32) for i in range(3)]
    return mark[0], mark[1] * DIGIT + mark[2]


def pack_kernel(me_ref, q_ref, up_ref, *refs):
    own_ref, other_refs = refs[-3], refs[-2:]
    for i in range(4):
        here = pl.ds(pl.multiple_of((me_ref[0] ^ i) * SPAN, SPAN), SPAN)
        for k, ref in enumerate((q_ref, up_ref)):
            if i % 2:
                other_refs[i // 2][k] = ref[:, here]
            else:
                own_ref[i // 2, k] = ref[:, here]


def pack_heads(me, queries, upstream):
    rows = queries.shape[0]
    out = [shaped((2, 2, rows, SPAN), BF16)] + [shaped((2, rows, SPAN), BF16)] * 2
    return call(pack_kernel, me, (queries, upstream), out, 1)


def place_kernel(me_ref, *refs):
    att_ref, gq_ref = refs[4:]
    for i, ref in enumerate(refs[:4]):
        here = pl.ds(pl.multiple_of((me_ref[0] ^ i) * SPAN, SPAN), SPAN)
        att_ref[:, here] = ref[0]
        gq_ref[:, here] = ref[1]


def place_heads(me, found):
    out = shaped((found[0].shape[1], 4 * SPAN), BF16)
    return call(place_kernel, me, found, [out, out], 3)


def project_kernel(steps, depth, halves, first, last, me_ref, *refs):
    parts, refs = refs[:8], refs[8:]
    weights, refs = refs[: len(steps) + halves], refs[len(steps) + halves :]
    whole_ref, sems = refs[-2:]
    rows, lanes = parts[0].shape[1:]
    owners = [owner_at(me_ref[1], by) for by in steps]
    copies = []
    for i, ref in enumerate(weights):
        there = whole_ref.at[owners[0], pl.ds(i, 1)] if halves else whole_ref.at[owners[i]]
        copies.append(pltpu.make_async_copy(ref, there, sems.at[i]))
    for copy in copies:
        copy.start()
    sums = [0.0, 0.0]
    for b, owner in enumerate(owners):
        left = jnp.concatenate([ref[owner][:, :depth] for ref in parts], axis=0)
        for e in range(2):
            right = weights[e][0] if halves else weights[b][e]
            sums[e] = sums[e] + contract(left, right, 1, 0)
    if not first:
        sums = [s + refs[0][:, e * PAIR : (e + 1) * PAIR] for e, s in enumerate(sums)]
    if not last:
        for e in range(2):
            refs[-3][:, e * PAIR : (e + 1) * PAIR] = sums[e]
    else:
        kv_ref, kind_ref, ids_ref, ids_row_ref = refs[-6:-2]
        for i, ref in enumerate(parts):
            here = pl.ds(piece_start(me_ref[0], i, rows), rows)
            kind, ids = read_marks(ref[0], depth)
            mine = slice(i * rows, (i + 1) * rows)
            kv_ref[here, :] = jnp.where(kind == 1.0, sums[1][mine], sums[0][mine]).astype(BF16)
            kind_ref[here, :] = kind
            ids_ref[here, :] = ids
        ids_row_ref[...] = jnp.broadcast_to(ids_ref[...], (8 * rows, 128)).T[:1]
    for copy in copies:
        copy.wait()


def project(me, steps, parts, weights, before, depth, last=False, halves=False):
    length = 8 * parts[0].shape[1]
    outs = [shaped((length, 2 * PAIR), F32)]
    if last:
        outs = [shaped((length, PAIR), BF16)] + [shaped(x, F32) for x in ((length, 1), (length, 1), (1, length))]
    outs.append(shaped((len(CYCLE), 2, depth, PAIR), BF16))
    operands = (*parts, *weights, *before)
    count = len(operands)
    return call(
        functools.partial(project_kernel, steps, depth, int(halves), not before, last),
        me,
        operands,
        outs,
        1,
        scratch=[pltpu.SemaphoreType.DMA((len(weights),))],
        far=(count - 1,) if before else (),
        far_out=(len(outs) - 1,),
        aliases={count: len(outs) - 1} if before else None,
    )


def hold_kernel(count, me_ref, *refs):
    for i in range(count):
        refs[i - count][...] = refs[i][...]


def hold(me, arrays, others):
    out = [shaped(x.shape, x.dtype) for x in arrays]
    return call(functools.partial(hold_kernel, len(arrays)), me, (*arrays, *others), out, 1)


def halve_kernel(me_ref, ups_ref, downs_ref, *refs):
    refs[-2][...] = ups_ref[:1]
    refs[-1][...] = downs_ref[1:]


def halve(me, ups, downs, wait):
    out = [shaped((1, *ups.shape[1:]), ups.dtype)] * 2
    return call(halve_kernel, me, (ups, downs, *wait), out, 1, far=tuple(range(2, 2 + len(wait))))


def attend_kernel(spot, me_ref, own_ref, sibling_ref, kv_ref, ids_ref, ids_row_ref, *refs):
    mine_ref, other_ref, early_ref, late_ref, bias, scores_all, dp_all, pbs, his, los = refs[-10:]
    rows = own_ref.shape[2]
    heads = [slice(h * HEAD_DIM, (h + 1) * HEAD_DIM) for h in range(GROUP)]
    for i in range(2):
        here = pl.ds(pl.multiple_of((me_ref[0] ^ i) * rows, rows), rows)
        bias[i * rows : (i + 1) * rows, :] = jnp.where(ids_row_ref[...] <= ids_ref[here, :], 0.0, HIDDEN)
    keys = kv_ref[:, :HEAD_DIM]
    values = kv_ref[:, HEAD_DIM:]
    q, up = [
        jnp.concatenate([own_ref[spot, i, :, c] for c in heads] + [sibling_ref[i, :, c] for c in heads], axis=0)
        for i in range(2)
    ]
    scores_all[...] = contract(q, keys, 1, 1)
    dp_all[...] = contract(up, values, 1, 1).astype(BF16)
    for h in range(2 * GROUP):
        here = slice(h * rows, (h + 1) * rows)
        side = h // GROUP
        scores = scores_all[here, :] * (SCALE * LOG2E) + bias[side * rows : (side + 1) * rows, :]
        expo = jnp.exp2(scores - jnp.max(scores, axis=-1, keepdims=True))
        probs = expo * (1.0 / jnp.sum(expo, axis=-1, keepdims=True))
        pbs[here, :] = probs.astype(BF16)
        dp = dp_all[here, :].astype(F32)
        ds = probs * (dp - jnp.sum(probs * dp, axis=-1, keepdims=True))
        hi = ds.astype(BF16)
        his[here, :] = hi
        los[here, :] = (ds - hi.astype(F32)).astype(BF16)
    att = contract(pbs[...], values, 1, 0).astype(BF16)
    gq = ((contract(his[...], keys, 1, 0) + contract(los[...], keys, 1, 0)) * SCALE).astype(BF16)
    for i, ref in enumerate((mine_ref, other_ref)):
        for h, cols in enumerate(heads):
            here = slice((i * GROUP + h) * rows, (i * GROUP + h + 1) * rows)
            ref[0, :, cols] = att[here]
            ref[1, :, cols] = gq[here]
    dk = (contract(q, his[...], 0, 0) + contract(q, los[...], 0, 0)) * SCALE
    dv = contract(up, pbs[...], 0, 0)
    half = early_ref.shape[0]
    for i, x in enumerate((dk.T, dv.T)):
        cols = slice(i * HEAD_DIM, (i + 1) * HEAD_DIM)
        early_ref[:, cols] = x[:half]
        late_ref[:, cols] = x[half:].astype(late_ref.dtype)


def attend(spot, me, own, other, kv, ids, ids_row, late, wait=()):
    rows = own.shape[2]
    length = kv.shape[0]
    stacked = (2 * GROUP * rows, length)
    side = shaped((2, rows, SPAN), BF16)
    return call(
        functools.partial(attend_kernel, spot),
        me,
        (own, other, kv, ids, ids_row, *wait),
        [side, side, shaped((length // 2, PAIR), F32), shaped((length // 2, PAIR), late)],
        6,
        scratch=[pltpu.VMEM((2 * rows, length), F32), pltpu.VMEM(stacked, F32)] + [pltpu.VMEM(stacked, BF16)] * 4,
        far=tuple(range(5, 5 + len(wait))),
    )


def by_expert(kind, x):
    return [jnp.where(kind == float(e), x, 0.0).astype(BF16) for e in range(2)]


def hidden_kernel(me_ref, kind_ref, g_ref, gc_ref, w_ref, wc_ref, *refs):
    mine_ref, away_ref = refs[-2:]
    rows = mine_ref.shape[0]
    count, _, depth, _ = w_ref.shape
    masked = []
    for ref in (g_ref, gc_ref):
        sides = []
        for i in range(2):
            here = pl.ds(pl.multiple_of((me_ref[0] ^ (2 * i)) * rows, rows), rows)
            sides.append(by_expert(kind_ref[here, :], ref[here, :].astype(F32)))
        masked += [jnp.concatenate([sides[0][e], sides[1][e]], axis=0) for e in range(2)]
    group = count // 4
    for j in range(4):
        total = 0.0
        for k, ref in enumerate((w_ref, wc_ref)):
            for e in range(2):
                w = ref[j * group : (j + 1) * group, e].reshape(group * depth, PAIR)
                total = total + contract(w, masked[2 * k + e], 1, 1)
        total = total.T
        cols = slice(j * group * depth, (j + 1) * group * depth)
        mine_ref[:, cols] = total[:rows]
        away_ref[:, cols] = total[rows:].astype(BF16)


def hidden_grad(me, kind, grad, grad_c, weight, weight_c, rows):
    count, _, depth, _ = weight.shape
    width = count * depth
    return call(
        hidden_kernel,
        me,
        (kind, grad, grad_c, weight, weight_c),
        [shaped((rows, width), F32), shaped((rows, width), BF16)],
        7,
    )


def share_kernel(steps, depth, split, me_ref, *refs):
    parts, g_ref, outs = refs[:8], refs[8], refs[-(2 if split else 1) * len(steps) :]
    rows, lanes = parts[0].shape[1:]
    pieces = [g_ref[pl.ds(piece_start(me_ref[0], i, rows), rows), :].astype(F32) for i in range(8)]
    kind = jnp.concatenate([read_marks(ref[0], depth)[0] for ref in parts], axis=0)
    right = jnp.concatenate(by_expert(kind, jnp.concatenate(pieces, axis=0)), axis=-1)
    for i, by in enumerate(steps):
        owner = owner_at(me_ref[1], by)
        left = jnp.concatenate([ref[owner] for ref in parts], axis=0)
        total = contract(left, right, 0, 0)
        for e in range(2):
            block = total[:depth, e * PAIR : (e + 1) * PAIR]
            if split:
                outs[2 * i + e][0] = block.astype(BF16)
            else:
                outs[i][e] = block


def shares(me, steps, parts, grad, depth, split=False, wait=()):
    if split:
        out = [shaped((1, depth, PAIR), BF16)] * (2 * len(steps))
    else:
        out = [shaped((2, depth, PAIR), F32)] * len(steps)
    far = tuple(range(9, 9 + len(wait)))
    return call(functools.partial(share_kernel, steps, depth, split), me, (*parts, grad, *wait), out, 1 + len(steps), far=far)


def in_order(parts, quarters):
    count, rows, lanes = parts[0].shape
    whole = jnp.stack(parts, axis=1).reshape(count, 4, 2 * rows, lanes)
    return jnp.take(whole, quarters, axis=1).reshape(count, 8 * rows, lanes)


def project_plain(quarters, parts, weights, depth):
    tokens = in_order(parts, quarters)
    kind, ids = read_marks(tokens[0], depth)
    sums = jnp.einsum("jmk,jekn->emn", tokens[:, :, :depth], weights, preferred_element_type=F32)
    return jnp.where(kind == 1.0, sums[1], sums[0]).astype(BF16), kind, ids, ids.reshape(1, -1)


def weight_plain(quarters, parts, grad, depth):
    tokens = in_order(parts, quarters)
    kind = tokens[0, :, depth : depth + 1].astype(F32)
    sums = [
        jnp.einsum("jmk,mn->jkn", tokens[:, :, :depth], g, preferred_element_type=F32)
        for g in by_expert(kind, grad.astype(F32))
    ]
    return lax.psum_scatter(jnp.stack(sums), "fsdp", scatter_dimension=1)


def per_device(fsdp, seq, tokens, queries, cotangent, modality, block_ids, kv_weight):
    tokens, queries, cotangent = tokens[0], queries[0], cotangent[0]
    me_f = lax.axis_index("fsdp")
    me_s = lax.axis_index("seq")
    rows, width = tokens.shape
    depth = kv_weight.shape[1]
    near_link = fsdp == len(CYCLE)

    def swap(x, bit):
        return lax.ppermute(x, "seq", [(i, i ^ bit) for i in range(seq)])

    def turn(x, by):
        return lax.ppermute(x, "fsdp", [(CYCLE[i], CYCLE[(i + by) % fsdp]) for i in range(fsdp)])

    def both_ways(ups, downs):
        return turn(ups, 1), turn(downs, -1)

    me = jnp.stack([me_s, me_f])
    quarters = me_s ^ jnp.arange(seq, dtype=jnp.int32)
    if near_link:
        weights = [kv_weight, *both_ways(kv_weight, kv_weight)]
        weights += both_ways(*weights[1:])
        weights += both_ways(*weights[3:])
    else:
        weight = lax.all_gather(kv_weight, "fsdp", axis=0)

    marks = block_ids * 2 + modality
    blocks = token_blocks(me, tokens, marks, fsdp)
    across = token_blocks(me, swap(tokens, 2), swap(marks, 2), fsdp)
    own, *others = pack_heads(me, queries, cotangent)
    others = [swap(x, 1) for x in others]
    here = hold(me, blocks, (*weights[1:3], *others)) if near_link else blocks
    parts = [*here, *[swap(x, 1) for x in here], *across, *[swap(x, 1) for x in across]]

    if near_link:
        before = project(me, STEPS[:5], parts, weights[:5], (), depth)
        weights += both_ways(*halve(me, *weights[5:], (before[0],)))
        before = project(me, STEPS[5:7], parts, weights[5:7], before, depth)
        kv, kind, ids, ids_row, weight = project(me, STEPS[7:], parts, weights[7:], before, depth, True, True)
    else:
        kv, kind, ids, ids_row = project_plain(quarters, parts, weight, depth)
    kv_far = swap(kv, 2)
    far_own, far_other, early, late = attend(1, me, own, others[1], kv_far, ids, ids_row, BF16)
    near_own, near_other, *near = attend(0, me, own, others[0], kv, ids, ids_row, F32, (early,))
    grad_kv = jnp.concatenate([near[0] + swap(early, 2), near[1] + swap(late, 2).astype(F32)]).astype(BF16)
    attended, grad_queries = place_heads(me, (near_own, swap(near_other, 1), far_own, swap(far_other, 1)))

    grad_c = swap(grad_kv, 1)
    if near_link:
        ups, downs = both_ways(*shares(me, STEPS[7:], parts, grad_kv, depth, True))
    mine, away = hidden_grad(me, kind, grad_kv, grad_c, weight, swap(weight, 1), rows)
    if near_link:
        terms = shares(me, STEPS[5:7], parts, grad_kv, depth, wait=(away,))
        terms += shares(me, STEPS[:5], parts, grad_kv, depth)
        none = jnp.zeros_like(ups)
        ups, downs = jnp.concatenate([ups, none]), jnp.concatenate([none, downs])
        for i in (0, 5, 3):
            down, up = terms[i : i + 2]
            ups, downs = both_ways((up + ups.astype(F32)).astype(BF16), (down + downs.astype(F32)).astype(BF16))
        grad_weight = terms[2] + ups.astype(F32) + downs.astype(F32)
    else:
        grad_weight = weight_plain(quarters, parts, grad_kv, depth)
    grad_tokens = (mine + swap(away, 2).astype(F32)).astype(BF16)
    return attended[None], grad_queries[None], grad_tokens[None], grad_weight


def solution(mesh):
    split = P("fsdp", "seq", None)
    weights = P(None, "fsdp", "seq")
    return jax.shard_map(
        functools.partial(per_device, mesh.shape["fsdp"], mesh.shape["seq"]),
        mesh=mesh,
        in_specs=(split, split, split, P("fsdp", "seq"), P("fsdp", "seq"), weights),
        out_specs=(split, split, split, weights),
        check_vma=False,
    )
```

```python
import functools

import jax
import jax.numpy as jnp
from jax import lax
from jax.experimental import pallas as pl
from jax.experimental.pallas import tpu as pltpu
from jax.sharding import PartitionSpec as P

HEAD_DIM = 128
GROUP = 7
SPAN = GROUP * HEAD_DIM
PAIR = 2 * HEAD_DIM
SCALE = HEAD_DIM ** (-0.5)
LOG2E = 1.4426950408889634
HIDDEN = -1e30
DIGIT = 16
F32 = jnp.float32
BF16 = jnp.bfloat16
ANYWHERE = pl.BlockSpec(memory_space=pl.ANY)
CYCLE = (0, 2, 4, 6, 7, 5, 3, 1)
STEPS = (0, -1, 1, -2, 2, -3, 3, 4)


def contract(a, b, da, db):
    return lax.dot_general(a, b, (((da,), (db,)), ((), ())), preferred_element_type=F32)


def shaped(shape, dtype):
    return jax.ShapeDtypeStruct(shape, dtype)


def call(body, me, operands, out_shape, micros, scratch=(), far=(), far_out=(), aliases=None):
    near = pl.BlockSpec(memory_space=pltpu.VMEM)
    outs = [ANYWHERE if i in far_out else near for i in range(len(out_shape))] if isinstance(out_shape, list) else near
    return pl.pallas_call(
        body,
        in_specs=[pl.BlockSpec(memory_space=pltpu.SMEM)]
        + [ANYWHERE if i in far else near for i in range(len(operands))],
        out_specs=outs,
        out_shape=out_shape,
        scratch_shapes=scratch,
        input_output_aliases=aliases or {},
        compiler_params=pltpu.CompilerParams(vmem_limit_bytes=24 * 1024 * 1024),
        cost_estimate=pl.CostEstimate(flops=0, bytes_accessed=micros * 3000000, transcendentals=0),
    )(me, *operands)


def owner_at(me_f, by):
    size = len(CYCLE)
    half = size // 2
    line, side = lax.div(me_f, 2), lax.rem(me_f, 2)
    spot = jnp.where(side == 1, size - 1 - line, line)
    spot = lax.rem(spot + (size + by), size)
    return jnp.where(spot < half, 2 * spot, 2 * (size - 1 - spot) + 1)


def as_column(row):
    return jnp.broadcast_to(row, (128, row.shape[1])).T[:, :1]


def blocks_kernel(depth, me_ref, tok_ref, ids_ref, *out_refs):
    count, rows, lanes = out_refs[0].shape
    base = lanes - 128
    lane = lax.broadcasted_iota(jnp.int32, (rows, 128), 1) - (depth - base)
    ids = lax.div(ids_ref[...], 2)
    marks = (lax.rem(ids_ref[...], 2), lax.div(ids, DIGIT), lax.rem(ids, DIGIT))
    marks = [as_column(x.astype(F32)) for x in marks]
    for h, out_ref in enumerate(out_refs):
        here = slice(h * rows, (h + 1) * rows)
        for j in range(count):
            out_ref[j, :, :depth] = tok_ref[here, j * depth : (j + 1) * depth]
            last = out_ref[j, :, base:].astype(F32)
            last = jnp.where(lane >= 0, 0.0, last)
            for i, mark in enumerate(marks):
                last = jnp.where(lane == i, mark[here], last)
            out_ref[j, :, base:] = last.astype(BF16)


def token_blocks(me, tokens, ids, count):
    rows, width = tokens.shape
    depth = width // count
    lanes = -(-(depth + 3) // 128) * 128
    out = [shaped((count, rows // 2, lanes), BF16)] * 2
    return call(functools.partial(blocks_kernel, depth), me, (tokens, ids), out, 1)


def piece_start(me, i, rows):
    return pl.multiple_of((me ^ (i // 2)) * (2 * rows) + i % 2 * rows, rows)


def read_marks(block, depth):
    mark = [block[:, depth + i : depth + i + 1].astype(F32) for i in range(3)]
    return mark[0], mark[1] * DIGIT + mark[2]


def pack_kernel(me_ref, q_ref, up_ref, *refs):
    own_ref, other_refs = refs[-3], refs[-2:]
    for i in range(4):
        here = pl.ds(pl.multiple_of((me_ref[0] ^ i) * SPAN, SPAN), SPAN)
        for k, ref in enumerate((q_ref, up_ref)):
            if i % 2:
                other_refs[i // 2][k] = ref[:, here]
            else:
                own_ref[i // 2, k] = ref[:, here]


def pack_heads(me, queries, upstream):
    rows = queries.shape[0]
    out = [shaped((2, 2, rows, SPAN), BF16)] + [shaped((2, rows, SPAN), BF16)] * 2
    return call(pack_kernel, me, (queries, upstream), out, 1)


def place_kernel(me_ref, *refs):
    att_ref, gq_ref = refs[4:]
    for i, ref in enumerate(refs[:4]):
        here = pl.ds(pl.multiple_of((me_ref[0] ^ i) * SPAN, SPAN), SPAN)
        att_ref[:, here] = ref[0]
        gq_ref[:, here] = ref[1]


def place_heads(me, found):
    out = shaped((found[0].shape[1], 4 * SPAN), BF16)
    return call(place_kernel, me, found, [out, out], 3)


def project_kernel(steps, depth, halves, first, last, me_ref, *refs):
    parts, refs = refs[:8], refs[8:]
    weights, refs = refs[: len(steps) + halves], refs[len(steps) + halves :]
    whole_ref, sems = refs[-2:]
    rows, lanes = parts[0].shape[1:]
    owners = [owner_at(me_ref[1], by) for by in steps]
    copies = []
    for i, ref in enumerate(weights):
        there = whole_ref.at[owners[0], pl.ds(i, 1)] if halves else whole_ref.at[owners[i]]
        copies.append(pltpu.make_async_copy(ref, there, sems.at[i]))
    for copy in copies:
        copy.start()
    sums = [0.0, 0.0]
    for b, owner in enumerate(owners):
        left = jnp.concatenate([ref[owner][:, :depth] for ref in parts], axis=0)
        for e in range(2):
            right = weights[e][0] if halves else weights[b][e]
            sums[e] = sums[e] + contract(left, right, 1, 0)
    if not first:
        sums = [s + refs[0][:, e * PAIR : (e + 1) * PAIR] for e, s in enumerate(sums)]
    if not last:
        for e in range(2):
            refs[-3][:, e * PAIR : (e + 1) * PAIR] = sums[e]
    for i, ref in enumerate(parts):
        here = pl.ds(piece_start(me_ref[0], i, rows), rows)
        kind, ids = read_marks(ref[0], depth)
        mine = slice(i * rows, (i + 1) * rows)
        if last:
            refs[-3][here, :] = jnp.where(kind == 1.0, sums[1][mine], sums[0][mine]).astype(BF16)
        if first:
            refs[-6][here, :] = kind
            refs[-5][here, :] = ids
    if first:
        refs[-4][...] = jnp.broadcast_to(refs[-5][...], (8 * rows, 128)).T[:1]
    for copy in copies:
        copy.wait()


def project(me, steps, parts, weights, before, depth, last=False, halves=False):
    length = 8 * parts[0].shape[1]
    outs = [shaped((length, PAIR), BF16) if last else shaped((length, 2 * PAIR), F32)]
    if not before:
        outs = [shaped(x, F32) for x in ((length, 1), (length, 1), (1, length))] + outs
    outs.append(shaped((len(CYCLE), 2, depth, PAIR), BF16))
    operands = (*parts, *weights, *before)
    count = len(operands)
    return call(
        functools.partial(project_kernel, steps, depth, int(halves), not before, last),
        me,
        operands,
        outs,
        1,
        scratch=[pltpu.SemaphoreType.DMA((len(weights),))],
        far=(count - 1,) if before else (),
        far_out=(len(outs) - 1,),
        aliases={count: len(outs) - 1} if before else None,
    )


def hold_kernel(count, me_ref, *refs):
    for i in range(count):
        refs[i - count][...] = refs[i][...]


def hold(me, arrays, others):
    out = [shaped(x.shape, x.dtype) for x in arrays]
    return call(functools.partial(hold_kernel, len(arrays)), me, (*arrays, *others), out, 1)


def halve_kernel(me_ref, ups_ref, downs_ref, *refs):
    refs[-2][...] = ups_ref[:1]
    refs[-1][...] = downs_ref[1:]


def halve(me, ups, downs, wait):
    out = [shaped((1, *ups.shape[1:]), ups.dtype)] * 2
    return call(halve_kernel, me, (ups, downs, *wait), out, 1, far=tuple(range(2, 2 + len(wait))))


def attend_kernel(spot, me_ref, own_ref, sibling_ref, kv_ref, ids_ref, ids_row_ref, *refs):
    mine_ref, other_ref, gkv_ref, bias, scores_all, dp_all, pbs, his, los = refs[-9:]
    rows = own_ref.shape[2]
    heads = [slice(h * HEAD_DIM, (h + 1) * HEAD_DIM) for h in range(GROUP)]
    for i in range(2):
        here = pl.ds(pl.multiple_of((me_ref[0] ^ i) * rows, rows), rows)
        bias[i * rows : (i + 1) * rows, :] = jnp.where(ids_row_ref[...] <= ids_ref[here, :], 0.0, HIDDEN)
    keys = kv_ref[:, :HEAD_DIM]
    values = kv_ref[:, HEAD_DIM:]
    q, up = [
        jnp.concatenate([own_ref[spot, i, :, c] for c in heads] + [sibling_ref[i, :, c] for c in heads], axis=0)
        for i in range(2)
    ]
    scores_all[...] = contract(q, keys, 1, 1)
    dp_all[...] = contract(up, values, 1, 1).astype(BF16)
    for h in range(2 * GROUP):
        here = slice(h * rows, (h + 1) * rows)
        side = h // GROUP
        scores = scores_all[here, :] * (SCALE * LOG2E) + bias[side * rows : (side + 1) * rows, :]
        expo = jnp.exp2(scores - jnp.max(scores, axis=-1, keepdims=True))
        probs = expo * (1.0 / jnp.sum(expo, axis=-1, keepdims=True))
        pbs[here, :] = probs.astype(BF16)
        dp = dp_all[here, :].astype(F32)
        ds = probs * (dp - jnp.sum(probs * dp, axis=-1, keepdims=True))
        hi = ds.astype(BF16)
        his[here, :] = hi
        los[here, :] = (ds - hi.astype(F32)).astype(BF16)
    att = contract(pbs[...], values, 1, 0).astype(BF16)
    gq = ((contract(his[...], keys, 1, 0) + contract(los[...], keys, 1, 0)) * SCALE).astype(BF16)
    for i, ref in enumerate((mine_ref, other_ref)):
        for h, cols in enumerate(heads):
            here = slice((i * GROUP + h) * rows, (i * GROUP + h + 1) * rows)
            ref[0, :, cols] = att[here]
            ref[1, :, cols] = gq[here]
    dk = (contract(q, his[...], 0, 0) + contract(q, los[...], 0, 0)) * SCALE
    dv = contract(up, pbs[...], 0, 0)
    for i, x in enumerate((dk.T, dv.T)):
        gkv_ref[:, i * HEAD_DIM : (i + 1) * HEAD_DIM] = x.astype(gkv_ref.dtype)


def attend(spot, me, own, other, kv, ids, ids_row, dtype, wait=()):
    rows = own.shape[2]
    length = kv.shape[0]
    stacked = (2 * GROUP * rows, length)
    side = shaped((2, rows, SPAN), BF16)
    return call(
        functools.partial(attend_kernel, spot),
        me,
        (own, other, kv, ids, ids_row, *wait),
        [side, side, shaped((length, PAIR), dtype)],
        6,
        scratch=[pltpu.VMEM((2 * rows, length), F32), pltpu.VMEM(stacked, F32)] + [pltpu.VMEM(stacked, BF16)] * 4,
        far=tuple(range(5, 5 + len(wait))),
    )


def by_expert(kind, x):
    return [jnp.where(kind == float(e), x, 0.0).astype(BF16) for e in range(2)]


def hidden_kernel(me_ref, kind_ref, g_ref, gc_ref, w_ref, wc_ref, *refs):
    mine_ref, away_ref = refs[-2:]
    rows = mine_ref.shape[0]
    count, _, depth, _ = w_ref.shape
    masked = []
    for ref in (g_ref, gc_ref):
        sides = []
        for i in range(2):
            here = pl.ds(pl.multiple_of((me_ref[0] ^ (2 * i)) * rows, rows), rows)
            sides.append(by_expert(kind_ref[here, :], ref[here, :].astype(F32)))
        masked += [jnp.concatenate([sides[0][e], sides[1][e]], axis=0) for e in range(2)]
    group = count // 4
    for j in range(4):
        total = 0.0
        for k, ref in enumerate((w_ref, wc_ref)):
            for e in range(2):
                w = ref[j * group : (j + 1) * group, e].reshape(group * depth, PAIR)
                total = total + contract(w, masked[2 * k + e], 1, 1)
        total = total.T
        cols = slice(j * group * depth, (j + 1) * group * depth)
        mine_ref[:, cols] = total[:rows]
        away_ref[:, cols] = total[rows:].astype(BF16)


def hidden_grad(me, kind, grad, grad_c, weight, weight_c, rows):
    count, _, depth, _ = weight.shape
    width = count * depth
    return call(
        hidden_kernel,
        me,
        (kind, grad, grad_c, weight, weight_c),
        [shaped((rows, width), F32), shaped((rows, width), BF16)],
        7,
    )


def share_kernel(steps, depth, split, me_ref, *refs):
    parts, g_ref, outs = refs[:8], refs[8], refs[-(2 if split else 1) * len(steps) :]
    rows, lanes = parts[0].shape[1:]
    pieces = [g_ref[pl.ds(piece_start(me_ref[0], i, rows), rows), :].astype(F32) for i in range(8)]
    kind = jnp.concatenate([read_marks(ref[0], depth)[0] for ref in parts], axis=0)
    right = jnp.concatenate(by_expert(kind, jnp.concatenate(pieces, axis=0)), axis=-1)
    for i, by in enumerate(steps):
        owner = owner_at(me_ref[1], by)
        left = jnp.concatenate([ref[owner] for ref in parts], axis=0)
        total = contract(left, right, 0, 0)
        for e in range(2):
            block = total[:depth, e * PAIR : (e + 1) * PAIR]
            if split:
                outs[2 * i + e][0] = block.astype(BF16)
            else:
                outs[i][e] = block


def shares(me, steps, parts, grad, depth, split=False, wait=()):
    if split:
        out = [shaped((1, depth, PAIR), BF16)] * (2 * len(steps))
    else:
        out = [shaped((2, depth, PAIR), F32)] * len(steps)
    far = tuple(range(9, 9 + len(wait)))
    return call(functools.partial(share_kernel, steps, depth, split), me, (*parts, grad, *wait), out, 1 + len(steps), far=far)


def in_order(parts, quarters):
    count, rows, lanes = parts[0].shape
    whole = jnp.stack(parts, axis=1).reshape(count, 4, 2 * rows, lanes)
    return jnp.take(whole, quarters, axis=1).reshape(count, 8 * rows, lanes)


def project_plain(quarters, parts, weights, depth):
    tokens = in_order(parts, quarters)
    kind, ids = read_marks(tokens[0], depth)
    sums = jnp.einsum("jmk,jekn->emn", tokens[:, :, :depth], weights, preferred_element_type=F32)
    return jnp.where(kind == 1.0, sums[1], sums[0]).astype(BF16), kind, ids, ids.reshape(1, -1)


def weight_plain(quarters, parts, grad, depth):
    tokens = in_order(parts, quarters)
    kind = tokens[0, :, depth : depth + 1].astype(F32)
    sums = [
        jnp.einsum("jmk,mn->jkn", tokens[:, :, :depth], g, preferred_element_type=F32)
        for g in by_expert(kind, grad.astype(F32))
    ]
    return lax.psum_scatter(jnp.stack(sums), "fsdp", scatter_dimension=1)


def per_device(fsdp, seq, tokens, queries, cotangent, modality, block_ids, kv_weight):
    tokens, queries, cotangent = tokens[0], queries[0], cotangent[0]
    me_f = lax.axis_index("fsdp")
    me_s = lax.axis_index("seq")
    rows, width = tokens.shape
    depth = kv_weight.shape[1]
    near_link = fsdp == len(CYCLE)

    def swap(x, bit):
        return lax.ppermute(x, "seq", [(i, i ^ bit) for i in range(seq)])

    def turn(x, by):
        return lax.ppermute(x, "fsdp", [(CYCLE[i], CYCLE[(i + by) % fsdp]) for i in range(fsdp)])

    def both_ways(ups, downs):
        return turn(ups, 1), turn(downs, -1)

    me = jnp.stack([me_s, me_f])
    quarters = me_s ^ jnp.arange(seq, dtype=jnp.int32)
    if near_link:
        weights = [kv_weight, *both_ways(kv_weight, kv_weight)]
        weights += both_ways(*weights[1:])
        weights += both_ways(*weights[3:])
    else:
        weight = lax.all_gather(kv_weight, "fsdp", axis=0)

    marks = block_ids * 2 + modality
    blocks = token_blocks(me, tokens, marks, fsdp)
    across = token_blocks(me, swap(tokens, 2), swap(marks, 2), fsdp)
    own, *others = pack_heads(me, queries, cotangent)
    others = [swap(x, 1) for x in others]
    here = hold(me, blocks, (*weights[1:3], *others)) if near_link else blocks
    parts = [*here, *[swap(x, 1) for x in here], *across, *[swap(x, 1) for x in across]]

    if near_link:
        kind, ids, ids_row, *before = project(me, STEPS[:5], parts, weights[:5], (), depth)
        weights += both_ways(*halve(me, *weights[5:], (before[0],)))
        before = project(me, STEPS[5:7], parts, weights[5:7], before, depth)
        kv, weight = project(me, STEPS[7:], parts, weights[7:], before, depth, True, True)
    else:
        kv, kind, ids, ids_row = project_plain(quarters, parts, weight, depth)
    kv_far = swap(kv, 2)
    far_own, far_other, far = attend(1, me, own, others[1], kv_far, ids, ids_row, BF16)
    near_own, near_other, near = attend(0, me, own, others[0], kv, ids, ids_row, F32, (far,))
    grad_kv = (near + swap(far, 2).astype(F32)).astype(BF16)
    attended, grad_queries = place_heads(me, (near_own, swap(near_other, 1), far_own, swap(far_other, 1)))

    grad_c = swap(grad_kv, 1)
    if near_link:
        ups, downs = both_ways(*shares(me, STEPS[7:], parts, grad_kv, depth, True))
    mine, away = hidden_grad(me, kind, grad_kv, grad_c, weight, swap(weight, 1), rows)
    if near_link:
        terms = shares(me, STEPS[5:7], parts, grad_kv, depth, wait=(away,))
        terms += shares(me, STEPS[:5], parts, grad_kv, depth)
        none = jnp.zeros_like(ups)
        ups, downs = jnp.concatenate([ups, none]), jnp.concatenate([none, downs])
        for i in (0, 5, 3):
            down, up = terms[i : i + 2]
            ups, downs = both_ways((up + ups.astype(F32)).astype(BF16), (down + downs.astype(F32)).astype(BF16))
        grad_weight = terms[2] + ups.astype(F32) + downs.astype(F32)
    else:
        grad_weight = weight_plain(quarters, parts, grad_kv, depth)
    grad_tokens = (mine + swap(away, 2).astype(F32)).astype(BF16)
    return attended[None], grad_queries[None], grad_tokens[None], grad_weight


def solution(mesh):
    split = P("fsdp", "seq", None)
    weights = P(None, "fsdp", "seq")
    return jax.shard_map(
        functools.partial(per_device, mesh.shape["fsdp"], mesh.shape["seq"]),
        mesh=mesh,
        in_specs=(split, split, split, P("fsdp", "seq"), P("fsdp", "seq"), weights),
        out_specs=(split, split, split, weights),
        check_vma=False,
    )
```
